32 devices in a mesh: dp: 16 (over z, y, core), tm: 2 (over x).
Axes of the slice: x: 2, y: 2, z: 4, core: 2. Of those that a mesh axis runs over, the one named last changes fastest.
Arguments:
- hidden_in: bfloat16 [2, 16, 512, 1024], P(None, 'dp', 'tm'), may hold values from -6 to 6
- memory: bfloat16 [2, 16, 512, 1024], P(None, 'dp', 'tm'), may hold values from -6 to 6
- compressed_in: bfloat16 [2, 16, 512, 1024], P(None, 'dp', 'tm'), may hold values from -6 to 6
- lengths: int32 [2, 16], P(None, 'dp'), may hold values from 128 to 512, as said below
- gain_attn: bfloat16 [1024], P(('dp', 'tm')), may hold values from 0.099609375 to 1.8984375
- gain_ffn: bfloat16 [1024], P(('dp', 'tm')), may hold values from 0.099609375 to 1.8984375
- w_query: bfloat16 [1024, 1024], P(None, ('dp', 'tm')), may hold values from -0.1875 to 0.1875
- w_key: bfloat16 [1024, 1024], P(None, ('dp', 'tm')), may hold values from -0.1875 to 0.1875
- w_value: bfloat16 [1024, 1024], P(None, ('dp', 'tm')), may hold values from -0.1875 to 0.1875
- w_out: bfloat16 [1024, 1024], P(None, ('dp', 'tm')), may hold values from -4 to 4
- w_up: bfloat16 [1024, 4096], P(None, ('dp', 'tm')), may hold values from -0.1875 to 0.1875
- w_down: bfloat16 [4096, 1024], P(None, ('dp', 'tm')), may hold values from -0.125 to 0.125
- w_compress: bfloat16 [2048, 1024], P(None, ('dp', 'tm')), may hold values from -0.125 to 0.125
- cot_out: bfloat16 [2, 16, 512, 1024], P(None, 'dp', 'tm'), may hold values from -6 to 6
- cot_comp: bfloat16 [2, 16, 256, 1024], P(None, 'dp', 'tm'), may hold values from -6 to 6
Outputs:
- layer_out: bfloat16 [2, 16, 512, 1024], P(None, 'dp', 'tm')
- compressed: bfloat16 [2, 16, 256, 1024], P(None, 'dp', 'tm')
- grad_in: bfloat16 [2, 16, 512, 1024], P(None, 'dp', 'tm')
- grad_gain_attn: float32 [1024], P(('dp', 'tm'))
- grad_gain_ffn: float32 [1024], P(('dp', 'tm'))
- grad_query: float32 [1024, 1024], P(None, ('dp', 'tm'))
- grad_key: float32 [1024, 1024], P(None, ('dp', 'tm'))
- grad_value: float32 [1024, 1024], P(None, ('dp', 'tm'))
- grad_out: float32 [1024, 1024], P(None, ('dp', 'tm'))
- grad_up: float32 [1024, 4096], P(None, ('dp', 'tm'))
- grad_down: float32 [4096, 1024], P(None, ('dp', 'tm'))
- grad_compress: float32 [2048, 1024], P(None, ('dp', 'tm'))
The draws below stay inside these ranges and needn't reach their ends.
Inputs may be any that keep to these rules, and one draw needn't show every extreme that they name: `lengths`: each length is a quarter of 512, half of 512 or 512. In each micro-batch at least one stream has length 512.
All inputs are finite; a program needn't handle non-finite values.
Results may differ from the reference program's by a relative error of at most 0.014.
Values may be sent and summed in bfloat16 or wider, within the bound.
No kernel may reach another device: no remote copies, remote signals or barrier semaphores. Data moves between devices by JAX's collectives and lax.ppermute only.
A program may use at most 256 MiB of HBM per device.

```python
import math
import jax
import jax.numpy as jnp
from jax import lax

D = 1024
H = 8
DH = 128
FF = 4096
MEM = 512
CMEM = 512
COMP = 2
MOST = 512
SEQ = 512
MB = 2
STREAMS = 16


def draw_lengths(key, part):
    key = jax.random.fold_in(key, 7)
    pick_key, long_key = jax.random.split(key)
    levels = jax.random.randint(pick_key, (MB, STREAMS), 0, 3)
    shorter = jnp.where(levels == 0, MOST // 4, jnp.where(levels == 1, MOST // 2, MOST))
    chosen = jax.random.randint(long_key, (MB, 1), 0, STREAMS)
    longest = jnp.arange(STREAMS, dtype=jnp.int32)[None, :] == chosen
    return jnp.where(longest, MOST, shorter).astype(jnp.int32)


def spiked(entries, key, source, target, parts, factor):
    def block_of(position):
        return (jnp.arange(entries.shape[position]) // (entries.shape[position] // parts)).reshape((-1,) + (1,) * (entries.ndim - 1 - position))

    one_side = jax.random.permutation(key, parts)[block_of(target)]
    second = (block_of(target) + parts // 2) % parts
    return jnp.where((block_of(source) == one_side) | (block_of(source) == second), factor * entries, entries)


def shard_levels(key, dims, shards, smallest, high):
    factor_of, own = 1.0, jax.random.fold_in(key, 6)
    for position, blocks in shards:
        steps = jnp.exp(jax.random.uniform(jax.random.fold_in(own, position), (blocks,), jnp.float32, smallest / len(shards), high / len(shards)))
        factor_of = factor_of * jnp.repeat(steps, dims[position] // blocks).reshape([-1 if axis == position else 1 for axis in range(len(dims))])
    return factor_of


def noise(rng, extent, scale, limit, shards=(), held_as=jnp.bfloat16):
    values = jax.random.normal(rng, extent, jnp.float32) * scale
    if len(shards) > 0:
        values = shard_levels(rng, extent, shards, -0.22, 0.18) * values
    return jnp.clip(values, min=-limit, max=limit).astype(held_as)


def bell_draw_with(rng, extent, deviation, most, cuts, heavy, held_as=jnp.bfloat16):
    drawn = deviation * jax.random.normal(rng, extent, jnp.float32)
    if cuts:
        drawn = drawn * shard_levels(rng, extent, cuts, -0.22, 0.18)
    return jnp.clip(spiked(drawn, jax.random.fold_in(rng, 3), *heavy), -most, most).astype(held_as)


def setup_inputs(seed: int = 0) -> dict:
    splits = jax.random.split(jax.random.key(seed), 16)
    hidden_in = noise(splits[0], (MB, STREAMS, SEQ, D), 1.0, 6.0, ((1, 16), (2, 2)))
    memory = noise(splits[1], (MB, STREAMS, MEM, D), 1.0, 6.0, ((1, 16), (2, 2)))
    compressed_in = noise(splits[2], (MB, STREAMS, CMEM, D), 1.0, 6.0, ((1, 16), (2, 2)))
    lengths = draw_lengths(jax.random.fold_in(splits[15], 71), 0)
    gain_attn = jnp.clip(1.0 + 0.18 * jax.random.normal(splits[4], (D,), jnp.float32), 0.099609375, 1.8984375).astype(jnp.bfloat16)
    gain_ffn = jnp.clip(1.0 + 0.18 * jax.random.normal(splits[5], (D,), jnp.float32), 0.099609375, 1.8984375).astype(jnp.bfloat16)
    w_query = noise(splits[6], (D, D), D ** -0.5, 0.1875, ((1, 32),))
    w_key = noise(splits[7], (D, D), D ** -0.5, 0.1875, ((1, 32),))
    w_value = noise(splits[8], (D, D), D ** -0.5, 0.1875, ((1, 32),))
    w_out = noise(splits[9], (D, D), 2 ** -0.5, 4.0, ((1, 32),))
    w_up = noise(splits[10], (D, FF), D ** -0.5, 0.1875, ((1, 32),))
    w_down = noise(splits[11], (FF, D), (FF // 2) ** -0.5, 0.125, ((1, 32),))
    w_compress = noise(splits[12], (COMP * D, D), (COMP * D) ** -0.5, 0.125, ((1, 32),))
    cot_out = bell_draw_with(splits[13], (MB, STREAMS, SEQ, D), 1.0, 6.0, ((1, 16), (2, 2)), (1, 3, 16, 2.0))
    cot_comp = bell_draw_with(splits[14], (MB, STREAMS, SEQ // COMP, D), 1.0, 6.0, ((1, 16), (2, 2)), (1, 3, 16, 2.0))
    return {"hidden_in": hidden_in, "memory": memory, "compressed_in": compressed_in, "lengths": lengths, "gain_attn": gain_attn, "gain_ffn": gain_ffn, "w_query": w_query, "w_key": w_key, "w_value": w_value, "w_out": w_out, "w_up": w_up, "w_down": w_down, "w_compress": w_compress, "cot_out": cot_out, "cot_comp": cot_comp}


EPSILON = 1e-05
ROPE_BASE = 10000.0
NEG_LARGE = -1e+30

@jax.custom_vjp
def low(v):
    return lax.optimization_barrier(v.astype(jnp.bfloat16)).astype(jnp.float32)

@jax.custom_vjp
def low_back(v):
    return v

def low_keep(v):
    return (low(v), None)

def low_pass(kept, grad):
    return (grad,)

def back_keep(v):
    return (v, None)

def back_low(kept, grad):
    return (low(grad),)
low.defvjp(low_keep, low_pass)
low_back.defvjp(back_keep, back_low)

def matmul(left, right):
    return jnp.dot(left, right, precision=lax.Precision.HIGHEST)

def layer_norm(values, gain):
    centre = values - lax.optimization_barrier(jnp.mean(values, axis=-1, keepdims=True))
    spread = lax.optimization_barrier(jnp.mean(centre * centre, axis=-1, keepdims=True))
    return centre * lax.rsqrt(spread + EPSILON) * gain

def rotate(values, positions):
    half_size = DH // 2
    frequency = jnp.exp(jnp.arange(half_size, dtype=jnp.float32) * (-2.0 * math.log(ROPE_BASE) / DH))
    angles = positions.astype(jnp.float32)[:, None] * frequency[None, :]
    cosine = jnp.cos(angles)[:, None, :]
    sine_part = jnp.sin(angles)[:, None, :]
    per_head = values.reshape(values.shape[:-1] + (H, DH))
    front_half = per_head[..., :half_size]
    back_half = per_head[..., half_size:]
    turned = jnp.concatenate([front_half * cosine - back_half * sine_part, back_half * cosine + front_half * sine_part], axis=-1)
    return turned.reshape(values.shape)

def gelu_tanh(values):
    inner = math.sqrt(2.0 / math.pi) * (values + 0.044715 * values * values * values)
    return 0.5 * values * (1.0 + jnp.tanh(inner))

def stream_layer(params, hidden, memory_rows, compressed_rows, length):
    gain_attn, gain_ffn, w_query, w_key, w_value, w_out, w_up, w_down, w_compress = params
    seq_len = hidden.shape[0]
    normed = low(layer_norm(hidden, gain_attn))
    padded = jnp.concatenate([jnp.zeros((COMP - 1, D), jnp.float32), normed], axis=0)
    windows = padded[:seq_len].reshape(seq_len // COMP, COMP * D)
    window_end = jnp.arange(seq_len // COMP, dtype=jnp.int32) * COMP
    window_mask = (window_end < length).astype(jnp.float32)[:, None]
    compressed = matmul(windows, w_compress) * window_mask
    source = jnp.concatenate([compressed_rows, memory_rows, normed], axis=0)
    query_pos = jnp.arange(seq_len, dtype=jnp.int32)
    key_pos = jnp.concatenate([COMP * (jnp.arange(CMEM, dtype=jnp.int32) - CMEM) - MEM, jnp.arange(MEM, dtype=jnp.int32) - MEM, query_pos])
    key_count = key_pos.shape[0]
    queries = low(rotate(low_back(matmul(normed, w_query)), query_pos))
    key_rows = low(rotate(matmul(source, w_key), key_pos))
    values = low(matmul(source, w_value))
    score_scale = 1.0 / math.sqrt(DH)
    scores = jnp.einsum('thd,jhd->htj', queries.reshape(seq_len, H, DH), key_rows.reshape(key_count, H, DH), precision=lax.Precision.HIGHEST) * score_scale
    scores = low_back(scores)
    key_rank = jnp.arange(key_count, dtype=jnp.int32) - (CMEM + MEM)
    allowed = key_rank[None, :] <= query_pos[:, None]
    masked = jnp.where(allowed[None], scores, NEG_LARGE)
    top_score = lax.optimization_barrier(jnp.max(masked, axis=-1, keepdims=True))
    exp_scores = jnp.exp(masked - top_score)
    attn_weights = exp_scores / lax.optimization_barrier(jnp.sum(exp_scores, axis=-1, keepdims=True))
    attn_low = low(attn_weights)
    context = jnp.einsum('htj,jhd->thd', attn_low, values.reshape(key_count, H, DH), precision=lax.Precision.HIGHEST).reshape(seq_len, D)
    context = low(low_back(context))
    attended = low_back(matmul(context, w_out))
    middle = hidden + attended
    normed_ffn = low(layer_norm(middle, gain_ffn))
    upper = low_back(matmul(normed_ffn, w_up))
    active = low(gelu_tanh(upper))
    branch = low_back(matmul(active, w_down))
    row_mask = (query_pos < length).astype(jnp.float32)[:, None]
    return ((middle + branch) * row_mask, compressed)

def reference(hidden_in, memory, compressed_in, lengths, gain_attn, gain_ffn, w_query, w_key, w_value, w_out, w_up, w_down, w_compress, cot_out, cot_comp):
    params = tuple((weight.astype(jnp.float32) for weight in (gain_attn, gain_ffn, w_query, w_key, w_value, w_out, w_up, w_down, w_compress)))
    stream_count = MB * STREAMS
    stream_items = (hidden_in.reshape(stream_count, SEQ, D), memory.reshape(stream_count, MEM, D), compressed_in.reshape(stream_count, CMEM, D), lengths.reshape(stream_count).astype(jnp.int32), cot_out.reshape(stream_count, SEQ, D), cot_comp.reshape(stream_count, SEQ // COMP, D))

    def visit_stream(totals, stream_item):
        hidden, memory_rows, compressed_rows, length, cot_rows, cot_windows = stream_item
        memory_float = memory_rows.astype(jnp.float32)
        compressed_float = compressed_rows.astype(jnp.float32)

        def apply_layer(weights, inputs):
            return stream_layer(weights, inputs, memory_float, compressed_float, length)
        outputs, pullback = jax.vjp(apply_layer, params, hidden.astype(jnp.float32))
        grad_params, grad_hidden = pullback((cot_rows.astype(jnp.float32), cot_windows.astype(jnp.float32)))
        totals = jax.tree.map(jnp.add, totals, grad_params)
        return (totals, (outputs[0].astype(jnp.bfloat16), outputs[1].astype(jnp.bfloat16), grad_hidden.astype(jnp.bfloat16)))
    zeros_start = tuple((jnp.zeros_like(weight) for weight in params))
    totals, (layer_out, compressed, grad_in) = lax.scan(visit_stream, zeros_start, stream_items)
    return (layer_out.reshape(MB, STREAMS, SEQ, D), compressed.reshape(MB, STREAMS, SEQ // COMP, D), grad_in.reshape(MB, STREAMS, SEQ, D), totals[0], totals[1], totals[2], totals[3], totals[4], totals[5], totals[6], totals[7], totals[8])
```

```python
import math

import jax
import jax.numpy as jnp
from jax import lax
from jax.experimental import pallas as pl
from jax.experimental.pallas import tpu as pltpu
from jax.sharding import PartitionSpec as P

H = 8
DH = 128
MEM = 512
CMEM = 512
COMP = 2

EPSILON = 1e-05
ROPE_BASE = 10000.0
NEG_LARGE = -1e30
SCALE = 1.0 / math.sqrt(DH)
BOTH = ("dp", "tm")
LOW = jnp.bfloat16
F32 = jnp.float32


def bit_of(bit):
    return (lax.axis_index("dp") * lax.axis_size("tm") + lax.axis_index("tm")) >> bit & 1


def swap(value, bit):
    count = lax.axis_size(BOTH)
    return lax.ppermute(value, BOTH, [(i, i ^ (1 << bit)) for i in range(count)])


def bit_count():
    return lax.axis_size(BOTH).bit_length() - 1


def gather_order(last):
    high = list(range(bit_count() - 1, 2, -1))
    return {"y": high + [0, 2, 1], "x": high + [2, 0, 1], "x_first": [0] + high + [2, 1]}[last]


def gather(shard, order):
    held, done = shard, []
    for bit in order:
        other = swap(held, bit)
        mine = bit_of(bit) == 1
        axis = 1 + sum(1 for d in done if d > bit)
        held = jnp.stack(
            [jnp.where(mine, other, held), jnp.where(mine, held, other)], axis=axis
        )
        done.append(bit)
    return held.reshape(shard.shape[0], -1, shard.shape[2])


def scatter(whole, order, kept=LOW):
    count = lax.axis_size(BOTH)
    bits = bit_count()
    held = whole.reshape((2,) * bits + (whole.shape[0] // count, whole.shape[1]))
    left = list(range(bits))
    for bit in order:
        axis = sum(1 for d in left if d > bit)
        mine = bit_of(bit)
        other = swap(lax.dynamic_index_in_dim(held, 1 - mine, axis, keepdims=False), bit)
        keep = lax.dynamic_index_in_dim(held, mine, axis, keepdims=False)
        left.remove(bit)
        held = keep.astype(F32) + other.astype(F32)
        if left:
            held = held.astype(kept)
    return held


def scatter_order(first):
    high = list(range(3, bit_count()))
    return {"y": [1, 2, 0] + high, "x": [1, 0, 2] + high}[first]


def norm_parts(values):
    centre = values - jnp.mean(values, axis=-1, keepdims=True)
    spread = jnp.mean(centre * centre, axis=-1, keepdims=True)
    rate = lax.rsqrt(spread + EPSILON)
    return centre * rate, rate


def norm_back(grad, unit, rate, gain):
    scaled = grad * gain
    return rate * (
        scaled
        - jnp.mean(scaled, axis=-1, keepdims=True)
        - unit * jnp.mean(scaled * unit, axis=-1, keepdims=True)
    )


def turn_tables(positions):
    half = DH // 2
    frequency = jnp.exp(jnp.arange(half, dtype=F32) * (-2.0 * math.log(ROPE_BASE) / DH))
    angles = positions.astype(F32)[:, None] * frequency[None, :]
    cosine, sine = jnp.cos(angles), jnp.sin(angles)
    return (
        jnp.concatenate([cosine, cosine], axis=1),
        jnp.concatenate([-sine, sine], axis=1),
    )


def turned(values, cosine, sine):
    return values * cosine + pltpu.roll(values, DH // 2, 1) * sine


def unturned(values, cosine, sine):
    return values * cosine - pltpu.roll(values, DH // 2, 1) * sine


def dot_nt(left, right):
    return lax.dot_general(left, right, (((1,), (1,)), ((), ())), preferred_element_type=F32)


def dot_nn(left, right):
    return lax.dot_general(left, right, (((1,), (0,)), ((), ())), preferred_element_type=F32)


def dot_tn(left, right):
    return lax.dot_general(left, right, (((0,), (0,)), ((), ())), preferred_element_type=F32)


def attend_kernel(
    late, q_lin, ka_lin, kb_lin, va, vb, cos_a, sin_a, cos_b, sin_b,
    context, q_out, ka_out, kb_out, pa_out, pb_out,
):
    rows = q_lin.shape[0]
    keys = ka_lin.shape[0]
    lead = keys - rows
    query = turned(q_lin[...], cos_a[lead:, :], sin_a[lead:, :]).astype(LOW)
    key_a = turned(ka_lin[...], cos_a[...], sin_a[...]).astype(LOW)
    key_b = turned(kb_lin[...], cos_b[...], sin_b[...]).astype(LOW)
    q_out[...] = query
    ka_out[...] = key_a
    kb_out[...] = key_b
    score_a = dot_nt(key_a, query) * SCALE
    score_b = dot_nt(key_b, query) * SCALE
    key_at = lax.broadcasted_iota(jnp.int32, (keys, rows), 0) - lead
    query_at = lax.broadcasted_iota(jnp.int32, (keys, rows), 1)
    score_a = jnp.where(key_at <= query_at, score_a, NEG_LARGE)
    score_b = jnp.where(key_at < late[0] * rows, score_b, NEG_LARGE)
    top = jnp.maximum(
        jnp.max(score_a, axis=0, keepdims=True), jnp.max(score_b, axis=0, keepdims=True)
    )
    exp_a = jnp.exp(score_a - top)
    exp_b = jnp.exp(score_b - top)
    total = jnp.sum(exp_a, axis=0, keepdims=True) + jnp.sum(exp_b, axis=0, keepdims=True)
    share = 1.0 / total
    attn_a = (exp_a * share).astype(LOW)
    attn_b = (exp_b * share).astype(LOW)
    pa_out[0, 0] = attn_a
    pb_out[0, 0] = attn_b
    mixed = dot_tn(va[...], attn_a) + dot_tn(vb[...], attn_b)
    context[...] = mixed.T.astype(LOW)


def attend_back_kernel(
    grad, query, ka, kb, va, vb, pa, pb, cos_a, sin_a, cos_b, sin_b,
    gq_out, gka_out, gkb_out, gva_out, gvb_out,
):
    rows = query.shape[0]
    keys = ka.shape[0]
    lead = keys - rows
    attn_a = pa[0, 0].astype(F32)
    attn_b = pb[0, 0].astype(F32)
    back_a = dot_nt(va[...], grad[...])
    back_b = dot_nt(vb[...], grad[...])
    inner = jnp.sum(attn_a * back_a, axis=0, keepdims=True) + jnp.sum(
        attn_b * back_b, axis=0, keepdims=True
    )
    score_a = (attn_a * (back_a - inner)).astype(LOW)
    score_b = (attn_b * (back_b - inner)).astype(LOW)
    gka_out[...] = unturned(
        dot_nn(score_a, query[...]) * SCALE, cos_a[...], sin_a[...]
    ).astype(LOW)
    gkb_out[...] = unturned(
        dot_nn(score_b, query[...]) * SCALE, cos_b[...], sin_b[...]
    ).astype(LOW)
    gva_out[...] = dot_nn(pa[0, 0], grad[...]).astype(LOW)
    gvb_out[...] = dot_nn(pb[0, 0], grad[...]).astype(LOW)
    mixed = dot_tn(ka[...], score_a) + dot_tn(kb[...], score_b)
    gq_out[...] = unturned(mixed.T * SCALE, cos_a[lead:, :], sin_a[lead:, :]).astype(LOW)


def head_spec(rows):
    return pl.BlockSpec((rows, DH), lambda b, h: (b, h))


def table_spec(rows):
    return pl.BlockSpec((rows, DH), lambda b, h: (0, 0))


def attn_spec(keys, rows):
    return pl.BlockSpec((1, 1, keys, rows), lambda b, h: (b, h, 0, 0))


def attend(late, q_lin, ka_lin, kb_lin, va, vb, tables, batch):
    rows = q_lin.shape[0] // batch
    keys = ka_lin.shape[0] // batch
    width = q_lin.shape[1]
    shape = jax.ShapeDtypeStruct
    return pl.pallas_call(
        attend_kernel,
        grid=(batch, H),
        in_specs=[pl.BlockSpec(memory_space=pltpu.SMEM), head_spec(rows)]
        + [head_spec(keys)] * 4
        + [table_spec(keys)] * 4,
        out_specs=[head_spec(rows), head_spec(rows), head_spec(keys), head_spec(keys)]
        + [attn_spec(keys, rows)] * 2,
        out_shape=[shape((batch * rows, width), LOW)] * 2
        + [shape((batch * keys, width), LOW)] * 2
        + [shape((batch, H, keys, rows), LOW)] * 2,
        compiler_params=pltpu.CompilerParams(vmem_limit_bytes=40 * 2**20),
        cost_estimate=pl.CostEstimate(
            flops=8 * batch * width * rows * keys,
            bytes_accessed=40 * 2**20,
            transcendentals=2 * batch * H * rows * keys,
        ),
        name="attend",
    )(late, q_lin, ka_lin, kb_lin, va, vb, *tables)


def attend_back(grad, query, ka, kb, va, vb, pa, pb, tables, batch):
    rows = query.shape[0] // batch
    keys = ka.shape[0] // batch
    width = query.shape[1]
    shape = jax.ShapeDtypeStruct
    return pl.pallas_call(
        attend_back_kernel,
        grid=(batch, H),
        in_specs=[head_spec(rows)] * 2
        + [head_spec(keys)] * 4
        + [attn_spec(keys, rows)] * 2
        + [table_spec(keys)] * 4,
        out_specs=[head_spec(rows)] + [head_spec(keys)] * 4,
        out_shape=[shape((batch * rows, width), LOW)] + [shape((batch * keys, width), LOW)] * 4,
        compiler_params=pltpu.CompilerParams(vmem_limit_bytes=40 * 2**20),
        cost_estimate=pl.CostEstimate(
            flops=16 * batch * width * rows * keys,
            bytes_accessed=40 * 2**20,
            transcendentals=0,
        ),
        name="attend_back",
    )(grad, query, ka, kb, va, vb, pa, pb, *tables)


def local(
    hidden_in, memory, compressed_in, lengths, gain_attn, gain_ffn,
    w_query, w_key, w_value, w_out, w_up, w_down, w_compress, cot_out, cot_comp,
):
    micro, streams, block, width = hidden_in.shape
    batch = micro * streams
    rows = batch * block
    late = lax.axis_index("tm")
    windows_each = block // COMP

    hidden = hidden_in.reshape(batch, block, width)
    mem = memory.reshape(batch, -1, width)
    cmem = compressed_in.reshape(batch, -1, width)
    hidden_far = swap(hidden, 0)
    mem_far = swap(mem, 0)
    cmem_far = swap(cmem, 0)

    gains = gather(
        jnp.stack([gain_attn, gain_ffn]).reshape(2, 1, -1), gather_order("x_first")
    ).reshape(2, width).astype(F32)
    gain_first, gain_second = gains[0], gains[1]
    key_value = gather(jnp.stack([w_key.T, w_value.T]), gather_order("x_first"))
    query_out = gather(jnp.stack([w_query.T, w_out.T]), gather_order("x_first"))
    up_t = gather(w_up.T[None], gather_order("x"))[0]
    down_t = gather(w_down.T[None], gather_order("y"))[0]
    compress_t = gather(w_compress.T[None], gather_order("y"))[0]
    key_t, value_t = key_value[0], key_value[1]
    query_t, out_t = query_out[0], query_out[1]

    cmem_size, mem_size = cmem.shape[1], mem.shape[1]

    def positions(half):
        return jnp.concatenate(
            [
                COMP * (half * cmem_size + jnp.arange(cmem_size, dtype=jnp.int32) - CMEM) - MEM,
                half * mem_size + jnp.arange(mem_size, dtype=jnp.int32) - MEM,
                half * block + jnp.arange(block, dtype=jnp.int32),
            ]
        )

    tables = turn_tables(positions(late)) + turn_tables(positions(1 - late))
    lens = lengths.reshape(batch)
    query_pos = late * block + jnp.arange(block, dtype=jnp.int32)
    window_end = late * block + COMP * jnp.arange(windows_each, dtype=jnp.int32)
    row_mask = (query_pos[None, :] < lens[:, None]).astype(F32)[..., None]
    window_mask = (window_end[None, :] < lens[:, None]).astype(F32)[..., None]

    inputs = hidden.astype(F32)
    unit, rate = norm_parts(inputs)
    normed = (unit * gain_first).astype(LOW)
    unit_far, _ = norm_parts(hidden_far.astype(F32))
    normed_far = (unit_far * gain_first).astype(LOW)

    rim = normed_far[:, block - 1 :] * (late == 1).astype(LOW)
    padded = jnp.concatenate([rim, normed[:, : block - 1]], axis=1)
    windows = padded.reshape(batch * windows_each, COMP * width)
    comp_grad = (
        (cot_comp.reshape(batch, windows_each, width).astype(F32) * window_mask)
        .astype(LOW)
        .reshape(batch * windows_each, width)
    )
    compressed = dot_nt(windows, compress_t).reshape(batch, windows_each, width) * window_mask
    grad_compress = scatter(dot_tn(comp_grad, windows).astype(LOW), scatter_order("y"))
    grad_windows = dot_nn(comp_grad, compress_t).reshape(batch, block, width)
    rim_grad = swap(grad_windows[:, :1].astype(LOW), 0).astype(F32) * (late == 0).astype(F32)
    grad_shifted = jnp.concatenate([grad_windows[:, 1:], rim_grad], axis=1)

    near = jnp.concatenate([cmem, mem, normed], axis=1).reshape(-1, width)
    far = jnp.concatenate([cmem_far, mem_far, normed_far], axis=1).reshape(-1, width)
    normed = normed.reshape(rows, width)
    q_lin = dot_nt(normed, query_t)
    ka_lin = dot_nt(near, key_t)
    kb_lin = dot_nt(far, key_t)
    va = dot_nt(near, value_t).astype(LOW)
    vb = dot_nt(far, value_t).astype(LOW)
    context, query, ka, kb, pa, pb = attend(
        late.reshape(1), q_lin, ka_lin, kb_lin, va, vb, tables, batch
    )
    middle = inputs.reshape(rows, width) + dot_nt(context, out_t)

    unit_ffn, rate_ffn = norm_parts(middle)
    ffn = (unit_ffn * gain_second).astype(LOW)
    upper = dot_nt(ffn, up_t)
    slope = math.sqrt(2.0 / math.pi)
    bent = jnp.tanh(slope * (upper + 0.044715 * upper * upper * upper))
    active = (0.5 * upper * (1.0 + bent)).astype(LOW)
    gelu_slope = 0.5 * (1.0 + bent) + 0.5 * upper * (1.0 - bent * bent) * slope * (
        1.0 + 3.0 * 0.044715 * upper * upper
    )
    branch = dot_nt(active, down_t)
    live = row_mask.reshape(rows, 1)
    layer_out = ((middle + branch) * live).astype(LOW)
    grad_live = cot_out.reshape(rows, width).astype(F32) * live
    grad_branch = grad_live.astype(LOW)
    grad_upper = (dot_nn(grad_branch, down_t) * gelu_slope).astype(LOW)
    grad_down = scatter(dot_tn(grad_branch, active).astype(LOW), scatter_order("y"))
    grad_up = scatter(dot_tn(grad_upper, ffn).astype(LOW), scatter_order("x"))
    grad_ffn = dot_nn(grad_upper, up_t)
    grad_gain_ffn = jnp.sum(grad_ffn * unit_ffn, axis=0)
    grad_middle = grad_live + norm_back(grad_ffn, unit_ffn, rate_ffn, gain_second)

    grad_attended = grad_middle.astype(LOW)
    grad_out = scatter(dot_tn(grad_attended, context).astype(LOW), scatter_order("y"))
    grad_context = dot_nn(grad_attended, out_t).astype(LOW)
    gq, gka, gkb, gva, gvb = attend_back(
        grad_context, query, ka, kb, va, vb, pa, pb, tables, batch
    )
    grad_value = scatter(
        (dot_tn(gva, near) + dot_tn(gvb, far)).astype(LOW), scatter_order("x")
    )
    grad_key = scatter((dot_tn(gka, near) + dot_tn(gkb, far)).astype(LOW), scatter_order("y"))
    grad_query = scatter(dot_tn(gq, normed).astype(LOW), scatter_order("x"))

    def token_rows(values):
        return values.reshape(batch, -1, width)[:, -block:].reshape(rows, width)

    token_far = dot_nn(token_rows(gkb), key_t) + dot_nn(token_rows(gvb), value_t)
    token_back = swap(token_far.astype(LOW), 0).astype(F32)
    grad_normed = (
        dot_nn(gq, query_t)
        + dot_nn(token_rows(gka), key_t)
        + dot_nn(token_rows(gva), value_t)
        + grad_shifted.reshape(rows, width)
        + token_back
    )
    unit = unit.reshape(rows, width)
    grad_gain_attn = jnp.sum(grad_normed * unit, axis=0)
    grad_in = grad_middle + norm_back(grad_normed, unit, rate.reshape(rows, 1), gain_first)
    gain_grads = scatter(
        jnp.stack([grad_gain_attn, grad_gain_ffn], axis=1), scatter_order("x"), F32
    )

    return (
        layer_out.reshape(hidden_in.shape),
        compressed.astype(LOW).reshape(cot_comp.shape),
        grad_in.astype(LOW).reshape(hidden_in.shape),
        gain_grads[:, 0],
        gain_grads[:, 1],
        grad_query.T,
        grad_key.T,
        grad_value.T,
        grad_out.T,
        grad_up.T,
        grad_down.T,
        grad_compress.T,
    )


def solution(mesh):
    rows = P(None, "dp", "tm", None)
    columns = P(None, BOTH)
    return jax.shard_map(
        local,
        mesh=mesh,
        in_specs=(rows, rows, rows, P(None, "dp"), P(BOTH), P(BOTH))
        + (columns,) * 7
        + (rows, rows),
        out_specs=(rows, rows, rows, P(BOTH), P(BOTH)) + (columns,) * 7,
        check_vma=False,
    )
```

```python
import math

import jax
import jax.numpy as jnp
import numpy as np
from jax import lax
from jax.experimental import pallas as pl
from jax.experimental.pallas import tpu as pltpu
from jax.sharding import PartitionSpec as P

H = 8
DH = 128
MEM = 512
CMEM = 512
COMP = 2

EPSILON = 1e-05
ROPE_BASE = 10000.0
NEG_LARGE = -1e30
SCALE = 1.0 / math.sqrt(DH)
BOTH = ("dp", "tm")
LOW = jnp.bfloat16
F32 = jnp.float32


TINY = pl.CostEstimate(flops=1024, bytes_accessed=1024, transcendentals=0)


def bit_of(bit):
    return (lax.axis_index("dp") * lax.axis_size("tm") + lax.axis_index("tm")) >> bit & 1


def swap(value, bit):
    count = lax.axis_size(BOTH)
    return lax.ppermute(value, BOTH, [(i, i ^ (1 << bit)) for i in range(count)])


def bit_count():
    return lax.axis_size(BOTH).bit_length() - 1


def after(value, *others):
    return lax.optimization_barrier((value,) + others)[0]


def merge_kernel(mine, own, other, out):
    out[:, mine[0]] = own[...]
    out[:, 1 - mine[0]] = other[...]


def merged(own, other, mine, before):
    width = own.shape[-1]
    own, other = own.reshape(before, -1, width), other.reshape(before, -1, width)
    rest = own.shape[1]
    each = max(1, min(before, 2**18 // (rest * width)))
    block = pl.BlockSpec((each, rest, width), lambda i: (i, 0, 0))
    return pl.pallas_call(
        merge_kernel,
        grid=(before // each,),
        in_specs=[pl.BlockSpec(memory_space=pltpu.SMEM), block, block],
        out_specs=pl.BlockSpec((each, 2, rest, width), lambda i: (i, 0, 0, 0)),
        out_shape=jax.ShapeDtypeStruct((before, 2, rest, width), own.dtype),
        compiler_params=pltpu.CompilerParams(vmem_limit_bytes=32 * 2**20),
        cost_estimate=pl.CostEstimate(flops=1024, bytes_accessed=1024, transcendentals=0),
        name="merge",
    )(mine.reshape(1), own, other)


class Gathering:
    def __init__(self, shard, order):
        self.held, self.order, self.done = shard, list(order), []
        self.lead, self.width = shard.shape[0], shard.shape[-1]
        self.other = swap(shard, order[0])

    def step(self, *last):
        bit = self.order.pop(0)
        before = self.lead * 2 ** sum(1 for d in self.done if d > bit)
        other = after(self.other, *last) if last else self.other
        self.held = merged(self.held, other, bit_of(bit), before).reshape(
            self.lead, -1, self.width
        )
        self.done.append(bit)
        if self.order:
            self.other = swap(self.held, self.order[0])
        return self.held


def combine_kernel(count, rest, stacked, mine, *refs):
    *refs, out = refs
    totals = [0.0] * count
    for whole in stacked:
        if whole:
            part = refs.pop(0)[...].reshape((-1, count) + rest).astype(F32)
            parts = [part[:, i] for i in range(count)]
        else:
            parts = [refs.pop(0)[...].reshape((-1,) + rest).astype(F32) for _ in range(count)]
        totals = [total + part for total, part in zip(totals, parts)]
    for i, total in enumerate(totals):
        out[..., i, :, :] = total.astype(LOW).reshape(out.shape[: -len(rest) - 1] + rest)


def combined(terms, count, rest, bit, done, free):
    whole, size = [], count * math.prod(rest)
    for b in reversed(free):
        if size < 2**18:
            whole, size = whole + [b], size * 2
    stepped = [b for b in free if b not in whole]

    def spec(bits, inner):
        def index(g, mine):
            place = []
            for b in bits:
                if b == bit:
                    place.append(1 - mine[b])
                elif b in done:
                    place.append(mine[b])
                elif b in whole:
                    place.append(0)
                else:
                    place.append(g >> (len(stepped) - 1 - stepped.index(b)) & 1)
            return tuple(place) + (0,) * len(inner)

        return pl.BlockSpec(tuple(2 if b in whole else 1 for b in bits) + inner, index)

    arrays = [array for group, _ in terms for array in group]
    stacked = [group[0].ndim > len(bits) + len(rest) for group, bits in terms]
    specs = [spec(bits, array.shape[len(bits) :]) for group, bits in terms for array in group]
    return pl.pallas_call(
        lambda *refs: combine_kernel(count, rest, stacked, *refs),
        grid_spec=pltpu.PrefetchScalarGridSpec(
            num_scalar_prefetch=1,
            grid=(2 ** len(stepped),),
            in_specs=specs,
            out_specs=spec(free, (count,) + rest),
        ),
        out_shape=jax.ShapeDtypeStruct((2,) * len(free) + (count,) + rest, LOW),
        compiler_params=pltpu.CompilerParams(vmem_limit_bytes=40 * 2**20),
        cost_estimate=TINY,
        name="combine",
    )(jnp.stack([bit_of(b) for b in range(bit_count())]), *arrays)


class Chain:
    def __init__(self, keeps, sends, order, rest):
        self.bits = [b for b in range(bit_count() - 1, -1, -1) if b != 1]
        self.count, self.rest = len(keeps), rest
        shape = (2,) * len(self.bits) + rest
        self.terms = [
            ([keep.reshape(shape) for keep in keeps], self.bits),
            ([swap(send.reshape(shape), 1) for send in sends], self.bits),
        ]
        self.order, self.done = list(order), [1]

    def step(self, *others):
        bit = self.order.pop(0)
        if others:
            group, bits = self.terms[-1]
            self.terms[-1] = (list(after(tuple(group), *others)), bits)
        self.bits = [b for b in self.bits if b != bit]
        send = combined(self.terms, self.count, self.rest, bit, self.done, self.bits)
        self.done.append(bit)
        self.terms.append(([swap(send, bit)], self.bits))
        return send

    def finish(self):
        while self.order:
            self.step()
        totals = [0.0] * self.count
        for group, bits in self.terms:
            for i in range(self.count):
                array = group[min(i, len(group) - 1)]
                inner = array.shape[len(bits) :]
                mine = [bit_of(b) for b in bits] + [0] * len(inner)
                piece = lax.dynamic_slice(array, mine, (1,) * len(bits) + inner).reshape(inner)
                if len(inner) > len(self.rest):
                    piece = piece[i]
                totals[i] = totals[i] + piece.astype(F32)
        return totals


class SmallReduction:
    def __init__(self, whole, order):
        count = lax.axis_size(BOTH)
        self.bits = list(range(bit_count() - 1, -1, -1))
        self.held = whole.reshape((2,) * len(self.bits) + (whole.shape[0] // count, -1))
        self.order, self.got = list(order), None

    def take(self, *others):
        if self.got is not None:
            got = after(self.got, *others) if others else self.got
            self.held, self.got = self.held + got, None

    def step(self, *others):
        self.take(*others)
        bit = self.order.pop(0)
        axis, mine = self.bits.index(bit), bit_of(bit)
        self.bits.remove(bit)
        send = lax.dynamic_index_in_dim(self.held, 1 - mine, axis, keepdims=False)
        self.held = lax.dynamic_index_in_dim(self.held, mine, axis, keepdims=False)
        self.got = swap(send, bit)
        return send

    def finish(self):
        self.take()
        return self.held


def gather_order(last):
    high = list(range(bit_count() - 1, 2, -1))
    return {"y": high + [0, 2, 1], "x": high + [2, 0, 1], "x_first": [0] + high + [2, 1]}[last]


def gather(shard, order):
    held, done = shard, []
    for bit in order:
        other = swap(held, bit)
        mine = bit_of(bit) == 1
        axis = 1 + sum(1 for d in done if d > bit)
        held = jnp.stack(
            [jnp.where(mine, other, held), jnp.where(mine, held, other)], axis=axis
        )
        done.append(bit)
    return held.reshape(shard.shape[0], -1, shard.shape[2])


def scatter(whole, order, kept=LOW):
    count = lax.axis_size(BOTH)
    bits = bit_count()
    held = whole.reshape((2,) * bits + (whole.shape[0] // count, whole.shape[1]))
    left = list(range(bits))
    for bit in order:
        axis = sum(1 for d in left if d > bit)
        mine = bit_of(bit)
        other = swap(lax.dynamic_index_in_dim(held, 1 - mine, axis, keepdims=False), bit)
        keep = lax.dynamic_index_in_dim(held, mine, axis, keepdims=False)
        left.remove(bit)
        held = keep.astype(F32) + other.astype(F32)
        if left:
            held = held.astype(kept)
    return held


def scatter_order(first):
    high = list(range(3, bit_count()))
    return {"y": [1, 2, 0] + high, "x": [1, 0, 2] + high}[first]


def norm_parts(values):
    centre = values - jnp.mean(values, axis=-1, keepdims=True)
    spread = jnp.mean(centre * centre, axis=-1, keepdims=True)
    rate = lax.rsqrt(spread + EPSILON)
    return centre * rate, rate


def norm_back(grad, unit, rate, gain):
    scaled = grad * gain
    return rate * (
        scaled
        - jnp.mean(scaled, axis=-1, keepdims=True)
        - unit * jnp.mean(scaled * unit, axis=-1, keepdims=True)
    )


def turn_tables(positions):
    half = DH // 2
    frequency = jnp.exp(jnp.arange(half, dtype=F32) * (-2.0 * math.log(ROPE_BASE) / DH))
    angles = positions.astype(F32)[:, None] * frequency[None, :]
    cosine, sine = jnp.cos(angles), jnp.sin(angles)
    return (
        jnp.concatenate([cosine, cosine], axis=1),
        jnp.concatenate([-sine, sine], axis=1),
    )


def turned(values, cosine, sine):
    return values * cosine + pltpu.roll(values, DH // 2, 1) * sine


def unturned(values, cosine, sine):
    return values * cosine - pltpu.roll(values, DH // 2, 1) * sine


def dot_nt(left, right):
    return lax.dot_general(left, right, (((1,), (1,)), ((), ())), preferred_element_type=F32)


def dot_nn(left, right):
    return lax.dot_general(left, right, (((1,), (0,)), ((), ())), preferred_element_type=F32)


def dot_tn(left, right):
    return lax.dot_general(left, right, (((0,), (0,)), ((), ())), preferred_element_type=F32)


def attend_kernel(
    late, q_lin, ka_lin, kb_lin, va, vb, cos_a, sin_a, cos_b, sin_b,
    context, q_out, ka_out, kb_out, pa_out, pb_out,
):
    rows = q_lin.shape[0]
    keys = 3 * rows
    lead = keys - rows
    query = turned(q_lin[...], cos_a[lead:, :], sin_a[lead:, :]).astype(LOW)
    key_a = turned(ka_lin[...].reshape(keys, DH), cos_a[...], sin_a[...]).astype(LOW)
    key_b = turned(kb_lin[...].reshape(keys, DH), cos_b[...], sin_b[...]).astype(LOW)
    q_out[...] = query
    ka_out[...] = key_a.reshape(ka_out.shape)
    kb_out[...] = key_b.reshape(kb_out.shape)
    score_a = dot_nt(key_a, query) * SCALE
    score_b = dot_nt(key_b, query) * SCALE
    key_at = lax.broadcasted_iota(jnp.int32, (keys, rows), 0) - lead
    query_at = lax.broadcasted_iota(jnp.int32, (keys, rows), 1)
    score_a = jnp.where(key_at <= query_at, score_a, NEG_LARGE)
    score_b = jnp.where(key_at < late[0] * rows, score_b, NEG_LARGE)
    top = jnp.maximum(
        jnp.max(score_a, axis=0, keepdims=True), jnp.max(score_b, axis=0, keepdims=True)
    )
    exp_a = jnp.exp(score_a - top)
    exp_b = jnp.exp(score_b - top)
    total = jnp.sum(exp_a, axis=0, keepdims=True) + jnp.sum(exp_b, axis=0, keepdims=True)
    share = 1.0 / total
    attn_a = (exp_a * share).astype(LOW)
    attn_b = (exp_b * share).astype(LOW)
    pa_out[0, 0] = attn_a
    pb_out[0, 0] = attn_b
    mixed = dot_tn(va[...].reshape(keys, DH), attn_a) + dot_tn(
        vb[...].reshape(keys, DH), attn_b
    )
    context[...] = mixed.T.astype(LOW)


def attend_back_kernel(
    grad, query, ka, kb, va, vb, pa, pb, cos_a, sin_a, cos_b, sin_b,
    gq_out, gka_out, gkb_out, gva_out, gvb_out,
):
    rows = query.shape[0]
    keys = 3 * rows
    lead = keys - rows
    attn_a = pa[0, 0].astype(F32)
    attn_b = pb[0, 0].astype(F32)
    back_a = dot_nt(va[...].reshape(keys, DH), grad[...])
    back_b = dot_nt(vb[...].reshape(keys, DH), grad[...])
    inner = jnp.sum(attn_a * back_a, axis=0, keepdims=True) + jnp.sum(
        attn_b * back_b, axis=0, keepdims=True
    )
    score_a = (attn_a * (back_a - inner)).astype(LOW)
    score_b = (attn_b * (back_b - inner)).astype(LOW)
    out = gka_out.shape
    gka_out[...] = (
        unturned(dot_nn(score_a, query[...]) * SCALE, cos_a[...], sin_a[...])
        .astype(LOW)
        .reshape(out)
    )
    gkb_out[...] = (
        unturned(dot_nn(score_b, query[...]) * SCALE, cos_b[...], sin_b[...])
        .astype(LOW)
        .reshape(out)
    )
    gva_out[...] = dot_nn(pa[0, 0], grad[...]).astype(LOW).reshape(out)
    gvb_out[...] = dot_nn(pb[0, 0], grad[...]).astype(LOW).reshape(out)
    mixed = dot_tn(ka[...].reshape(keys, DH), score_a) + dot_tn(
        kb[...].reshape(keys, DH), score_b
    )
    gq_out[...] = unturned(mixed.T * SCALE, cos_a[lead:, :], sin_a[lead:, :]).astype(LOW)


def feed_kernel(
    core, ffn, grad, up_own, up_far, down_own, down_far,
    branch, grad_ffn, up_keep, up_send, down_keep, down_send, ffn_t, grad_t, down_nat,
):
    half = up_own.shape[1]
    mine, theirs = core[0], 1 - core[0]
    own_at = pl.multiple_of(mine * half, half)
    far_at = pl.multiple_of(theirs * half, half)
    first = pl.program_id(0) == 0
    group, each = down_nat.shape[0], down_nat.shape[2]

    @pl.when(first)
    def _():
        ffn_t[...] = ffn[...].T
        grad_t[...] = grad[...].T.reshape(grad_t.shape)

    up_rows = jnp.concatenate([up_own[0], up_far[0]], axis=0)
    for ref, at in ((down_own, mine), (down_far, theirs)):
        down_nat[:, at, :, :half] = ref[:, pl.ds(own_at, half)].reshape(group, each, half)
        down_nat[:, at, :, half:] = ref[:, pl.ds(far_at, half)].reshape(group, each, half)
    down_rows = down_nat[...].reshape(-1, 2 * half)
    upper = dot_nt(ffn[...], up_rows)
    slope = math.sqrt(2.0 / math.pi)
    square = upper * upper
    bent = jnp.tanh(slope * upper * (1.0 + 0.044715 * square))
    share = 0.5 + 0.5 * bent
    active = (upper * share).astype(LOW)
    gelu_slope = share + 0.5 * upper * (1.0 - bent * bent) * (
        slope + (3.0 * 0.044715 * slope) * square
    )
    grad_hidden = (dot_nn(grad[...], down_rows) * gelu_slope).astype(LOW)
    more_out = dot_nt(active, down_rows)
    more_grad = dot_nn(grad_hidden, up_rows)

    @pl.when(first)
    def _():
        branch[...] = more_out
        grad_ffn[...] = more_grad

    @pl.when(jnp.logical_not(first))
    def _():
        branch[...] += more_out
        grad_ffn[...] += more_grad

    for ref, at in ((up_keep, 0), (up_send, half)):
        part = dot_nn(ffn_t[...], grad_hidden[:, at : at + half]).astype(LOW)
        ref[0, 0] = part[:, : half // 2]
        ref[0, 1] = part[:, half // 2 :]
    for ref, at in ((down_keep, mine), (down_send, theirs)):
        part = dot_nn(grad_t[:, at].reshape(group * each, -1), active).astype(LOW)
        ref[:, pl.ds(own_at, half)] = part[:, :half]
        ref[:, pl.ds(far_at, half)] = part[:, half:]


def feed_forward(core, ffn, grad_branch, up_own, up_far, down_own, down_far):
    rows, width = ffn.shape
    steps, half = up_own.shape[:2]
    wide = 2 * half

    def whole(*shape):
        return pl.BlockSpec(shape, lambda h: (0,) * len(shape))

    shape = jax.ShapeDtypeStruct
    rows_in = pl.BlockSpec((1, half, width), lambda h: (h, 0, 0))
    lanes = pl.BlockSpec((width // 2, wide), lambda h: (0, h))
    up_spec = pl.BlockSpec((1, 2, width, half // 2), lambda h: (h, 0, 0, 0))
    return pl.pallas_call(
        feed_kernel,
        grid=(steps,),
        in_specs=[
            pl.BlockSpec(memory_space=pltpu.SMEM),
            whole(rows, width),
            whole(rows, width),
            rows_in,
            rows_in,
            lanes,
            lanes,
        ],
        out_specs=[whole(rows, width), whole(rows, width), up_spec, up_spec, lanes, lanes],
        out_shape=[shape((rows, width), F32)] * 2
        + [shape((steps, 2, width, half // 2), LOW)] * 2
        + [shape((width // 2, steps * wide), LOW)] * 2,
        scratch_shapes=[
            pltpu.VMEM((width, rows), LOW),
            pltpu.VMEM((steps, 2, width // 2 // steps, rows), LOW),
            pltpu.VMEM((steps, 2, width // 2 // steps, wide), LOW),
        ],
        compiler_params=pltpu.CompilerParams(vmem_limit_bytes=48 * 2**20),
        cost_estimate=pl.CostEstimate(
            flops=1024, bytes_accessed=1024, transcendentals=0
        ),
        name="feed_forward",
    )(core.reshape(1), ffn, grad_branch, up_own, up_far, down_own, down_far)


def project_kernel(own, cmem, mem, hidden, gain, w_key, w_value, *refs):
    if own:
        w_query, key, value, normed, query, even, odd, source, wide = refs
    else:
        key, value, normed, source = refs
    rows, width = cmem.shape
    segment = pl.program_id(0)

    @pl.when(segment == 0)
    def _():
        source[...] = cmem[...]

    @pl.when(segment == 1)
    def _():
        source[...] = mem[...]

    @pl.when(segment == 2)
    def _():
        unit, _ = norm_parts(hidden[...].astype(F32))
        source[...] = (unit * gain[...]).astype(LOW)
        normed[...] = source[...]
        if own:
            query[...] = dot_nt(source[...], w_query[...].reshape(width, width))
            for i in range(width // DH):
                lanes = slice(i * DH, (i + 1) * DH)
                wide[i] = source[:, lanes].astype(F32)
                even[:, lanes] = wide[i, pl.ds(0, rows // 2, 2), :].astype(LOW)
                odd[:, lanes] = wide[i, pl.ds(1, rows // 2, 2), :].astype(LOW)

    key[0] = dot_nt(source[...], w_key[...].reshape(width, width))
    value[0] = dot_nt(source[...], w_value[...].reshape(width, width)).astype(LOW)


def project(cmem, mem, hidden, gain, weights, own):
    rows, width = hidden.shape
    shape = jax.ShapeDtypeStruct
    whole = whole_spec
    segment = pl.BlockSpec((1, rows, width), lambda i: (i, 0, 0))
    half = whole(rows // 2, width)
    return pl.pallas_call(
        lambda *refs: project_kernel(own, *refs),
        grid=(3,),
        in_specs=[whole(rows, width)] * 3
        + [whole(1, width)]
        + [weight_spec(weights, i) for i in range(3 if own else 2)],
        out_specs=[segment, segment, whole(rows, width)]
        + ([whole(rows, width), half, half] if own else []),
        out_shape=[
            shape((3, rows, width), F32),
            shape((3, rows, width), LOW),
            shape((rows, width), LOW),
        ]
        + [shape((rows, width), F32)] * own
        + [shape((rows // 2, width), LOW)] * (2 * own),
        scratch_shapes=[pltpu.VMEM((rows, width), LOW)]
        + [pltpu.VMEM((width // DH, rows, DH), F32)] * own,
        compiler_params=pltpu.CompilerParams(vmem_limit_bytes=48 * 2**20),
        cost_estimate=TINY,
        name="project",
    )(cmem, mem, hidden, gain, *[weights] * (3 if own else 2))


def weight_grads_kernel(counts, core, *refs):
    total_count = sum(counts)
    grads, sources = refs[:total_count], refs[total_count : 2 * total_count]
    outs = refs[2 * total_count :]
    first, at = core[0] == 0, 0
    for place, count in enumerate(counts):
        keep, send = outs[2 * place : 2 * place + 2]
        total = sum(dot_tn(grads[i][0], sources[i][...]) for i in range(at, at + count))
        at += count
        groups, each, depth = keep.shape
        total = total.astype(LOW).reshape(groups, 2, each, depth)
        keep[...] = jnp.where(first, total[:, 0], total[:, 1])
        send[...] = jnp.where(first, total[:, 1], total[:, 0])


def weight_grads(core, problems, each):
    pairs = [pair for problem in problems for pair in problem]
    grads = [g if isinstance(g, tuple) else (g[None], 0) for g, _ in pairs]
    sources = [source for _, source in pairs]
    width, depth = grads[0][0].shape[2], sources[0].shape[1]
    groups = 4
    wide = groups * 2 * each

    def spec(array, place):
        return pl.BlockSpec((1, array.shape[1], wide), lambda i: (place, 0, i))

    outs = pl.pallas_call(
        lambda *refs: weight_grads_kernel([len(p) for p in problems], *refs),
        grid=(width // wide,),
        in_specs=[pl.BlockSpec(memory_space=pltpu.SMEM)]
        + [spec(array, place) for array, place in grads]
        + [whole_spec(*source.shape) for source in sources],
        out_specs=[pl.BlockSpec((groups, each, depth), lambda i: (i, 0, 0))] * (2 * len(problems)),
        out_shape=[jax.ShapeDtypeStruct((width // 2 // each, each, depth), LOW)]
        * (2 * len(problems)),
        compiler_params=pltpu.CompilerParams(vmem_limit_bytes=48 * 2**20),
        cost_estimate=TINY,
        name="weight_grads",
    )(core.reshape(1), *[array for array, _ in grads], *sources)
    return outs[0::2], outs[1::2]


def weight_spec(weights, which):
    count, _, unit, width = weights.shape
    per = width // count // unit
    return pl.BlockSpec((count, per, unit, width), lambda i: (0, which, 0, 0))


def rows_spec(rows, width):
    return pl.BlockSpec((rows, width), lambda i: (i, 0))


def whole_spec(*dims):
    return pl.BlockSpec(dims, lambda i: (0,) * len(dims))


def far_kernel(late, grad_key, grad_value, comp, w_key, w_value, w_before, out):
    rows, width = out.shape
    total = dot_nn(grad_key[0], w_key[...].reshape(width, width))
    total += dot_nn(grad_value[0], w_value[...].reshape(width, width))
    rim = dot_nn(comp[0, :16], w_before[...].reshape(width, width))[:1] * late[0].astype(F32)
    last = lax.broadcasted_iota(jnp.int32, (rows, width), 0) == rows - 1
    out[...] = (total + jnp.where(last, rim, 0.0)).astype(LOW)


def far_back(late, grad_keys, grad_values, comp_grad, weights, later):
    batch, _, width = comp_grad.shape
    rows = grad_keys.shape[1] // batch
    last_part = pl.BlockSpec((1, rows, width), lambda i: (2, i, 0))
    return pl.pallas_call(
        far_kernel,
        grid=(batch,),
        in_specs=[pl.BlockSpec(memory_space=pltpu.SMEM), last_part, last_part]
        + [pl.BlockSpec((1,) + comp_grad.shape[1:], lambda i: (i, 0, 0))]
        + [weight_spec(weights, 0), weight_spec(weights, 1), weight_spec(later, 1)],
        out_specs=rows_spec(rows, width),
        out_shape=jax.ShapeDtypeStruct((batch * rows, width), LOW),
        compiler_params=pltpu.CompilerParams(vmem_limit_bytes=48 * 2**20),
        cost_estimate=TINY,
        name="far_back",
    )(late.reshape(1), grad_keys, grad_values, comp_grad, weights, weights, later)


def finish_kernel(
    grad_query, grad_key, grad_value, comp, token, hidden, grad_middle, gain,
    w_query, w_key, w_value, w_before, w_at, grad_in, grad_gain, wide,
):
    rows, width = hidden.shape
    half = rows // 2
    before = dot_nn(comp[0], w_before[...].reshape(width, width))
    before = jnp.where(
        lax.broadcasted_iota(jnp.int32, (half, width), 0) == half - 1,
        0.0,
        pltpu.roll(before, half - 1, 0),
    )
    at = dot_nn(comp[0], w_at[...].reshape(width, width))
    for i in range(width // DH):
        lanes = slice(i * DH, (i + 1) * DH)
        wide[i, pl.ds(0, half, 2), :] = at[:, lanes]
        wide[i, pl.ds(1, half, 2), :] = before[:, lanes]
    grads = jnp.concatenate([wide[i] for i in range(width // DH)], axis=1)
    grads += token[...].astype(F32)
    for left, weight in ((grad_query, w_query), (grad_key, w_key), (grad_value, w_value)):
        grads += dot_nn(left[...].reshape(rows, width), weight[...].reshape(width, width))
    unit, rate = norm_parts(hidden[...].astype(F32))
    total = jnp.sum(grads * unit, axis=0, keepdims=True)
    grad_in[...] = (grad_middle[...] + norm_back(grads, unit, rate, gain[...])).astype(LOW)
    first = pl.program_id(0) == 0

    @pl.when(first)
    def _():
        grad_gain[...] = total

    @pl.when(jnp.logical_not(first))
    def _():
        grad_gain[...] += total


def finish(
    grad_query, grad_keys, grad_values, comp_grad, token, hidden, grad_middle, gain, weights, later
):
    batch = comp_grad.shape[0]
    rows, width = hidden.shape
    some = rows // batch
    block = rows_spec(some, width)
    last_part = pl.BlockSpec((1, some, width), lambda i: (2, i, 0))
    shape = jax.ShapeDtypeStruct
    return pl.pallas_call(
        finish_kernel,
        grid=(batch,),
        in_specs=[block, last_part, last_part]
        + [pl.BlockSpec((1,) + comp_grad.shape[1:], lambda i: (i, 0, 0))]
        + [block] * 3
        + [whole_spec(1, width)]
        + [weight_spec(weights, which) for which in (2, 0, 1)]
        + [weight_spec(later, which) for which in (1, 2)],
        out_specs=[block, whole_spec(1, width)],
        out_shape=[shape((rows, width), LOW), shape((1, width), F32)],
        scratch_shapes=[pltpu.VMEM((width // DH, some, DH), F32)],
        compiler_params=pltpu.CompilerParams(vmem_limit_bytes=56 * 2**20),
        cost_estimate=TINY,
        name="finish",
    )(
        grad_query, grad_keys, grad_values, comp_grad, token, hidden, grad_middle, gain,
        weights, weights, weights, later, later,
    )


def compress_kernel(before, at, mask, w_before, w_at, out):
    width = out.shape[1]
    total = dot_nt(before[...], w_before[...].reshape(width, width))
    total += dot_nt(at[...], w_at[...].reshape(width, width))
    out[...] = (total * mask[...]).astype(LOW)


def compress(before, at, mask, later):
    rows, width = at.shape
    return pl.pallas_call(
        compress_kernel,
        grid=(1,),
        in_specs=[whole_spec(rows, width)] * 2
        + [whole_spec(rows, 1)]
        + [weight_spec(later, which) for which in (1, 2)],
        out_specs=whole_spec(rows, width),
        out_shape=jax.ShapeDtypeStruct((rows, width), LOW),
        compiler_params=pltpu.CompilerParams(vmem_limit_bytes=48 * 2**20),
        cost_estimate=TINY,
        name="compress",
    )(before, at, mask, later, later)


def join_kernel(context, hidden, gain, weight, middle, ffn):
    width = middle.shape[1]
    middle[...] = hidden[...].astype(F32) + dot_nt(
        context[...], weight[...].reshape(width, width)
    )
    unit, _ = norm_parts(middle[...])
    ffn[...] = (unit * gain[...]).astype(LOW)


def join(context, hidden, gain, weights):
    rows, width = hidden.shape
    some = rows // 2
    block = rows_spec(some, width)
    shape = jax.ShapeDtypeStruct
    return pl.pallas_call(
        join_kernel,
        grid=(2,),
        in_specs=[block, block, whole_spec(1, width), weight_spec(weights, 0)],
        out_specs=[block, block],
        out_shape=[shape((rows, width), F32), shape((rows, width), LOW)],
        compiler_params=pltpu.CompilerParams(vmem_limit_bytes=48 * 2**20),
        cost_estimate=TINY,
        name="join",
    )(context, hidden, gain, weights)


def part_kernel(
    grad_ffn, middle, cot, live, gain, weight, grad_middle, grad_low, grad_context, grad_gain
):
    width = middle.shape[1]
    unit, rate = norm_parts(middle[...])
    grads = grad_ffn[...]
    grad_middle[...] = cot[...].astype(F32) * live[...] + norm_back(
        grads, unit, rate, gain[...]
    )
    grad_low[...] = grad_middle[...].astype(LOW)
    grad_context[...] = dot_nn(grad_low[...], weight[...].reshape(width, width)).astype(LOW)
    total = jnp.sum(grads * unit, axis=0, keepdims=True)
    first = pl.program_id(0) == 0

    @pl.when(first)
    def _():
        grad_gain[...] = total

    @pl.when(jnp.logical_not(first))
    def _():
        grad_gain[...] += total


def part(grad_ffn, middle, cot, live, gain, weights):
    rows, width = middle.shape
    some = rows // 2
    block = rows_spec(some, width)
    shape = jax.ShapeDtypeStruct
    return pl.pallas_call(
        part_kernel,
        grid=(2,),
        in_specs=[block] * 3
        + [rows_spec(some, 1), whole_spec(1, width), weight_spec(weights, 0)],
        out_specs=[block] * 3 + [whole_spec(1, width)],
        out_shape=[
            shape((rows, width), F32),
            shape((rows, width), LOW),
            shape((rows, width), LOW),
            shape((1, width), F32),
        ],
        compiler_params=pltpu.CompilerParams(vmem_limit_bytes=48 * 2**20),
        cost_estimate=TINY,
        name="part",
    )(grad_ffn, middle, cot, live, gain, weights)


def head_spec(rows):
    return pl.BlockSpec((rows, DH), lambda b, h: (b, h))


def keys_spec(rows):
    return pl.BlockSpec((3, rows, DH), lambda b, h: (0, b, h))


def table_spec(rows):
    return pl.BlockSpec((rows, DH), lambda b, h: (0, 0))


def attn_spec(keys, rows):
    return pl.BlockSpec((1, 1, keys, rows), lambda b, h: (b, h, 0, 0))


def attend(late, q_lin, ka_lin, kb_lin, va, vb, tables, batch):
    rows, width = q_lin.shape[0] // batch, q_lin.shape[1]
    keys = 3 * rows
    shape = jax.ShapeDtypeStruct
    return pl.pallas_call(
        attend_kernel,
        grid=(batch, H),
        in_specs=[pl.BlockSpec(memory_space=pltpu.SMEM), head_spec(rows)]
        + [keys_spec(rows)] * 4
        + [table_spec(keys)] * 4,
        out_specs=[head_spec(rows), head_spec(rows), keys_spec(rows), keys_spec(rows)]
        + [attn_spec(keys, rows)] * 2,
        out_shape=[shape((batch * rows, width), LOW)] * 2
        + [shape((3, batch * rows, width), LOW)] * 2
        + [shape((batch, H, keys, rows), LOW)] * 2,
        compiler_params=pltpu.CompilerParams(vmem_limit_bytes=40 * 2**20),
        cost_estimate=TINY,
        name="attend",
    )(late, q_lin, ka_lin, kb_lin, va, vb, *tables)


def attend_back(grad, query, ka, kb, va, vb, pa, pb, tables, batch):
    rows, width = query.shape[0] // batch, query.shape[1]
    keys = 3 * rows
    shape = jax.ShapeDtypeStruct
    return pl.pallas_call(
        attend_back_kernel,
        grid=(batch, H),
        in_specs=[head_spec(rows)] * 2
        + [keys_spec(rows)] * 4
        + [attn_spec(keys, rows)] * 2
        + [table_spec(keys)] * 4,
        out_specs=[head_spec(rows)] + [keys_spec(rows)] * 4,
        out_shape=[shape((batch * rows, width), LOW)]
        + [shape((3, batch * rows, width), LOW)] * 4,
        compiler_params=pltpu.CompilerParams(vmem_limit_bytes=40 * 2**20),
        cost_estimate=TINY,
        name="attend_back",
    )(grad, query, ka, kb, va, vb, pa, pb, *tables)


def local_general(
    hidden_in, memory, compressed_in, lengths, gain_attn, gain_ffn,
    w_query, w_key, w_value, w_out, w_up, w_down, w_compress, cot_out, cot_comp,
):
    micro, streams, block, width = hidden_in.shape
    batch = micro * streams
    rows = batch * block
    late = lax.axis_index("tm")
    windows_each = block // COMP

    hidden = hidden_in.reshape(batch, block, width)
    mem = memory.reshape(batch, -1, width)
    cmem = compressed_in.reshape(batch, -1, width)
    hidden_far = swap(hidden, 0)
    mem_far = swap(mem, 0)
    cmem_far = swap(cmem, 0)

    gains = gather(
        jnp.stack([gain_attn, gain_ffn]).reshape(2, 1, -1), gather_order("x_first")
    ).reshape(2, width).astype(F32)
    gain_first, gain_second = gains[0], gains[1]
    key_value = gather(jnp.stack([w_key.T, w_value.T]), gather_order("x_first"))
    query_out = gather(jnp.stack([w_query.T, w_out.T]), gather_order("x_first"))
    up_t = gather(w_up.T[None], gather_order("x"))[0]
    down_t = gather(w_down.T[None], gather_order("y"))[0]
    compress_t = gather(w_compress.T[None], gather_order("y"))[0]
    key_t, value_t = key_value[0], key_value[1]
    query_t, out_t = query_out[0], query_out[1]

    cmem_size, mem_size = cmem.shape[1], mem.shape[1]

    def positions(half):
        return jnp.concatenate(
            [
                COMP * (half * cmem_size + jnp.arange(cmem_size, dtype=jnp.int32) - CMEM) - MEM,
                half * mem_size + jnp.arange(mem_size, dtype=jnp.int32) - MEM,
                half * block + jnp.arange(block, dtype=jnp.int32),
            ]
        )

    tables = turn_tables(positions(late)) + turn_tables(positions(1 - late))
    lens = lengths.reshape(batch)
    query_pos = late * block + jnp.arange(block, dtype=jnp.int32)
    window_end = late * block + COMP * jnp.arange(windows_each, dtype=jnp.int32)
    row_mask = (query_pos[None, :] < lens[:, None]).astype(F32)[..., None]
    window_mask = (window_end[None, :] < lens[:, None]).astype(F32)[..., None]

    inputs = hidden.astype(F32)
    unit, rate = norm_parts(inputs)
    normed = (unit * gain_first).astype(LOW)
    unit_far, _ = norm_parts(hidden_far.astype(F32))
    normed_far = (unit_far * gain_first).astype(LOW)

    rim = normed_far[:, block - 1 :] * (late == 1).astype(LOW)
    padded = jnp.concatenate([rim, normed[:, : block - 1]], axis=1)
    windows = padded.reshape(batch * windows_each, COMP * width)
    comp_grad = (
        (cot_comp.reshape(batch, windows_each, width).astype(F32) * window_mask)
        .astype(LOW)
        .reshape(batch * windows_each, width)
    )
    compressed = dot_nt(windows, compress_t).reshape(batch, windows_each, width) * window_mask
    grad_compress = scatter(dot_tn(comp_grad, windows).astype(LOW), scatter_order("y"))
    grad_windows = dot_nn(comp_grad, compress_t).reshape(batch, block, width)
    rim_grad = swap(grad_windows[:, :1].astype(LOW), 0).astype(F32) * (late == 0).astype(F32)
    grad_shifted = jnp.concatenate([grad_windows[:, 1:], rim_grad], axis=1)

    near = jnp.stack([cmem, mem, normed]).reshape(-1, width)
    far = jnp.stack([cmem_far, mem_far, normed_far]).reshape(-1, width)
    normed = normed.reshape(rows, width)
    q_lin = dot_nt(normed, query_t)
    ka_lin, kb_lin = (dot_nt(part, key_t).reshape(3, rows, width) for part in (near, far))
    va, vb = (
        dot_nt(part, value_t).astype(LOW).reshape(3, rows, width) for part in (near, far)
    )
    context, query, ka, kb, pa, pb = attend(
        late.reshape(1), q_lin, ka_lin, kb_lin, va, vb, tables, batch
    )
    middle = inputs.reshape(rows, width) + dot_nt(context, out_t)

    unit_ffn, rate_ffn = norm_parts(middle)
    ffn = (unit_ffn * gain_second).astype(LOW)
    upper = dot_nt(ffn, up_t)
    slope = math.sqrt(2.0 / math.pi)
    bent = jnp.tanh(slope * (upper + 0.044715 * upper * upper * upper))
    active = (0.5 * upper * (1.0 + bent)).astype(LOW)
    gelu_slope = 0.5 * (1.0 + bent) + 0.5 * upper * (1.0 - bent * bent) * slope * (
        1.0 + 3.0 * 0.044715 * upper * upper
    )
    branch = dot_nt(active, down_t)
    live = row_mask.reshape(rows, 1)
    layer_out = ((middle + branch) * live).astype(LOW)
    grad_live = cot_out.reshape(rows, width).astype(F32) * live
    grad_branch = grad_live.astype(LOW)
    grad_upper = (dot_nn(grad_branch, down_t) * gelu_slope).astype(LOW)
    grad_down = scatter(dot_tn(grad_branch, active).astype(LOW), scatter_order("y"))
    grad_up = scatter(dot_tn(grad_upper, ffn).astype(LOW), scatter_order("x"))
    grad_ffn = dot_nn(grad_upper, up_t)
    grad_gain_ffn = jnp.sum(grad_ffn * unit_ffn, axis=0)
    grad_middle = grad_live + norm_back(grad_ffn, unit_ffn, rate_ffn, gain_second)

    grad_attended = grad_middle.astype(LOW)
    grad_out = scatter(dot_tn(grad_attended, context).astype(LOW), scatter_order("y"))
    grad_context = dot_nn(grad_attended, out_t).astype(LOW)
    gq, *parts = attend_back(grad_context, query, ka, kb, va, vb, pa, pb, tables, batch)
    gka, gkb, gva, gvb = (part.reshape(-1, width) for part in parts)
    grad_value = scatter(
        (dot_tn(gva, near) + dot_tn(gvb, far)).astype(LOW), scatter_order("x")
    )
    grad_key = scatter((dot_tn(gka, near) + dot_tn(gkb, far)).astype(LOW), scatter_order("y"))
    grad_query = scatter(dot_tn(gq, normed).astype(LOW), scatter_order("x"))

    def token_rows(values):
        return values[-rows:]

    token_far = dot_nn(token_rows(gkb), key_t) + dot_nn(token_rows(gvb), value_t)
    token_back = swap(token_far.astype(LOW), 0).astype(F32)
    grad_normed = (
        dot_nn(gq, query_t)
        + dot_nn(token_rows(gka), key_t)
        + dot_nn(token_rows(gva), value_t)
        + grad_shifted.reshape(rows, width)
        + token_back
    )
    unit = unit.reshape(rows, width)
    grad_gain_attn = jnp.sum(grad_normed * unit, axis=0)
    grad_in = grad_middle + norm_back(grad_normed, unit, rate.reshape(rows, 1), gain_first)
    gain_grads = scatter(
        jnp.stack([grad_gain_attn, grad_gain_ffn], axis=1), scatter_order("x"), F32
    )

    return (
        layer_out.reshape(hidden_in.shape),
        compressed.astype(LOW).reshape(cot_comp.shape),
        grad_in.astype(LOW).reshape(hidden_in.shape),
        gain_grads[:, 0],
        gain_grads[:, 1],
        grad_query.T,
        grad_key.T,
        grad_value.T,
        grad_out.T,
        grad_up.T,
        grad_down.T,
        grad_compress.T,
    )


def local(
    hidden_in, memory, compressed_in, lengths, gain_attn, gain_ffn,
    w_query, w_key, w_value, w_out, w_up, w_down, w_compress, cot_out, cot_comp,
):
    count = lax.axis_size(BOTH)
    micro, streams, block, width = hidden_in.shape
    unit_rows, hidden_rows = width // count, w_up.shape[1]
    if unit_rows % 32 or hidden_rows % 128:
        return local_general(
            hidden_in, memory, compressed_in, lengths, gain_attn, gain_ffn,
            w_query, w_key, w_value, w_out, w_up, w_down, w_compress, cot_out, cot_comp,
        )
    batch = micro * streams
    rows = batch * block
    late, core = lax.axis_index("tm"), bit_of(1)
    windows_each = block // COMP
    hidden = hidden_in.reshape(batch, block, width)
    mem = memory.reshape(batch, -1, width)
    cmem = compressed_in.reshape(batch, -1, width)
    high = list(range(bit_count() - 1, 2, -1))
    early = [0] + high + [2, 1]

    half_unit = unit_rows // 2
    gain_rows = jnp.zeros((half_unit, width), LOW)
    gain_rows = gain_rows.at[0, : 2 * unit_rows].set(jnp.concatenate([gain_attn, gain_ffn]))
    attention_in = lax.all_gather(
        jnp.concatenate([w_key.T, w_value.T, w_query.T, gain_rows]).reshape(
            1, -1, half_unit, width
        ),
        BOTH,
        axis=0,
        tiled=True,
    )
    hidden, mem, cmem = (part.reshape(rows, width) for part in (hidden, mem, cmem))
    cmem_far, mem_far, hidden_far = swap(cmem, 0), swap(mem, 0), swap(hidden, 0)
    up_in = Gathering(w_up.T[None], [0] + high + [2])
    down_in = Gathering(w_down.T[None], high + [2, 0])
    positions = np.concatenate(
        [
            COMP * (np.arange(CMEM) - CMEM) - MEM,
            np.arange(MEM) - MEM,
            np.arange(2 * block),
        ]
    ).astype(np.float32)
    frequency = np.exp(
        np.arange(DH // 2, dtype=np.float32) * np.float32(-2.0 * math.log(ROPE_BASE) / DH)
    ).astype(np.float32)
    angles = positions[:, None] * frequency[None, :]
    turns = np.stack(
        [
            np.concatenate([np.cos(angles), np.cos(angles)], axis=1),
            np.concatenate([-np.sin(angles), np.sin(angles)], axis=1),
        ]
    ).astype(np.float32)
    turns = jnp.asarray(turns.reshape(2, 3, 2, -1, DH))

    def tables_of(half):
        return tuple(lax.dynamic_index_in_dim(turns, half, 2, False).reshape(2, -1, DH))

    tables = tables_of(late) + tables_of(1 - late)
    lens = lengths.reshape(batch)
    query_pos = late * block + jnp.arange(block, dtype=jnp.int32)
    window_end = late * block + COMP * jnp.arange(windows_each, dtype=jnp.int32)
    row_mask = (query_pos[None, :] < lens[:, None]).astype(F32)[..., None]
    window_mask = (window_end[None, :] < lens[:, None]).astype(F32)[..., None]
    live = row_mask.reshape(rows, 1)
    grad_live = cot_out.reshape(rows, width).astype(F32) * live
    grad_branch = grad_live.astype(LOW)

    last = down_in.step()
    last = up_in.step(last)
    later_in = lax.all_gather(
        after(jnp.stack([w_out.T, w_compress[:width].T, w_compress[width:].T])[None], last),
        BOTH,
        axis=0,
        tiled=True,
    )
    last = down_in.step(last, cmem_far, grad_branch, *tables)
    last = up_in.step(last, mem_far)
    last = down_in.step(last, hidden_far)
    last = up_in.step(last)
    gains = (
        after(attention_in, last)[:, 6, 0, : 2 * unit_rows]
        .reshape(count, 2, unit_rows)
        .transpose(1, 0, 2)
        .reshape(2, width)
        .astype(F32)
    )
    gain_first, gain_second = gains[:1], gains[1:]

    ka_lin, va, normed, q_lin, even, odd = project(
        cmem, mem, after(hidden, last), gain_first, attention_in, True
    )
    kb_lin, vb, normed_far = project(
        after(cmem_far, q_lin), mem_far, hidden_far, gain_first, attention_in, False
    )

    context, query, ka, kb, pa, pb = attend(
        late.reshape(1), q_lin, ka_lin, kb_lin, va, vb, tables, batch
    )
    outward = high[::-1]
    steps = count // 4
    down_own = down_in.step(context)[0]
    down_far = swap(down_own, 1)
    up_own = up_in.step(down_own)[0]
    up_far = swap(up_own, 1)
    middle, ffn = join(after(context, up_own), hidden, gain_second, later_in)

    branch, grad_ffn, up_keep, up_send, down_keep, down_send = feed_forward(
        core,
        ffn,
        grad_branch,
        up_own.reshape(steps, -1, width),
        up_far.reshape(steps, -1, width),
        down_own,
        down_far,
    )
    up_sum = Chain([up_keep], [up_send], [0, 2] + outward, up_keep.shape[2:])
    down_sum = Chain(
        [down_keep], [down_send], [2, 0] + outward, (unit_rows, hidden_rows * count)
    )

    grad_middle, grad_low, grad_context, grad_gain_ffn = part(
        grad_ffn, middle, cot_out.reshape(rows, width), live, gain_second, later_in
    )
    last = up_sum.step(grad_context)
    last = down_sum.step(last)

    normed_far3, odd3 = (value.reshape(batch, -1, width) for value in (normed_far, odd))
    rim = normed_far3[:, block - 1 :] * (late == 1).astype(LOW)
    before = jnp.concatenate([rim, odd3[:, : windows_each - 1]], axis=1).reshape(-1, width)
    comp_grad = (cot_comp.reshape(batch, windows_each, width).astype(F32) * window_mask).astype(LOW)
    comp_rows = after(comp_grad, last).reshape(-1, width)
    early_sum = Chain(
        *weight_grads(
            core,
            [[(comp_rows, before)], [(comp_rows, even)], [(grad_low, context)]],
            2 * unit_rows,
        ),
        outward + [2, 0],
        (unit_rows, width),
    )
    last = early_sum.step(last)

    gq, gka, gkb, gva, gvb = attend_back(
        after(grad_context, last), query, ka, kb, va, vb, pa, pb, tables, batch
    )
    token_far = far_back(late, after(gkb, gq), gvb, comp_grad, attention_in, later_in)
    token_back = swap(token_far, 0)
    last = up_sum.step(token_far)
    last = down_sum.step(last)
    sources = (cmem, mem, normed, cmem_far, mem_far, normed_far)

    def source_problem(near, far):
        grads = [(grad, i) for grad in (near, far) for i in range(3)]
        return list(zip(grads, sources))

    value_sum = Chain(
        *weight_grads(core, [source_problem(after(gva, last), gvb)], 2 * unit_rows),
        [2, 0] + outward,
        (unit_rows, width),
    )
    last = early_sum.step(value_sum.terms[0][0][0])
    last = up_sum.step(last)
    key_query_sum = Chain(
        *weight_grads(
            core,
            [source_problem(after(gka, last), gkb), [(gq, normed)]],
            2 * unit_rows,
        ),
        [2, 0] + outward,
        (unit_rows, width),
    )
    last = value_sum.step(key_query_sum.terms[0][0][0])
    last = key_query_sum.step(last)

    grad_in, grad_gain_attn = finish(
        after(gq, last), gka, gva, comp_grad, token_back, hidden, grad_middle, gain_first,
        attention_in, later_in,
    )
    gain_sum = SmallReduction(
        jnp.concatenate([grad_gain_attn, grad_gain_ffn]).T, [1, 2, 0] + outward
    )
    last = gain_sum.step()
    last = up_sum.step(last)
    last = value_sum.step(last)
    last = gain_sum.step(last)
    last = early_sum.step(last)
    last = down_sum.step(last)
    last = key_query_sum.step(last)
    last = gain_sum.step(last)
    last = value_sum.step(last)
    last = early_sum.step(last)
    last = down_sum.step(last)
    last = gain_sum.step(last)
    last = key_query_sum.step(last)
    last = value_sum.step(last)
    last = gain_sum.step(last)
    last = key_query_sum.step(last)

    branch, before, even = after((branch, before, even), last)
    layer_out = ((middle + branch) * live).astype(LOW)
    compressed = compress(before, even, window_mask.reshape(-1, 1), later_in)
    gain_grads = gain_sum.finish()
    grad_key, grad_query = key_query_sum.finish()
    grad_before, grad_at, grad_out = early_sum.finish()

    return (
        layer_out.reshape(hidden_in.shape),
        compressed.reshape(cot_comp.shape),
        grad_in.reshape(hidden_in.shape),
        gain_grads[:, 0],
        gain_grads[:, 1],
        grad_query.T,
        grad_key.T,
        value_sum.finish()[0].T,
        grad_out.T,
        up_sum.finish()[0],
        down_sum.finish()[0].T,
        jnp.concatenate([grad_before.T, grad_at.T]),
    )


def solution(mesh):
    rows = P(None, "dp", "tm", None)
    columns = P(None, BOTH)
    return jax.shard_map(
        local,
        mesh=mesh,
        in_specs=(rows, rows, rows, P(None, "dp"), P(BOTH), P(BOTH))
        + (columns,) * 7
        + (rows, rows),
        out_specs=(rows, rows, rows, P(BOTH), P(BOTH)) + (columns,) * 7,
        check_vma=False,
    )
```

```python
import functools
import math

import jax
import jax.numpy as jnp
import numpy as np
from jax import lax
from jax.experimental import pallas as pl
from jax.experimental.pallas import tpu as pltpu
from jax.sharding import PartitionSpec as P

H = 8
DH = 128
MEM = 512
CMEM = 512
COMP = 2

EPSILON = 1e-05
ROPE_BASE = 10000.0
NEG_LARGE = -1e30
SCALE = 1.0 / math.sqrt(DH)
BOTH = ("dp", "tm")
LOW = jnp.bfloat16
F32 = jnp.float32


VMEM = 60 * 2**20
TOGETHER = 2
SMALL = 16 * 2**20
LONG = pl.CostEstimate(flops=10**11, bytes_accessed=2**20, transcendentals=0)


def bit_of(bit):
    return (lax.axis_index("dp") * lax.axis_size("tm") + lax.axis_index("tm")) >> bit & 1


def swap(value, bit):
    count = lax.axis_size(BOTH)
    return lax.ppermute(value, BOTH, [(i, i ^ (1 << bit)) for i in range(count)])


def bit_count():
    return lax.axis_size(BOTH).bit_length() - 1


def ordered_call(kernel, args, waits, in_specs, **settings):
    count, more = len(args), len(waits)

    def body(*refs):
        kernel(*refs[:count], *refs[count + more :])

    return pl.pallas_call(
        body,
        in_specs=list(in_specs) + [pl.BlockSpec(memory_space=pl.ANY)] * more,
        cost_estimate=LONG,
        **settings,
    )(*args, *waits)


def copy_kernel(value, out):
    out[...] = value[...]


def copied(value, waits):
    block = pl.BlockSpec(value.shape, lambda i: (0,) * value.ndim)
    return ordered_call(
        copy_kernel,
        (value,),
        waits,
        [block],
        grid=(1,),
        out_specs=block,
        out_shape=jax.ShapeDtypeStruct(value.shape, value.dtype),
        compiler_params=pltpu.CompilerParams(vmem_limit_bytes=SMALL),
        name="copied",
    )


def merge_kernel(mine, own, other, out):
    out[:, mine[0]] = own[...]
    out[:, 1 - mine[0]] = other[...]


def merged(own, other, mine, before, waits):
    width = own.shape[-1]
    own, other = own.reshape(before, -1, width), other.reshape(before, -1, width)
    rest = own.shape[1]
    each = max(1, min(before, 2**18 // (rest * width)))
    block = pl.BlockSpec((each, rest, width), lambda i: (i, 0, 0))
    return ordered_call(
        merge_kernel,
        (mine.reshape(1), own, other),
        waits,
        [pl.BlockSpec(memory_space=pltpu.SMEM), block, block],
        grid=(before // each,),
        out_specs=pl.BlockSpec((each, 2, rest, width), lambda i: (i, 0, 0, 0)),
        out_shape=jax.ShapeDtypeStruct((before, 2, rest, width), own.dtype),
        compiler_params=pltpu.CompilerParams(vmem_limit_bytes=VMEM),
        name="merge",
    )


class Gathering:
    def __init__(self, shard, order):
        self.held, self.order, self.done = shard, list(order), []
        self.lead, self.width = shard.shape[0], shard.shape[-1]
        self.other = swap(shard, order[0])

    def step(self, *waits):
        bit = self.order.pop(0)
        before = self.lead * 2 ** sum(1 for d in self.done if d > bit)
        self.held = merged(self.held, self.other, bit_of(bit), before, waits).reshape(
            self.lead, -1, self.width
        )
        self.done.append(bit)
        if self.order:
            self.other = swap(self.held, self.order[0])
        return self.held


def combine_kernel(count, mine, *refs):
    refs, out = refs[:count], refs[-1]
    total = sum(ref[...].reshape(out.shape).astype(F32) for ref in refs)
    out[...] = total.astype(out.dtype)


def combined(terms, rest, bit, done, free, waits):
    whole, size = [], math.prod(rest)
    for b in reversed(free):
        if size < 2**18:
            whole, size = whole + [b], size * 2
    stepped = [b for b in free if b not in whole]

    def spec(bits):
        def index(g, mine):
            place = []
            for b in bits:
                if b == bit:
                    place.append(1 - mine[b])
                elif b in done:
                    place.append(mine[b])
                elif b in whole:
                    place.append(0)
                else:
                    place.append(g >> (len(stepped) - 1 - stepped.index(b)) & 1)
            return tuple(place) + (0,) * len(rest)

        return pl.BlockSpec(tuple(2 if b in whole else 1 for b in bits) + rest, index)

    return pl.pallas_call(
        lambda *refs: combine_kernel(len(terms), *refs),
        grid_spec=pltpu.PrefetchScalarGridSpec(
            num_scalar_prefetch=1,
            grid=(2 ** len(stepped),),
            in_specs=[spec(bits) for _, bits in terms]
            + [pl.BlockSpec(memory_space=pl.ANY)] * len(waits),
            out_specs=spec(free),
        ),
        out_shape=jax.ShapeDtypeStruct((2,) * len(free) + rest, F32 if bit is None else LOW),
        compiler_params=pltpu.CompilerParams(
            vmem_limit_bytes=VMEM
        ),
        cost_estimate=LONG,
        name="combine",
    )(jnp.stack([bit_of(b) for b in range(bit_count())]), *[term for term, _ in terms], *waits)


class Chain:
    def __init__(self, keep, send, order, rest):
        self.bits = [b for b in range(bit_count() - 1, -1, -1) if b != 1]
        self.rest = rest
        shape = (2,) * len(self.bits) + rest
        self.terms = [
            (keep.reshape(shape), self.bits),
            (swap(send.reshape(shape), 1), self.bits),
        ]
        self.order, self.done = list(order), [1]

    def step(self, *waits):
        bit = self.order.pop(0)
        self.bits = [b for b in self.bits if b != bit]
        send = combined(self.terms, self.rest, bit, self.done, self.bits, waits)
        self.done.append(bit)
        self.terms.append((swap(send, bit), self.bits))
        return send

    def finish(self, *waits):
        return combined(self.terms, self.rest, None, self.done, [], waits)


def gather_order(last):
    high = list(range(bit_count() - 1, 2, -1))
    return {"y": high + [0, 2, 1], "x": high + [2, 0, 1], "x_first": [0] + high + [2, 1]}[last]


def gather(shard, order):
    held, done = shard, []
    for bit in order:
        other = swap(held, bit)
        mine = bit_of(bit) == 1
        axis = 1 + sum(1 for d in done if d > bit)
        held = jnp.stack(
            [jnp.where(mine, other, held), jnp.where(mine, held, other)], axis=axis
        )
        done.append(bit)
    return held.reshape(shard.shape[0], -1, shard.shape[2])


def scatter(whole, order, kept=LOW):
    count = lax.axis_size(BOTH)
    bits = bit_count()
    held = whole.reshape((2,) * bits + (whole.shape[0] // count, whole.shape[1]))
    left = list(range(bits))
    for bit in order:
        axis = sum(1 for d in left if d > bit)
        mine = bit_of(bit)
        other = swap(lax.dynamic_index_in_dim(held, 1 - mine, axis, keepdims=False), bit)
        keep = lax.dynamic_index_in_dim(held, mine, axis, keepdims=False)
        left.remove(bit)
        held = keep.astype(F32) + other.astype(F32)
        if left:
            held = held.astype(kept)
    return held


def scatter_order(first):
    high = list(range(3, bit_count()))
    return {"y": [1, 2, 0] + high, "x": [1, 0, 2] + high}[first]


def norm_parts(values):
    centre = values - jnp.mean(values, axis=-1, keepdims=True)
    spread = jnp.mean(centre * centre, axis=-1, keepdims=True)
    rate = lax.rsqrt(spread + EPSILON)
    return centre * rate, rate


def norm_back(grad, unit, rate, gain):
    scaled = grad * gain
    return rate * (
        scaled
        - jnp.mean(scaled, axis=-1, keepdims=True)
        - unit * jnp.mean(scaled * unit, axis=-1, keepdims=True)
    )


def turn_tables(positions):
    half = DH // 2
    frequency = jnp.exp(jnp.arange(half, dtype=F32) * (-2.0 * math.log(ROPE_BASE) / DH))
    angles = positions.astype(F32)[:, None] * frequency[None, :]
    cosine, sine = jnp.cos(angles), jnp.sin(angles)
    return (
        jnp.concatenate([cosine, cosine], axis=1),
        jnp.concatenate([-sine, sine], axis=1),
    )


def turned(values, cosine, sine):
    return values * cosine + pltpu.roll(values, DH // 2, 1) * sine


def unturned(values, cosine, sine):
    return values * cosine - pltpu.roll(values, DH // 2, 1) * sine


def dot_nt(left, right):
    return lax.dot_general(left, right, (((1,), (1,)), ((), ())), preferred_element_type=F32)


def dot_nn(left, right):
    return lax.dot_general(left, right, (((1,), (0,)), ((), ())), preferred_element_type=F32)


def dot_tn(left, right):
    return lax.dot_general(left, right, (((0,), (0,)), ((), ())), preferred_element_type=F32)


def attend_kernel(late, query, ka, kb, va, vb, context, pa_out, pb_out):
    rows = query.shape[0]
    base = SCALE * math.log2(math.e)
    sides = ((ka, va, pa_out), (kb, vb, pb_out))
    for head in range(query.shape[1] // DH):
        lanes = slice(head * DH, (head + 1) * DH)
        scores = []
        for side, (key, _, _) in enumerate(sides):
            for part in range(3):
                score = dot_nt(key[part, :, lanes], query[:, lanes])
                if part == 2:
                    key_at = lax.broadcasted_iota(jnp.int32, (rows, rows), 0)
                    if side == 0:
                        seen = key_at <= lax.broadcasted_iota(jnp.int32, (rows, rows), 1)
                    else:
                        seen = key_at < late[0] * rows
                    score = jnp.where(seen, score, NEG_LARGE)
                scores.append(score)
        top = functools.reduce(jnp.maximum, scores)
        top = jnp.max(top, axis=0, keepdims=True) * base
        exps = [jnp.exp2(score * base - top) for score in scores]
        total = jnp.sum(sum(exps), axis=0, keepdims=True)
        share = 1.0 / total
        mixed = 0.0
        for i, value in enumerate(exps):
            attn = (value * share).astype(LOW)
            side, part = divmod(i, 3)
            sides[side][2][0, head, part * rows : (part + 1) * rows, :] = attn
            mixed += dot_tn(sides[side][1][part, :, lanes], attn)
        context[:, lanes] = mixed.T.astype(LOW)


def attend_back_kernel(
    grad, query, ka, kb, va, vb, pa, pb, cos_a, sin_a, cos_b, sin_b,
    gq_out, gka_out, gkb_out, gva_out, gvb_out,
):
    rows = query.shape[0]
    lead = 2 * rows
    sides = (
        (ka, va, pa, cos_a, sin_a, gka_out, gva_out),
        (kb, vb, pb, cos_b, sin_b, gkb_out, gvb_out),
    )
    for head in range(query.shape[1] // DH):
        lanes = slice(head * DH, (head + 1) * DH)
        here, own = grad[:, lanes], query[:, lanes]
        backs, inner = [], 0.0
        for _, value, attn, _, _, _, out in sides:
            for part in range(3):
                weights = attn[0, head, part * rows : (part + 1) * rows, :]
                back = dot_nt(value[part, :, lanes], here)
                inner += weights.astype(F32) * back
                out[part, :, lanes] = dot_nn(weights, here).astype(LOW)
                backs.append(back)
        inner = jnp.sum(inner, axis=0, keepdims=True)
        mixed = 0.0
        for i, back in enumerate(backs):
            side, part = divmod(i, 3)
            key, _, attn, cosine, sine, out, _ = sides[side]
            at = slice(part * rows, (part + 1) * rows)
            score = (attn[0, head, at, :].astype(F32) * (back - inner)).astype(LOW)
            grads = dot_nn(score, own) * SCALE
            out[part, :, lanes] = unturned(grads, cosine[at, :], sine[at, :]).astype(LOW)
            mixed += dot_tn(key[part, :, lanes], score)
        gq_out[:, lanes] = unturned(mixed.T * SCALE, cos_a[lead:, :], sin_a[lead:, :]).astype(LOW)


def feed_kernel(
    core, ffn, grad, up_own, up_far, down_own, down_far,
    branch, grad_ffn, up_keep, up_send, down_keep, down_send, ffn_t, grad_t, down_nat,
):
    half = up_own.shape[1]
    mine, theirs = core[0], 1 - core[0]
    own_at = pl.multiple_of(mine * half, half)
    far_at = pl.multiple_of(theirs * half, half)
    first = pl.program_id(0) == 0
    group, each = down_nat.shape[0], down_nat.shape[2]

    @pl.when(first)
    def _():
        ffn_t[...] = ffn[...].T
        grad_t[...] = grad[...].T.reshape(grad_t.shape)

    up_rows = jnp.concatenate([up_own[0], up_far[0]], axis=0)
    for ref, at in ((down_own, mine), (down_far, theirs)):
        down_nat[:, at, :, :half] = ref[:, pl.ds(own_at, half)].reshape(group, each, half)
        down_nat[:, at, :, half:] = ref[:, pl.ds(far_at, half)].reshape(group, each, half)
    down_rows = down_nat[...].reshape(-1, 2 * half)
    upper = dot_nt(ffn[...], up_rows)
    slope = math.sqrt(2.0 / math.pi)
    square = upper * upper
    bent = jnp.tanh(slope * upper * (1.0 + 0.044715 * square))
    share = 0.5 + 0.5 * bent
    active = (upper * share).astype(LOW)
    gelu_slope = share + 0.5 * upper * (1.0 - bent * bent) * (
        slope + (3.0 * 0.044715 * slope) * square
    )
    grad_hidden = (dot_nn(grad[...], down_rows) * gelu_slope).astype(LOW)
    more_out = dot_nt(active, down_rows)
    more_grad = dot_nn(grad_hidden, up_rows)

    @pl.when(first)
    def _():
        branch[...] = more_out
        grad_ffn[...] = more_grad

    @pl.when(jnp.logical_not(first))
    def _():
        branch[...] += more_out
        grad_ffn[...] += more_grad

    for ref, at in ((up_keep, 0), (up_send, half)):
        part = dot_nn(ffn_t[...], grad_hidden[:, at : at + half]).astype(LOW)
        ref[0, 0] = part[:, : half // 2]
        ref[0, 1] = part[:, half // 2 :]
    for ref, at in ((down_keep, mine), (down_send, theirs)):
        part = dot_nn(grad_t[:, at].reshape(group * each, -1), active).astype(LOW)
        ref[:, pl.ds(own_at, half)] = part[:, :half]
        ref[:, pl.ds(far_at, half)] = part[:, half:]


def feed_forward(core, ffn, grad_branch, up_own, up_far, down_own, down_far, waits=()):
    rows, width = ffn.shape
    steps, half = up_own.shape[:2]
    wide = 2 * half

    def whole(*shape):
        return pl.BlockSpec(shape, lambda h: (0,) * len(shape))

    shape = jax.ShapeDtypeStruct
    rows_in = pl.BlockSpec((1, half, width), lambda h: (h, 0, 0))
    lanes = pl.BlockSpec((width // 2, wide), lambda h: (0, h))
    up_spec = pl.BlockSpec((1, 2, width, half // 2), lambda h: (h, 0, 0, 0))
    return ordered_call(
        feed_kernel,
        (core.reshape(1), ffn, grad_branch, up_own, up_far, down_own, down_far,),
        waits,
        [
            pl.BlockSpec(memory_space=pltpu.SMEM),
            whole(rows, width),
            whole(rows, width),
            rows_in,
            rows_in,
            lanes,
            lanes,
        ],
        grid=(steps,),
        out_specs=[whole(rows, width), whole(rows, width), up_spec, up_spec, lanes, lanes],
        out_shape=[shape((rows, width), F32)] * 2
        + [shape((steps, 2, width, half // 2), LOW)] * 2
        + [shape((width // 2, steps * wide), LOW)] * 2,
        scratch_shapes=[
            pltpu.VMEM((width, rows), LOW),
            pltpu.VMEM((steps, 2, width // 2 // steps, rows), LOW),
            pltpu.VMEM((steps, 2, width // 2 // steps, wide), LOW),
        ],
        compiler_params=pltpu.CompilerParams(vmem_limit_bytes=VMEM),
        name="feed_forward",
    )


def norm_kernel(hidden, gain, normed, even, odd, wide):
    rows, width = hidden.shape
    unit, _ = norm_parts(hidden[...].astype(F32))
    normed[...] = (unit * gain[...]).astype(LOW)
    for i in range(width // DH):
        lanes = slice(i * DH, (i + 1) * DH)
        wide[i] = normed[:, lanes].astype(F32)
        even[:, lanes] = wide[i, pl.ds(0, rows // 2, 2), :].astype(LOW)
        odd[:, lanes] = wide[i, pl.ds(1, rows // 2, 2), :].astype(LOW)


def norm_rows(hidden, gain, waits=()):
    rows, width = hidden.shape
    some = rows // 2
    block, half = rows_spec(some, width), rows_spec(some // 2, width)
    shape = jax.ShapeDtypeStruct
    return ordered_call(
        norm_kernel,
        (hidden, gain,),
        waits,
        [block, whole_spec(1, width)],
        grid=(2,),
        out_specs=[block, half, half],
        out_shape=[shape((rows, width), LOW)] + [shape((rows // 2, width), LOW)] * 2,
        scratch_shapes=[pltpu.VMEM((width // DH, some, DH), F32)],
        compiler_params=pltpu.CompilerParams(vmem_limit_bytes=SMALL),
        name="norm_rows",
    )


def project_kernel(own, cmem, mem, normed, weight, cosine, sine, key, value, *query):
    rows, width = cmem.shape
    which, segment = pl.program_id(0), pl.program_id(1)
    times = rows // cosine.shape[1]

    def product(source):
        return dot_nt(source[...], weight[...].reshape(width, width))

    def turned_product(source, out):
        lin = product(source)
        cos = jnp.concatenate([cosine[0]] * times, axis=0)
        sin = jnp.concatenate([sine[0]] * times, axis=0)
        for head in range(width // DH):
            lanes = slice(head * DH, (head + 1) * DH)
            out[:, lanes] = turned(lin[:, lanes], cos, sin).astype(LOW)

    for i, source in enumerate((cmem, mem, normed)):

        @pl.when((segment == i) & (which == 0))
        def _():
            turned_product(source, key.at[0])

        @pl.when((segment == i) & (which == 1))
        def _():
            value[0] = product(source).astype(LOW)

    if own:

        @pl.when((segment == 2) & (which == 2))
        def _():
            turned_product(normed, query[0])


def project(cmem, mem, normed, weights, tables, own, waits=()):
    rows, width = normed.shape
    count, _, unit, _ = weights.shape
    per = width // count // unit
    shape = jax.ShapeDtypeStruct
    whole = pl.BlockSpec((rows, width), lambda w, i: (0, 0))
    tables = [table.reshape(3, -1, DH) for table in tables]
    table = pl.BlockSpec((1,) + tables[0].shape[1:], lambda w, i: (jnp.where(w < 2, i, 2), 0, 0))
    outs = [
        pl.BlockSpec((1, rows, width), lambda w, i: (jnp.where(w == 0, i, 2), 0, 0)),
        pl.BlockSpec(
            (1, rows, width),
            lambda w, i: (jnp.where(w == 0, 0, jnp.where(w == 1, i, 2)), 0, 0),
        ),
    ]
    return ordered_call(
        lambda *refs: project_kernel(own, *refs),
        (cmem, mem, normed, weights, *tables,),
        waits,
        [whole] * 3
        + [pl.BlockSpec((count, per, unit, width), lambda w, i: (0, w, 0, 0))]
        + [table] * 2,
        grid=(3 if own else 2, 3),
        out_specs=outs + [whole] * own,
        out_shape=[shape((3, rows, width), LOW)] * 2 + [shape((rows, width), LOW)] * own,
        compiler_params=pltpu.CompilerParams(vmem_limit_bytes=VMEM),
        name="project",
    )


def weight_grads_kernel(counts, each, core, *refs):
    total_count = sum(counts)
    grads, sources = refs[:total_count], refs[total_count : 2 * total_count]
    *extra, keep, send = refs[2 * total_count :]
    first, at = core[0] == 0, 0
    groups, depth = keep.shape[0], keep.shape[-1]
    for place, count in enumerate(counts):
        total = sum(dot_tn(grads[i][0], sources[i][...]) for i in range(at, at + count))
        at += count
        total = total.astype(LOW).reshape(groups, 2, 2, each, depth)
        rows = slice(place * each, (place + 1) * each)
        keep[:, :, rows] = jnp.where(first, total[:, 0], total[:, 1])
        send[:, :, rows] = jnp.where(first, total[:, 1], total[:, 0])
    if extra:
        rows = slice(len(counts) * each, None)
        keep[:, :, rows] = extra[0][...]
        send[:, :, rows] = extra[1][...]


def weight_grads(core, problems, each, waits=(), extra=()):
    pairs = [pair for problem in problems for pair in problem]
    grads = [g if isinstance(g, tuple) else (g[None], 0) for g, _ in pairs]
    sources = [source for _, source in pairs]
    width, depth = grads[0][0].shape[2], sources[0].shape[1]
    groups = 4
    wide = groups * 4 * each
    more = extra[0].shape[2] if extra else 0

    def spec(array, place):
        return pl.BlockSpec((1, array.shape[1], wide), lambda i: (place, 0, i))

    out = (groups, 2, len(problems) * each + more, depth)
    return ordered_call(
        lambda *refs: weight_grads_kernel([len(p) for p in problems], each, *refs),
        (core.reshape(1), *[array for array, _ in grads], *sources, *extra),
        waits,
        [pl.BlockSpec(memory_space=pltpu.SMEM)]
        + [spec(array, place) for array, place in grads]
        + [whole_spec(*source.shape) for source in sources]
        + [pl.BlockSpec((groups, 2, more, depth), lambda i: (i, 0, 0, 0))] * len(extra),
        grid=(width // wide,),
        out_specs=[pl.BlockSpec(out, lambda i: (i, 0, 0, 0))] * 2,
        out_shape=[jax.ShapeDtypeStruct((width // (4 * each),) + out[1:], LOW)] * 2,
        compiler_params=pltpu.CompilerParams(vmem_limit_bytes=VMEM),
        name="weight_grads",
    )


def weight_spec(weights, which):
    count, _, unit, width = weights.shape
    per = width // count // unit
    return pl.BlockSpec((count, per, unit, width), lambda i: (0, which, 0, 0))


def rows_spec(rows, width):
    return pl.BlockSpec((rows, width), lambda i: (i, 0))


def whole_spec(*dims):
    return pl.BlockSpec(dims, lambda i: (0,) * len(dims))


def far_kernel(late, grad_key, grad_value, comp, w_key, w_value, w_before, out):
    rows, width = out.shape
    total = dot_nn(grad_key[0], w_key[...].reshape(width, width))
    total += dot_nn(grad_value[0], w_value[...].reshape(width, width))
    rim = dot_nn(comp[0, :16], w_before[...].reshape(width, width))[:1] * late[0].astype(F32)
    last = lax.broadcasted_iota(jnp.int32, (rows, width), 0) == rows - 1
    out[...] = (total + jnp.where(last, rim, 0.0)).astype(LOW)


def far_back(late, grad_keys, grad_values, comp_grad, weights, later, waits=()):
    batch, _, width = comp_grad.shape
    rows = grad_keys.shape[1] // batch
    last_part = pl.BlockSpec((1, rows, width), lambda i: (2, i, 0))
    return ordered_call(
        far_kernel,
        (late.reshape(1), grad_keys, grad_values, comp_grad, weights, weights, later,),
        waits,
        [pl.BlockSpec(memory_space=pltpu.SMEM), last_part, last_part]
        + [pl.BlockSpec((1,) + comp_grad.shape[1:], lambda i: (i, 0, 0))]
        + [weight_spec(weights, 0), weight_spec(weights, 1), weight_spec(later, 0)],
        grid=(batch,),
        out_specs=rows_spec(rows, width),
        out_shape=jax.ShapeDtypeStruct((batch * rows, width), LOW),
        compiler_params=pltpu.CompilerParams(vmem_limit_bytes=VMEM),
        name="far_back",
    )


def finish_kernel(
    grad_query, grad_key, grad_value, comp, token, hidden, grad_middle, gain,
    w_query, w_key, w_value, w_before, w_at, grad_in, grad_gain, wide,
):
    rows, width = hidden.shape
    half = rows // 2
    before = dot_nn(comp[0], w_before[...].reshape(width, width))
    before = jnp.where(
        lax.broadcasted_iota(jnp.int32, (half, width), 0) == half - 1,
        0.0,
        pltpu.roll(before, half - 1, 0),
    )
    at = dot_nn(comp[0], w_at[...].reshape(width, width))
    for i in range(width // DH):
        lanes = slice(i * DH, (i + 1) * DH)
        wide[i, pl.ds(0, half, 2), :] = at[:, lanes]
        wide[i, pl.ds(1, half, 2), :] = before[:, lanes]
    grads = jnp.concatenate([wide[i] for i in range(width // DH)], axis=1)
    grads += token[...].astype(F32)
    for left, weight in ((grad_query, w_query), (grad_key, w_key), (grad_value, w_value)):
        grads += dot_nn(left[...].reshape(rows, width), weight[...].reshape(width, width))
    unit, rate = norm_parts(hidden[...].astype(F32))
    total = jnp.sum(grads * unit, axis=0, keepdims=True)
    grad_in[...] = (grad_middle[...] + norm_back(grads, unit, rate, gain[...])).astype(LOW)
    first = pl.program_id(0) == 0

    @pl.when(first)
    def _():
        grad_gain[...] = total

    @pl.when(jnp.logical_not(first))
    def _():
        grad_gain[...] += total


def finish(
    grad_query, grad_keys, grad_values, comp_grad, token, hidden, grad_middle, gain, weights, later, waits=()):
    batch = comp_grad.shape[0]
    rows, width = hidden.shape
    some = rows // batch
    block = rows_spec(some, width)
    last_part = pl.BlockSpec((1, some, width), lambda i: (2, i, 0))
    shape = jax.ShapeDtypeStruct
    return ordered_call(
        finish_kernel,
        (grad_query, grad_keys, grad_values, comp_grad, token, hidden, grad_middle, gain,
        weights, weights, weights, later, later,),
        waits,
        [block, last_part, last_part]
        + [pl.BlockSpec((1,) + comp_grad.shape[1:], lambda i: (i, 0, 0))]
        + [block] * 3
        + [whole_spec(1, width)]
        + [weight_spec(weights, which) for which in (2, 0, 1)]
        + [weight_spec(later, which) for which in (0, 1)],
        grid=(batch,),
        out_specs=[block, whole_spec(1, width)],
        out_shape=[shape((rows, width), LOW), shape((1, width), F32)],
        scratch_shapes=[pltpu.VMEM((width // DH, some, DH), F32)],
        compiler_params=pltpu.CompilerParams(vmem_limit_bytes=VMEM),
        name="finish",
    )


def outputs_kernel(before, at, mask, middle, branch, live, w_before, w_at, compressed, layer_out):
    width = compressed.shape[1]
    total = dot_nt(before[...], w_before[...].reshape(width, width))
    total += dot_nt(at[...], w_at[...].reshape(width, width))
    compressed[...] = (total * mask[...]).astype(LOW)
    layer_out[...] = ((middle[...] + branch[...]) * live[...]).astype(LOW)


def outputs(before, at, mask, middle, branch, live, later, waits=()):
    rows, width = middle.shape
    some, few = rows // 2, at.shape[0] // 2
    shape = jax.ShapeDtypeStruct
    return ordered_call(
        outputs_kernel,
        (before, at, mask, middle, branch, live, later, later),
        waits,
        [rows_spec(few, width), rows_spec(few, width), rows_spec(few, 1)]
        + [rows_spec(some, width), rows_spec(some, width), rows_spec(some, 1)]
        + [weight_spec(later, which) for which in (0, 1)],
        grid=(2,),
        out_specs=[rows_spec(few, width), rows_spec(some, width)],
        out_shape=[shape(at.shape, LOW), shape((rows, width), LOW)],
        compiler_params=pltpu.CompilerParams(vmem_limit_bytes=VMEM),
        name="outputs",
    )


def join_kernel(context, hidden, gain, weight, middle, ffn):
    width = middle.shape[1]
    middle[...] = hidden[...].astype(F32) + dot_nt(
        context[...], weight[...].reshape(width, width)
    )
    unit, _ = norm_parts(middle[...])
    ffn[...] = (unit * gain[...]).astype(LOW)


def join(context, hidden, gain, weights, waits=()):
    rows, width = hidden.shape
    some = rows // 2
    block = rows_spec(some, width)
    shape = jax.ShapeDtypeStruct
    return ordered_call(
        join_kernel,
        (context, hidden, gain, weights,),
        waits,
        [block, block, whole_spec(1, width), weight_spec(weights, 0)],
        grid=(2,),
        out_specs=[block, block],
        out_shape=[shape((rows, width), F32), shape((rows, width), LOW)],
        compiler_params=pltpu.CompilerParams(vmem_limit_bytes=VMEM),
        name="join",
    )


def part_kernel(
    grad_ffn, middle, cot, live, gain, weight, grad_middle, grad_low, grad_context, grad_gain
):
    width = middle.shape[1]
    unit, rate = norm_parts(middle[...])
    grads = grad_ffn[...]
    grad_middle[...] = cot[...].astype(F32) * live[...] + norm_back(
        grads, unit, rate, gain[...]
    )
    grad_low[...] = grad_middle[...].astype(LOW)
    grad_context[...] = dot_nn(grad_low[...], weight[...].reshape(width, width)).astype(LOW)
    total = jnp.sum(grads * unit, axis=0, keepdims=True)
    first = pl.program_id(0) == 0

    @pl.when(first)
    def _():
        grad_gain[...] = total

    @pl.when(jnp.logical_not(first))
    def _():
        grad_gain[...] += total


def part(grad_ffn, middle, cot, live, gain, weights, waits=()):
    rows, width = middle.shape
    some = rows // 2
    block = rows_spec(some, width)
    shape = jax.ShapeDtypeStruct
    return ordered_call(
        part_kernel,
        (grad_ffn, middle, cot, live, gain, weights,),
        waits,
        [block] * 3
        + [rows_spec(some, 1), whole_spec(1, width), weight_spec(weights, 0)],
        grid=(2,),
        out_specs=[block] * 3 + [whole_spec(1, width)],
        out_shape=[
            shape((rows, width), F32),
            shape((rows, width), LOW),
            shape((rows, width), LOW),
            shape((1, width), F32),
        ],
        compiler_params=pltpu.CompilerParams(vmem_limit_bytes=VMEM),
        name="part",
    )


def head_spec(rows):
    return pl.BlockSpec((rows, TOGETHER * DH), lambda b, h: (b, h))


def keys_spec(rows):
    return pl.BlockSpec((3, rows, TOGETHER * DH), lambda b, h: (0, b, h))


def table_spec(rows):
    return pl.BlockSpec((rows, DH), lambda b, h: (0, 0))


def attn_spec(keys, rows):
    return pl.BlockSpec((1, TOGETHER, keys, rows), lambda b, h: (b, h, 0, 0))


def attend(late, query, ka, kb, va, vb, batch, waits=()):
    rows, width = query.shape[0] // batch, query.shape[1]
    keys = 3 * rows
    shape = jax.ShapeDtypeStruct
    return ordered_call(
        attend_kernel,
        (late, query, ka, kb, va, vb,),
        waits,
        [pl.BlockSpec(memory_space=pltpu.SMEM), head_spec(rows)] + [keys_spec(rows)] * 4,
        grid=(batch, H // TOGETHER),
        out_specs=[head_spec(rows)] + [attn_spec(keys, rows)] * 2,
        out_shape=[shape((batch * rows, width), LOW)]
        + [shape((batch, H, keys, rows), LOW)] * 2,
        compiler_params=pltpu.CompilerParams(vmem_limit_bytes=VMEM),
        name="attend",
    )


def attend_back(grad, query, ka, kb, va, vb, pa, pb, tables, batch, waits=()):
    rows, width = query.shape[0] // batch, query.shape[1]
    keys = 3 * rows
    shape = jax.ShapeDtypeStruct
    return ordered_call(
        attend_back_kernel,
        (grad, query, ka, kb, va, vb, pa, pb, *tables,),
        waits,
        [head_spec(rows)] * 2
        + [keys_spec(rows)] * 4
        + [attn_spec(keys, rows)] * 2
        + [table_spec(keys)] * 4,
        grid=(batch, H // TOGETHER),
        out_specs=[head_spec(rows)] + [keys_spec(rows)] * 4,
        out_shape=[shape((batch * rows, width), LOW)]
        + [shape((3, batch * rows, width), LOW)] * 4,
        compiler_params=pltpu.CompilerParams(vmem_limit_bytes=VMEM),
        name="attend_back",
    )


def local_general(
    hidden_in, memory, compressed_in, lengths, gain_attn, gain_ffn,
    w_query, w_key, w_value, w_out, w_up, w_down, w_compress, cot_out, cot_comp,
):
    micro, streams, block, width = hidden_in.shape
    batch = micro * streams
    rows = batch * block
    late = lax.axis_index("tm")
    windows_each = block // COMP

    hidden = hidden_in.reshape(batch, block, width)
    mem = memory.reshape(batch, -1, width)
    cmem = compressed_in.reshape(batch, -1, width)
    hidden_far = swap(hidden, 0)
    mem_far = swap(mem, 0)
    cmem_far = swap(cmem, 0)

    gains = gather(
        jnp.stack([gain_attn, gain_ffn]).reshape(2, 1, -1), gather_order("x_first")
    ).reshape(2, width).astype(F32)
    gain_first, gain_second = gains[0], gains[1]
    key_value = gather(jnp.stack([w_key.T, w_value.T]), gather_order("x_first"))
    query_out = gather(jnp.stack([w_query.T, w_out.T]), gather_order("x_first"))
    up_t = gather(w_up.T[None], gather_order("x"))[0]
    down_t = gather(w_down.T[None], gather_order("y"))[0]
    compress_t = gather(w_compress.T[None], gather_order("y"))[0]
    key_t, value_t = key_value[0], key_value[1]
    query_t, out_t = query_out[0], query_out[1]

    cmem_size, mem_size = cmem.shape[1], mem.shape[1]

    def positions(half):
        return jnp.concatenate(
            [
                COMP * (half * cmem_size + jnp.arange(cmem_size, dtype=jnp.int32) - CMEM) - MEM,
                half * mem_size + jnp.arange(mem_size, dtype=jnp.int32) - MEM,
                half * block + jnp.arange(block, dtype=jnp.int32),
            ]
        )

    tables = turn_tables(positions(late)) + turn_tables(positions(1 - late))
    lens = lengths.reshape(batch)
    query_pos = late * block + jnp.arange(block, dtype=jnp.int32)
    window_end = late * block + COMP * jnp.arange(windows_each, dtype=jnp.int32)
    row_mask = (query_pos[None, :] < lens[:, None]).astype(F32)[..., None]
    window_mask = (window_end[None, :] < lens[:, None]).astype(F32)[..., None]

    inputs = hidden.astype(F32)
    unit, rate = norm_parts(inputs)
    normed = (unit * gain_first).astype(LOW)
    unit_far, _ = norm_parts(hidden_far.astype(F32))
    normed_far = (unit_far * gain_first).astype(LOW)

    rim = normed_far[:, block - 1 :] * (late == 1).astype(LOW)
    padded = jnp.concatenate([rim, normed[:, : block - 1]], axis=1)
    windows = padded.reshape(batch * windows_each, COMP * width)
    comp_grad = (
        (cot_comp.reshape(batch, windows_each, width).astype(F32) * window_mask)
        .astype(LOW)
        .reshape(batch * windows_each, width)
    )
    compressed = dot_nt(windows, compress_t).reshape(batch, windows_each, width) * window_mask
    grad_compress = scatter(dot_tn(comp_grad, windows).astype(LOW), scatter_order("y"))
    grad_windows = dot_nn(comp_grad, compress_t).reshape(batch, block, width)
    rim_grad = swap(grad_windows[:, :1].astype(LOW), 0).astype(F32) * (late == 0).astype(F32)
    grad_shifted = jnp.concatenate([grad_windows[:, 1:], rim_grad], axis=1)

    near = jnp.stack([cmem, mem, normed]).reshape(-1, width)
    far = jnp.stack([cmem_far, mem_far, normed_far]).reshape(-1, width)
    normed = normed.reshape(rows, width)

    def by_head(lin, cosine, sine):
        shape = (-1, batch, block, H, DH)
        cosine, sine = (table.reshape(-1, 1, block, 1, DH) for table in (cosine, sine))
        lin = lin.reshape(shape)
        turn = lin * cosine + jnp.roll(lin, DH // 2, axis=-1) * sine
        return turn.astype(LOW).reshape(-1, rows, width)

    query = by_head(dot_nt(normed, query_t), tables[0][-block:], tables[1][-block:])[0]
    ka = by_head(dot_nt(near, key_t), *tables[:2])
    kb = by_head(dot_nt(far, key_t), *tables[2:])
    va, vb = (
        dot_nt(part, value_t).astype(LOW).reshape(3, rows, width) for part in (near, far)
    )
    context, pa, pb = attend(late.reshape(1), query, ka, kb, va, vb, batch)
    middle = inputs.reshape(rows, width) + dot_nt(context, out_t)

    unit_ffn, rate_ffn = norm_parts(middle)
    ffn = (unit_ffn * gain_second).astype(LOW)
    upper = dot_nt(ffn, up_t)
    slope = math.sqrt(2.0 / math.pi)
    bent = jnp.tanh(slope * (upper + 0.044715 * upper * upper * upper))
    active = (0.5 * upper * (1.0 + bent)).astype(LOW)
    gelu_slope = 0.5 * (1.0 + bent) + 0.5 * upper * (1.0 - bent * bent) * slope * (
        1.0 + 3.0 * 0.044715 * upper * upper
    )
    branch = dot_nt(active, down_t)
    live = row_mask.reshape(rows, 1)
    layer_out = ((middle + branch) * live).astype(LOW)
    grad_live = cot_out.reshape(rows, width).astype(F32) * live
    grad_branch = grad_live.astype(LOW)
    grad_upper = (dot_nn(grad_branch, down_t) * gelu_slope).astype(LOW)
    grad_down = scatter(dot_tn(grad_branch, active).astype(LOW), scatter_order("y"))
    grad_up = scatter(dot_tn(grad_upper, ffn).astype(LOW), scatter_order("x"))
    grad_ffn = dot_nn(grad_upper, up_t)
    grad_gain_ffn = jnp.sum(grad_ffn * unit_ffn, axis=0)
    grad_middle = grad_live + norm_back(grad_ffn, unit_ffn, rate_ffn, gain_second)

    grad_attended = grad_middle.astype(LOW)
    grad_out = scatter(dot_tn(grad_attended, context).astype(LOW), scatter_order("y"))
    grad_context = dot_nn(grad_attended, out_t).astype(LOW)
    gq, *parts = attend_back(grad_context, query, ka, kb, va, vb, pa, pb, tables, batch)
    gka, gkb, gva, gvb = (part.reshape(-1, width) for part in parts)
    grad_value = scatter(
        (dot_tn(gva, near) + dot_tn(gvb, far)).astype(LOW), scatter_order("x")
    )
    grad_key = scatter((dot_tn(gka, near) + dot_tn(gkb, far)).astype(LOW), scatter_order("y"))
    grad_query = scatter(dot_tn(gq, normed).astype(LOW), scatter_order("x"))

    def token_rows(values):
        return values[-rows:]

    token_far = dot_nn(token_rows(gkb), key_t) + dot_nn(token_rows(gvb), value_t)
    token_back = swap(token_far.astype(LOW), 0).astype(F32)
    grad_normed = (
        dot_nn(gq, query_t)
        + dot_nn(token_rows(gka), key_t)
        + dot_nn(token_rows(gva), value_t)
        + grad_shifted.reshape(rows, width)
        + token_back
    )
    unit = unit.reshape(rows, width)
    grad_gain_attn = jnp.sum(grad_normed * unit, axis=0)
    grad_in = grad_middle + norm_back(grad_normed, unit, rate.reshape(rows, 1), gain_first)
    gain_grads = scatter(
        jnp.stack([grad_gain_attn, grad_gain_ffn], axis=1), scatter_order("x"), F32
    )

    return (
        layer_out.reshape(hidden_in.shape),
        compressed.astype(LOW).reshape(cot_comp.shape),
        grad_in.astype(LOW).reshape(hidden_in.shape),
        gain_grads[:, 0],
        gain_grads[:, 1],
        grad_query.T,
        grad_key.T,
        grad_value.T,
        grad_out.T,
        grad_up.T,
        grad_down.T,
        grad_compress.T,
    )


def local(
    hidden_in, memory, compressed_in, lengths, gain_attn, gain_ffn,
    w_query, w_key, w_value, w_out, w_up, w_down, w_compress, cot_out, cot_comp,
):
    count = lax.axis_size(BOTH)
    micro, streams, block, width = hidden_in.shape
    unit_rows, hidden_rows = width // count, w_up.shape[1]
    if unit_rows % 32 or hidden_rows % 128:
        return local_general(
            hidden_in, memory, compressed_in, lengths, gain_attn, gain_ffn,
            w_query, w_key, w_value, w_out, w_up, w_down, w_compress, cot_out, cot_comp,
        )
    batch = micro * streams
    rows = batch * block
    late, core = lax.axis_index("tm"), bit_of(1)
    windows_each = block // COMP
    hidden = hidden_in.reshape(batch, block, width)
    mem = memory.reshape(batch, -1, width)
    cmem = compressed_in.reshape(batch, -1, width)
    high = list(range(bit_count() - 1, 2, -1))
    early = [0] + high + [2, 1]

    half_unit = unit_rows // 2

    def gathered_groups(parts, *waits):
        shard = jnp.concatenate(parts).reshape(1, -1, half_unit, width)
        shard = copied(shard, waits) if waits else shard
        return lax.all_gather(shard, BOTH, axis=0, tiled=True)

    gain_rows = jnp.zeros((half_unit, width), LOW)
    gain_rows = gain_rows.at[0, : 2 * unit_rows].set(jnp.concatenate([gain_attn, gain_ffn]))
    attention_in = gathered_groups([w_key.T, w_value.T, w_query.T, gain_rows])
    out_in = gathered_groups([w_out.T])
    hidden, mem, cmem = (part.reshape(rows, width) for part in (hidden, mem, cmem))
    up_in = Gathering(w_up.T[None], [0] + high + [2])
    down_in = Gathering(w_down.T[None], high + [2, 0])
    hidden_far, cmem_far, mem_far = (swap(part, 0) for part in (hidden, cmem, mem))

    positions = np.concatenate(
        [
            COMP * (np.arange(CMEM) - CMEM) - MEM,
            np.arange(MEM) - MEM,
            np.arange(2 * block),
        ]
    ).astype(np.float32)
    frequency = np.exp(
        np.arange(DH // 2, dtype=np.float32) * np.float32(-2.0 * math.log(ROPE_BASE) / DH)
    ).astype(np.float32)
    angles = positions[:, None] * frequency[None, :]
    turns = np.stack(
        [
            np.concatenate([np.cos(angles), np.cos(angles)], axis=1),
            np.concatenate([-np.sin(angles), np.sin(angles)], axis=1),
        ]
    ).astype(np.float32)
    turns = jnp.asarray(turns.reshape(2, 3, 2, -1, DH))

    def tables_of(half):
        return tuple(lax.dynamic_index_in_dim(turns, half, 2, False).reshape(2, -1, DH))

    tables = tables_of(late) + tables_of(1 - late)
    lens = lengths.reshape(batch)
    query_pos = late * block + jnp.arange(block, dtype=jnp.int32)
    window_end = late * block + COMP * jnp.arange(windows_each, dtype=jnp.int32)
    row_mask = (query_pos[None, :] < lens[:, None]).astype(F32)[..., None]
    window_mask = (window_end[None, :] < lens[:, None]).astype(F32)[..., None]
    live = row_mask.reshape(rows, 1)
    grad_live = cot_out.reshape(rows, width).astype(F32) * live
    grad_branch = grad_live.astype(LOW)

    outward = high[::-1]
    last = down_in.step()
    last = up_in.step(last)
    last = down_in.step(last)
    last = up_in.step(last)

    last = down_in.step(last, grad_branch, *tables)
    last = up_in.step(last)

    gains = (
        attention_in[:, 6, 0, : 2 * unit_rows]
        .reshape(count, 2, unit_rows)
        .transpose(1, 0, 2)
        .reshape(2, width)
        .astype(F32)
    )
    gain_first, gain_second = gains[:1], gains[1:]
    normed, even, odd = norm_rows(hidden, gain_first, (last,))
    ka, va, query = project(cmem, mem, normed, attention_in, tables[:2], True)
    normed_far, _, _ = norm_rows(hidden_far, gain_first, (query,))
    kb, vb = project(cmem_far, mem_far, normed_far, attention_in, tables[2:], False)

    context, pa, pb = attend(late.reshape(1), query, ka, kb, va, vb, batch)
    compress_in = gathered_groups([w_compress[:width].T, w_compress[width:].T], context)
    last = down_in.step(context)
    down_own = last[0]
    down_far = swap(down_own, 1)
    last = up_in.step(last)
    up_own = last[0]
    up_far = swap(up_own, 1)
    middle, ffn = join(context, hidden, gain_second, out_in, (last,))

    steps = count // 4
    branch, grad_ffn, up_keep, up_send, down_keep, down_send = feed_forward(
        core,
        ffn,
        grad_branch,
        up_own.reshape(steps, -1, width),
        up_far.reshape(steps, -1, width),
        down_own,
        down_far,
    )
    up_sum = Chain(up_keep, up_send, [0, 2] + outward, up_keep.shape[2:])
    down_sum = Chain(
        down_keep, down_send, [2, 0] + outward, (unit_rows, hidden_rows * count)
    )

    grad_middle, grad_low, grad_context, grad_gain_ffn = part(
        grad_ffn, middle, cot_out.reshape(rows, width), live, gain_second, out_in
    )
    last = up_sum.step(grad_context)
    last = down_sum.step(last)

    gq, gka, gkb, gva, gvb = attend_back(
        grad_context, query, ka, kb, va, vb, pa, pb, tables, batch, (last,)
    )
    comp_grad = (cot_comp.reshape(batch, windows_each, width).astype(F32) * window_mask).astype(LOW)
    comp_rows = comp_grad.reshape(-1, width)
    far_rows, odd_rows = (value.reshape(batch, -1, width) for value in (normed_far, odd))
    rim = far_rows[:, block - 1 :] * (late == 1).astype(LOW)
    before = jnp.concatenate([rim, odd_rows[:, : windows_each - 1]], axis=1).reshape(-1, width)
    sources = (cmem, mem, normed, cmem_far, mem_far, normed_far)

    def source_problem(near, far):
        grads = [(grad, i) for grad in (near, far) for i in range(3)]
        return list(zip(grads, sources))

    keep, send = weight_grads(
        core, [source_problem(gva, gvb), [(comp_rows, before)], [(comp_rows, even)]], unit_rows
    )
    value_sum = Chain(keep, send, [0, 2] + outward, (3 * unit_rows, width))
    token_far = far_back(late, gkb, gvb, comp_grad, attention_in, compress_in, (keep,))
    token_back = swap(token_far, 0)
    last = up_sum.step(token_far)
    last = down_sum.step(last)
    last = value_sum.step(last)
    keep, send = weight_grads(
        core,
        [source_problem(gka, gkb), [(gq, normed)], [(grad_low, context)]],
        unit_rows,
        (last,),
    )
    key_sum = Chain(keep, send, [2, 0] + outward, (3 * unit_rows, width))
    last = up_sum.step(keep)
    last = key_sum.step(last)

    grad_in, grad_gain_attn = finish(
        gq, gka, gva, comp_grad, token_back, hidden, grad_middle, gain_first,
        attention_in, compress_in, (last,),
    )
    gain_pair = (
        jnp.concatenate([grad_gain_attn, grad_gain_ffn])
        .reshape(2, -1, 2, 2, unit_rows)
        .transpose(2, 1, 3, 0, 4)
        .reshape(2, -1, 2, 1, 2 * unit_rows)
        .astype(LOW)
    )
    gain_pair = jnp.pad(gain_pair, ((0, 0),) * 3 + ((0, 15), (0, DH - 2 * unit_rows)))
    gain_sum = Chain(
        lax.dynamic_index_in_dim(gain_pair, core, 0, keepdims=False),
        lax.dynamic_index_in_dim(gain_pair, 1 - core, 0, keepdims=False),
        [2, 0] + outward,
        (16, DH),
    )
    last = down_sum.step(grad_in)
    last = up_sum.step(last)
    last = gain_sum.step(last)
    compressed, layer_out = outputs(
        before, even, window_mask.reshape(-1, 1), middle, branch, live, compress_in, (last,)
    )
    last = value_sum.step(compressed)
    last = key_sum.step(last)
    last = gain_sum.step(last)
    last = down_sum.step(last)
    last = value_sum.step(last)
    grad_up = up_sum.finish(last)
    last = gain_sum.step(grad_up)
    last = key_sum.step(last)
    last = value_sum.step(last)
    last = gain_sum.step(last)
    grad_down = down_sum.finish(last)
    last = key_sum.step(grad_down)
    grad_value, grad_before, grad_at = jnp.split(value_sum.finish(last), 3)
    gain_grads = gain_sum.finish(grad_value)[0, : 2 * unit_rows]
    grad_key, grad_query, grad_out = jnp.split(key_sum.finish(gain_grads), 3)

    return (
        layer_out.reshape(hidden_in.shape),
        compressed.reshape(cot_comp.shape),
        grad_in.reshape(hidden_in.shape),
        gain_grads[:unit_rows],
        gain_grads[unit_rows:],
        grad_query.T,
        grad_key.T,
        grad_value.T,
        grad_out.T,
        grad_up,
        grad_down.T,
        jnp.concatenate([grad_before.T, grad_at.T]),
    )


def solution(mesh):
    rows = P(None, "dp", "tm", None)
    columns = P(None, BOTH)
    return jax.shard_map(
        local,
        mesh=mesh,
        in_specs=(rows, rows, rows, P(None, "dp"), P(BOTH), P(BOTH))
        + (columns,) * 7
        + (rows, rows),
        out_specs=(rows, rows, rows, P(BOTH), P(BOTH)) + (columns,) * 7,
        check_vma=False,
    )
```

```python
import functools
import math

import jax
import jax.numpy as jnp
import numpy as np
from jax import lax
from jax.experimental import pallas as pl
from jax.experimental.pallas import tpu as pltpu
from jax.sharding import PartitionSpec as P

H = 8
DH = 128
MEM = 512
CMEM = 512
COMP = 2

EPSILON = 1e-05
ROPE_BASE = 10000.0
NEG_LARGE = -1e30
SCALE = 1.0 / math.sqrt(DH)
BOTH = ("dp", "tm")
LOW = jnp.bfloat16
F32 = jnp.float32


VMEM = 60 * 2**20
TOGETHER = 2
SMALL = 16 * 2**20
LONG = pl.CostEstimate(flops=10**11, bytes_accessed=2**20, transcendentals=0)


def bit_of(bit):
    return (lax.axis_index("dp") * lax.axis_size("tm") + lax.axis_index("tm")) >> bit & 1


def swap(value, bit):
    count = lax.axis_size(BOTH)
    return lax.ppermute(value, BOTH, [(i, i ^ (1 << bit)) for i in range(count)])


def bit_count():
    return lax.axis_size(BOTH).bit_length() - 1


def ordered_call(kernel, args, waits, in_specs, **settings):
    count, more = len(args), len(waits)

    def body(*refs):
        kernel(*refs[:count], *refs[count + more :])

    return pl.pallas_call(
        body,
        in_specs=list(in_specs) + [pl.BlockSpec(memory_space=pl.ANY)] * more,
        cost_estimate=LONG,
        **settings,
    )(*args, *waits)


def gate_kernel(value, out):
    pass


def gate(value, *waits):
    anywhere = pl.BlockSpec(memory_space=pl.ANY)
    return ordered_call(
        gate_kernel,
        (value,),
        waits,
        [anywhere],
        out_specs=anywhere,
        out_shape=jax.ShapeDtypeStruct(value.shape, value.dtype),
        input_output_aliases={0: 0},
        compiler_params=pltpu.CompilerParams(vmem_limit_bytes=VMEM),
        name="gate",
    )


def copy_kernel(value, out):
    out[...] = value[...]


def copied(value, waits):
    block = pl.BlockSpec(value.shape, lambda i: (0,) * value.ndim)
    return ordered_call(
        copy_kernel,
        (value,),
        waits,
        [block],
        grid=(1,),
        out_specs=block,
        out_shape=jax.ShapeDtypeStruct(value.shape, value.dtype),
        compiler_params=pltpu.CompilerParams(vmem_limit_bytes=VMEM),
        name="copied",
    )


def merge_kernel(mine, own, other, out):
    out[:, mine[0]] = own[...]
    out[:, 1 - mine[0]] = other[...]


def merged(own, other, mine, before, waits):
    width = own.shape[-1]
    own, other = own.reshape(before, -1, width), other.reshape(before, -1, width)
    rest = own.shape[1]
    each = max(1, min(before, 2**18 // (rest * width)))
    block = pl.BlockSpec((each, rest, width), lambda i: (i, 0, 0))
    return ordered_call(
        merge_kernel,
        (mine.reshape(1), own, other),
        waits,
        [pl.BlockSpec(memory_space=pltpu.SMEM), block, block],
        grid=(before // each,),
        out_specs=pl.BlockSpec((each, 2, rest, width), lambda i: (i, 0, 0, 0)),
        out_shape=jax.ShapeDtypeStruct((before, 2, rest, width), own.dtype),
        compiler_params=pltpu.CompilerParams(vmem_limit_bytes=VMEM),
        name="merge",
    )


class Gathering:
    def __init__(self, shard, order):
        self.held, self.order, self.done = shard, list(order), []
        self.lead, self.width = shard.shape[0], shard.shape[-1]
        self.other = swap(shard, order[0])

    def step(self, *waits):
        bit = self.order.pop(0)
        before = self.lead * 2 ** sum(1 for d in self.done if d > bit)
        self.held = merged(self.held, self.other, bit_of(bit), before, waits).reshape(
            self.lead, -1, self.width
        )
        self.done.append(bit)
        if self.order:
            self.other = swap(self.held, self.order[0])
        return self.held


def combine_kernel(count, mine, *refs):
    refs, out = refs[:count], refs[-1]
    total = sum(ref[...].reshape(out.shape).astype(F32) for ref in refs)
    out[...] = total.astype(out.dtype)


def combine_both_kernel(count, axis, bit, mine, *refs):
    refs, (send, kept) = refs[:count], refs[-2:]
    shape = kept.shape[:axis] + (2,) + kept.shape[axis:]
    total = sum(ref[...].reshape(shape).astype(F32) for ref in refs)
    zero, one = (lax.index_in_dim(total, i, axis, keepdims=False) for i in range(2))
    first = mine[bit] == 0
    send[...] = jnp.where(first, one, zero).astype(LOW)
    kept[...] = jnp.where(first, zero, one)


def combined(terms, rest, bit, done, free, waits, both=False):
    whole, size = [], math.prod(rest)
    for b in reversed(free):
        if size < 2**18:
            whole, size = whole + [b], size * 2
    stepped = [b for b in free if b not in whole]

    def spec(bits):
        def index(g, mine):
            place = []
            for b in bits:
                if b == bit:
                    place.append(0 if both else 1 - mine[b])
                elif b in done:
                    place.append(mine[b])
                elif b in whole:
                    place.append(0)
                else:
                    place.append(g >> (len(stepped) - 1 - stepped.index(b)) & 1)
            return tuple(place) + (0,) * len(rest)

        dims = tuple(2 if b in whole or (both and b == bit) else 1 for b in bits)
        return pl.BlockSpec(dims + rest, index)

    out = jax.ShapeDtypeStruct((2,) * len(free) + rest, F32 if bit is None else LOW)
    if both:
        axis = sum(1 for b in free if b > bit)
        kernel = lambda *refs: combine_both_kernel(len(terms), axis, bit, *refs)
        outs, out_specs = [out, jax.ShapeDtypeStruct(out.shape, F32)], [spec(free)] * 2
    else:
        kernel = lambda *refs: combine_kernel(len(terms), *refs)
        outs, out_specs = out, spec(free)
    large = sum(term.size for term, _ in terms) > 2**21
    return pl.pallas_call(
        kernel,
        grid_spec=pltpu.PrefetchScalarGridSpec(
            num_scalar_prefetch=1,
            grid=(2 ** len(stepped),),
            in_specs=[spec(bits) for _, bits in terms]
            + [pl.BlockSpec(memory_space=pl.ANY)] * len(waits),
            out_specs=out_specs,
        ),
        out_shape=outs,
        compiler_params=pltpu.CompilerParams(vmem_limit_bytes=VMEM if large else SMALL),
        cost_estimate=LONG,
        name="combine",
    )(jnp.stack([bit_of(b) for b in range(bit_count())]), *[term for term, _ in terms], *waits)


def round_kernel(plans, mine, *refs):
    ins, outs = refs[: sum(plan[0] for plan in plans)], refs[-sum(1 + plan[3] for plan in plans) :]
    at, out_at = 0, 0
    for count, axis, bit, both in plans:
        terms, at = ins[at : at + count], at + count
        if both:
            send, kept = outs[out_at : out_at + 2]
            combine_both_kernel(count, axis, bit, mine, *terms, send, kept)
        else:
            combine_kernel(count, mine, *terms, outs[out_at])
        out_at += 1 + both


def round_of(chains, waits):
    in_specs, out_specs, outs, args, plans = [], [], [], [], []
    for chain in chains:
        bit = chain.order.pop(0) if chain.order else None
        free = [b for b in chain.bits if b != bit]
        both = bit is not None and len(chain.done) > 1

        def spec(bits, bit=bit, free=free, both=both, done=tuple(chain.done), rest=chain.rest):
            def index(g, mine):
                place = [
                    (0 if both else 1 - mine[b]) if b == bit else mine[b] if b in done else 0
                    for b in bits
                ]
                return tuple(place) + (0,) * len(rest)

            dims = tuple(2 if b in free or (both and b == bit) else 1 for b in bits)
            return pl.BlockSpec(dims + rest, index)

        for term, bits in chain.terms:
            args.append(term)
            in_specs.append(spec(bits))
        shape = (2,) * len(free) + chain.rest
        outs.append(jax.ShapeDtypeStruct(shape, F32 if bit is None else LOW))
        outs.extend([jax.ShapeDtypeStruct(shape, F32)] * both)
        out_specs.extend([spec(free)] * (1 + both))
        axis = sum(1 for b in free if bit is not None and b > bit)
        plans.append((len(chain.terms), axis, bit, both))
    results = list(
        pl.pallas_call(
            lambda *refs: round_kernel(plans, *refs),
            grid_spec=pltpu.PrefetchScalarGridSpec(
                num_scalar_prefetch=1,
                grid=(1,),
                in_specs=in_specs + [pl.BlockSpec(memory_space=pl.ANY)] * len(waits),
                out_specs=out_specs,
            ),
            out_shape=outs,
            compiler_params=pltpu.CompilerParams(vmem_limit_bytes=VMEM),
            cost_estimate=LONG,
            name="round",
        )(jnp.stack([bit_of(b) for b in range(bit_count())]), *args, *waits)
    )
    last = results[0]
    for chain, (_, _, bit, both) in zip(chains, plans):
        send = results.pop(0)
        if bit is None:
            chain.total = send
            continue
        chain.bits = [b for b in chain.bits if b != bit]
        if both:
            chain.terms = [(results.pop(0), chain.bits)]
        chain.done.append(bit)
        chain.terms.append((swap(send, bit), chain.bits))
    return last


class Chain:
    def __init__(self, keep, send, order, rest):
        self.bits = [b for b in range(bit_count() - 1, -1, -1) if b != 1]
        self.rest = rest
        shape = (2,) * len(self.bits) + rest
        self.terms = [
            (keep.reshape(shape), self.bits),
            (swap(send.reshape(shape), 1), self.bits),
        ]
        self.order, self.done = list(order), [1]

    def step(self, *waits):
        bit = self.order.pop(0)
        self.bits = [b for b in self.bits if b != bit]
        both = len(self.done) > 1
        send = combined(self.terms, self.rest, bit, self.done, self.bits, waits, both)
        if both:
            send, kept = send
            self.terms = [(kept, self.bits)]
        self.done.append(bit)
        self.terms.append((swap(send, bit), self.bits))
        return send

    def finish(self, *waits):
        return combined(self.terms, self.rest, None, self.done, [], waits)


def gather_order(last):
    high = list(range(bit_count() - 1, 2, -1))
    return {"y": high + [0, 2, 1], "x": high + [2, 0, 1], "x_first": [0] + high + [2, 1]}[last]


def gather(shard, order):
    held, done = shard, []
    for bit in order:
        other = swap(held, bit)
        mine = bit_of(bit) == 1
        axis = 1 + sum(1 for d in done if d > bit)
        held = jnp.stack(
            [jnp.where(mine, other, held), jnp.where(mine, held, other)], axis=axis
        )
        done.append(bit)
    return held.reshape(shard.shape[0], -1, shard.shape[2])


def scatter(whole, order, kept=LOW):
    count = lax.axis_size(BOTH)
    bits = bit_count()
    held = whole.reshape((2,) * bits + (whole.shape[0] // count, whole.shape[1]))
    left = list(range(bits))
    for bit in order:
        axis = sum(1 for d in left if d > bit)
        mine = bit_of(bit)
        other = swap(lax.dynamic_index_in_dim(held, 1 - mine, axis, keepdims=False), bit)
        keep = lax.dynamic_index_in_dim(held, mine, axis, keepdims=False)
        left.remove(bit)
        held = keep.astype(F32) + other.astype(F32)
        if left:
            held = held.astype(kept)
    return held


def scatter_order(first):
    high = list(range(3, bit_count()))
    return {"y": [1, 2, 0] + high, "x": [1, 0, 2] + high}[first]


def norm_parts(values):
    centre = values - jnp.mean(values, axis=-1, keepdims=True)
    spread = jnp.mean(centre * centre, axis=-1, keepdims=True)
    rate = lax.rsqrt(spread + EPSILON)
    return centre * rate, rate


def norm_back(grad, unit, rate, gain):
    scaled = grad * gain
    return rate * (
        scaled
        - jnp.mean(scaled, axis=-1, keepdims=True)
        - unit * jnp.mean(scaled * unit, axis=-1, keepdims=True)
    )


def turn_tables(positions):
    half = DH // 2
    frequency = jnp.exp(jnp.arange(half, dtype=F32) * (-2.0 * math.log(ROPE_BASE) / DH))
    angles = positions.astype(F32)[:, None] * frequency[None, :]
    cosine, sine = jnp.cos(angles), jnp.sin(angles)
    return (
        jnp.concatenate([cosine, cosine], axis=1),
        jnp.concatenate([-sine, sine], axis=1),
    )


def turned(values, cosine, sine):
    return values * cosine + pltpu.roll(values, DH // 2, 1) * sine


def unturned(values, cosine, sine):
    return values * cosine - pltpu.roll(values, DH // 2, 1) * sine


def dot_nt(left, right):
    return lax.dot_general(left, right, (((1,), (1,)), ((), ())), preferred_element_type=F32)


def dot_nn(left, right):
    return lax.dot_general(left, right, (((1,), (0,)), ((), ())), preferred_element_type=F32)


def dot_tn(left, right):
    return lax.dot_general(left, right, (((0,), (0,)), ((), ())), preferred_element_type=F32)


def attend_kernel(late, query, ka, kb, va, vb, context, pa_out, pb_out):
    rows = query.shape[0]
    base = SCALE * math.log2(math.e)
    sides = ((ka, va, pa_out), (kb, vb, pb_out))
    for head in range(query.shape[1] // DH):
        lanes = slice(head * DH, (head + 1) * DH)
        scores = []
        for side, (key, _, _) in enumerate(sides):
            for part in range(3):
                score = dot_nt(key[part, :, lanes], query[:, lanes])
                if part == 2:
                    key_at = lax.broadcasted_iota(jnp.int32, (rows, rows), 0)
                    if side == 0:
                        seen = key_at <= lax.broadcasted_iota(jnp.int32, (rows, rows), 1)
                    else:
                        seen = key_at < late[0] * rows
                    score = jnp.where(seen, score, NEG_LARGE)
                scores.append(score)
        top = functools.reduce(jnp.maximum, scores)
        top = jnp.max(top, axis=0, keepdims=True) * base
        exps = [jnp.exp2(score * base - top) for score in scores]
        total = jnp.sum(sum(exps), axis=0, keepdims=True)
        share = 1.0 / total
        mixed = 0.0
        for i, value in enumerate(exps):
            attn = (value * share).astype(LOW)
            side, part = divmod(i, 3)
            sides[side][2][0, head, part * rows : (part + 1) * rows, :] = attn
            mixed += dot_tn(sides[side][1][part, :, lanes], attn)
        context[:, lanes] = mixed.T.astype(LOW)


def attend_back_kernel(
    grad, query, ka, kb, va, vb, pa, pb, cos_a, sin_a, cos_b, sin_b,
    gq_out, gka_out, gkb_out, gva_out, gvb_out,
):
    rows = query.shape[0]
    lead = 2 * rows
    sides = (
        (ka, va, pa, cos_a, sin_a, gka_out, gva_out),
        (kb, vb, pb, cos_b, sin_b, gkb_out, gvb_out),
    )
    for head in range(query.shape[1] // DH):
        lanes = slice(head * DH, (head + 1) * DH)
        here, own = grad[:, lanes], query[:, lanes]
        backs, inner = [], 0.0
        for _, value, attn, _, _, _, out in sides:
            for part in range(3):
                weights = attn[0, head, part * rows : (part + 1) * rows, :]
                back = dot_nt(value[part, :, lanes], here)
                inner += weights.astype(F32) * back
                out[part, :, lanes] = dot_nn(weights, here).astype(LOW)
                backs.append(back)
        inner = jnp.sum(inner, axis=0, keepdims=True)
        mixed = 0.0
        for i, back in enumerate(backs):
            side, part = divmod(i, 3)
            key, _, attn, cosine, sine, out, _ = sides[side]
            at = slice(part * rows, (part + 1) * rows)
            score = (attn[0, head, at, :].astype(F32) * (back - inner)).astype(LOW)
            grads = dot_nn(score, own) * SCALE
            out[part, :, lanes] = unturned(grads, cosine[at, :], sine[at, :]).astype(LOW)
            mixed += dot_tn(key[part, :, lanes], score)
        gq_out[:, lanes] = unturned(mixed.T * SCALE, cos_a[lead:, :], sin_a[lead:, :]).astype(LOW)


def feed_kernel(
    mine, ffn, grad, up_a_own, up_a_far, up_b_own, up_b_far,
    down_p_own, down_p_far, down_q_own, down_q_far,
    branch, grad_ffn, up_keep, up_send, down_keep, down_send, ffn_t, grad_t, up_nat, down_nat,
):
    half = up_a_own.shape[1]
    core, across = mine[0], mine[2]
    own_at = pl.multiple_of(core * half, half)
    far_at = pl.multiple_of((1 - core) * half, half)
    step = pl.program_id(0)
    first = step == 0
    group, _, _, each, _ = down_nat.shape

    @pl.when(first)
    def _():
        ffn_t[...] = ffn[...].T
        grad_t[...] = grad[...].T.reshape(grad_t.shape)

    for place, (own, far) in enumerate(((up_a_own, up_a_far), (up_b_own, up_b_far))):

        @pl.when(step % 2 == place)
        def _():
            up_nat[:half] = own[0]
            up_nat[half:] = far[0]

    for ref, at_core, at in (
        (down_p_own, core, across),
        (down_p_far, 1 - core, across),
        (down_q_own, core, 1 - across),
        (down_q_far, 1 - core, 1 - across),
    ):
        down_nat[:, at_core, at, :, :half] = ref[:, pl.ds(own_at, half)].reshape(group, each, half)
        down_nat[:, at_core, at, :, half:] = ref[:, pl.ds(far_at, half)].reshape(group, each, half)
    up_rows = up_nat[...]
    down_rows = down_nat[...].reshape(-1, 2 * half)
    upper = dot_nt(ffn[...], up_rows)
    slope = math.sqrt(2.0 / math.pi)
    square = upper * upper
    bent = jnp.tanh(slope * upper * (1.0 + 0.044715 * square))
    share = 0.5 + 0.5 * bent
    active = (upper * share).astype(LOW)
    gelu_slope = share + 0.5 * upper * (1.0 - bent * bent) * (
        slope + (3.0 * 0.044715 * slope) * square
    )
    grad_hidden = (dot_nn(grad[...], down_rows) * gelu_slope).astype(LOW)
    more_out = dot_nt(active, down_rows)
    more_grad = dot_nn(grad_hidden, up_rows)

    @pl.when(first)
    def _():
        branch[...] = more_out
        grad_ffn[...] = more_grad

    @pl.when(jnp.logical_not(first))
    def _():
        branch[...] += more_out
        grad_ffn[...] += more_grad

    for ref, at in ((up_keep, 0), (up_send, half)):
        part = dot_nn(ffn_t[...], grad_hidden[:, at : at + half]).astype(LOW)
        ref[0, 0] = part[:, : half // 2]
        ref[0, 1] = part[:, half // 2 :]
    for ref, at in ((down_keep, core), (down_send, 1 - core)):
        part = dot_nn(grad_t[:, at].reshape(group * 2 * each, -1), active).astype(LOW)
        ref[:, pl.ds(own_at, half)] = part[:, :half]
        ref[:, pl.ds(far_at, half)] = part[:, half:]


def feed_forward(mine, ffn, grad_branch, up_parts, down_parts):
    rows, width = ffn.shape
    groups, half = up_parts[0].shape[:2]
    steps, wide = 2 * groups, 2 * half

    def whole(*dims):
        return pl.BlockSpec(dims, lambda t, m: (0,) * len(dims))

    def place(t, m):
        return t // 2 * 2 + (m[1] + t) % 2

    shape = jax.ShapeDtypeStruct
    up_in = pl.BlockSpec((1, half, width), lambda t, m: (t // 2, 0, 0))
    up_out = pl.BlockSpec((1, 2, width, half // 2), lambda t, m: (place(t, m), 0, 0, 0))

    def lanes(count):
        return pl.BlockSpec((count, wide), lambda t, m: (0, place(t, m)))

    return pl.pallas_call(
        feed_kernel,
        grid_spec=pltpu.PrefetchScalarGridSpec(
            num_scalar_prefetch=1,
            grid=(steps,),
            in_specs=[whole(rows, width)] * 2 + [up_in] * 4 + [lanes(width // 4)] * 4,
            out_specs=[whole(rows, width)] * 2 + [up_out] * 2 + [lanes(width // 2)] * 2,
            scratch_shapes=[
                pltpu.VMEM((width, rows), LOW),
                pltpu.VMEM((steps, 2, width // 2 // steps, rows), LOW),
                pltpu.VMEM((wide, width), LOW),
                pltpu.VMEM((steps, 2, 2, width // 4 // steps, wide), LOW),
            ],
        ),
        out_shape=[shape((rows, width), F32)] * 2
        + [shape((steps, 2, width, half // 2), LOW)] * 2
        + [shape((width // 2, steps * wide), LOW)] * 2,
        compiler_params=pltpu.CompilerParams(vmem_limit_bytes=VMEM),
        cost_estimate=LONG,
        name="feed_forward",
    )(mine, ffn, grad_branch, *up_parts, *down_parts)


def norm_kernel(hidden, gain, normed, even, odd, wide):
    rows, width = hidden.shape
    unit, _ = norm_parts(hidden[...].astype(F32))
    normed[...] = (unit * gain[...]).astype(LOW)
    for i in range(width // DH):
        lanes = slice(i * DH, (i + 1) * DH)
        wide[i] = normed[:, lanes].astype(F32)
        even[:, lanes] = wide[i, pl.ds(0, rows // 2, 2), :].astype(LOW)
        odd[:, lanes] = wide[i, pl.ds(1, rows // 2, 2), :].astype(LOW)


def norm_rows(hidden, gain, waits=()):
    rows, width = hidden.shape
    some = rows // 2
    block, half = rows_spec(some, width), rows_spec(some // 2, width)
    shape = jax.ShapeDtypeStruct
    return ordered_call(
        norm_kernel,
        (hidden, gain,),
        waits,
        [block, whole_spec(1, width)],
        grid=(2,),
        out_specs=[block, half, half],
        out_shape=[shape((rows, width), LOW)] + [shape((rows // 2, width), LOW)] * 2,
        scratch_shapes=[pltpu.VMEM((width // DH, some, DH), F32)],
        compiler_params=pltpu.CompilerParams(vmem_limit_bytes=VMEM),
        name="norm_rows",
    )


def project_kernel(own, cmem, mem, normed, weight, cosine, sine, key, value, *query):
    rows, width = cmem.shape
    which, segment = pl.program_id(0), pl.program_id(1)
    times = rows // cosine.shape[1]

    def product(source):
        return dot_nt(source[...], weight[...].reshape(width, width))

    def turned_product(source, out):
        lin = product(source)
        cos = jnp.concatenate([cosine[0]] * times, axis=0)
        sin = jnp.concatenate([sine[0]] * times, axis=0)
        for head in range(width // DH):
            lanes = slice(head * DH, (head + 1) * DH)
            out[:, lanes] = turned(lin[:, lanes], cos, sin).astype(LOW)

    for i, source in enumerate((cmem, mem, normed)):

        @pl.when((segment == i) & (which == 0))
        def _():
            turned_product(source, key.at[0])

        @pl.when((segment == i) & (which == 1))
        def _():
            value[0] = product(source).astype(LOW)

    if own:

        @pl.when((segment == 2) & (which == 2))
        def _():
            turned_product(normed, query[0])


def project(cmem, mem, normed, weights, tables, own, waits=()):
    rows, width = normed.shape
    count, _, unit, _ = weights.shape
    per = width // count // unit
    shape = jax.ShapeDtypeStruct
    whole = pl.BlockSpec((rows, width), lambda w, i: (0, 0))
    tables = [table.reshape(3, -1, DH) for table in tables]
    table = pl.BlockSpec((1,) + tables[0].shape[1:], lambda w, i: (jnp.where(w < 2, i, 2), 0, 0))
    outs = [
        pl.BlockSpec((1, rows, width), lambda w, i: (jnp.where(w == 0, i, 2), 0, 0)),
        pl.BlockSpec(
            (1, rows, width),
            lambda w, i: (jnp.where(w == 0, 0, jnp.where(w == 1, i, 2)), 0, 0),
        ),
    ]
    return ordered_call(
        lambda *refs: project_kernel(own, *refs),
        (cmem, mem, normed, weights, *tables,),
        waits,
        [whole] * 3
        + [pl.BlockSpec((count, per, unit, width), lambda w, i: (0, w, 0, 0))]
        + [table] * 2,
        grid=(3 if own else 2, 3),
        out_specs=outs + [whole] * own,
        out_shape=[shape((3, rows, width), LOW)] * 2 + [shape((rows, width), LOW)] * own,
        compiler_params=pltpu.CompilerParams(vmem_limit_bytes=VMEM),
        name="project",
    )


def weight_grads_kernel(counts, each, core, *refs):
    total_count = sum(counts)
    grads, sources = refs[:total_count], refs[total_count : 2 * total_count]
    *extra, keep, send = refs[2 * total_count :]
    first, at = core[0] == 0, 0
    groups, depth = keep.shape[0], keep.shape[-1]
    for place, count in enumerate(counts):
        total = sum(dot_tn(grads[i][0], sources[i][...]) for i in range(at, at + count))
        at += count
        total = total.astype(LOW).reshape(groups, 2, 2, each, depth)
        rows = slice(place * each, (place + 1) * each)
        keep[:, :, rows] = jnp.where(first, total[:, 0], total[:, 1])
        send[:, :, rows] = jnp.where(first, total[:, 1], total[:, 0])
    if extra:
        rows = slice(len(counts) * each, None)
        keep[:, :, rows] = extra[0][...]
        send[:, :, rows] = extra[1][...]


def weight_grads(core, problems, each, waits=(), extra=()):
    pairs = [pair for problem in problems for pair in problem]
    grads = [g if isinstance(g, tuple) else (g[None], 0) for g, _ in pairs]
    sources = [source for _, source in pairs]
    width, depth = grads[0][0].shape[2], sources[0].shape[1]
    groups = 4
    wide = groups * 4 * each
    more = extra[0].shape[2] if extra else 0

    def spec(array, place):
        return pl.BlockSpec((1, array.shape[1], wide), lambda i: (place, 0, i))

    out = (groups, 2, len(problems) * each + more, depth)
    return ordered_call(
        lambda *refs: weight_grads_kernel([len(p) for p in problems], each, *refs),
        (core.reshape(1), *[array for array, _ in grads], *sources, *extra),
        waits,
        [pl.BlockSpec(memory_space=pltpu.SMEM)]
        + [spec(array, place) for array, place in grads]
        + [whole_spec(*source.shape) for source in sources]
        + [pl.BlockSpec((groups, 2, more, depth), lambda i: (i, 0, 0, 0))] * len(extra),
        grid=(width // wide,),
        out_specs=[pl.BlockSpec(out, lambda i: (i, 0, 0, 0))] * 2,
        out_shape=[jax.ShapeDtypeStruct((width // (4 * each),) + out[1:], LOW)] * 2,
        compiler_params=pltpu.CompilerParams(vmem_limit_bytes=VMEM),
        name="weight_grads",
    )


def weight_spec(weights, which):
    count, _, unit, width = weights.shape
    per = width // count // unit
    return pl.BlockSpec((count, per, unit, width), lambda i: (0, which, 0, 0))


def rows_spec(rows, width):
    return pl.BlockSpec((rows, width), lambda i: (i, 0))


def whole_spec(*dims):
    return pl.BlockSpec(dims, lambda i: (0,) * len(dims))


def far_kernel(late, grad_key, grad_value, comp, w_key, w_value, w_before, out):
    rows, width = out.shape
    total = dot_nn(grad_key[0], w_key[...].reshape(width, width))
    total += dot_nn(grad_value[0], w_value[...].reshape(width, width))
    rim = dot_nn(comp[0, :16], w_before[...].reshape(width, width))[:1] * late[0].astype(F32)
    last = lax.broadcasted_iota(jnp.int32, (rows, width), 0) == rows - 1
    out[...] = (total + jnp.where(last, rim, 0.0)).astype(LOW)


def far_back(late, grad_keys, grad_values, comp_grad, weights, later, waits=()):
    batch, _, width = comp_grad.shape
    rows = grad_keys.shape[1] // batch
    last_part = pl.BlockSpec((1, rows, width), lambda i: (2, i, 0))
    return ordered_call(
        far_kernel,
        (late.reshape(1), grad_keys, grad_values, comp_grad, weights, weights, later,),
        waits,
        [pl.BlockSpec(memory_space=pltpu.SMEM), last_part, last_part]
        + [pl.BlockSpec((1,) + comp_grad.shape[1:], lambda i: (i, 0, 0))]
        + [weight_spec(weights, 0), weight_spec(weights, 1), weight_spec(later, 0)],
        grid=(batch,),
        out_specs=rows_spec(rows, width),
        out_shape=jax.ShapeDtypeStruct((batch * rows, width), LOW),
        compiler_params=pltpu.CompilerParams(vmem_limit_bytes=VMEM),
        name="far_back",
    )


def finish_kernel(
    grad_query, grad_key, grad_value, comp, token, hidden, grad_middle, gain,
    w_query, w_key, w_value, w_before, w_at, grad_in, grad_gain, wide,
):
    rows, width = hidden.shape
    half = rows // 2
    before = dot_nn(comp[0], w_before[...].reshape(width, width))
    before = jnp.where(
        lax.broadcasted_iota(jnp.int32, (half, width), 0) == half - 1,
        0.0,
        pltpu.roll(before, half - 1, 0),
    )
    at = dot_nn(comp[0], w_at[...].reshape(width, width))
    for i in range(width // DH):
        lanes = slice(i * DH, (i + 1) * DH)
        wide[i, pl.ds(0, half, 2), :] = at[:, lanes]
        wide[i, pl.ds(1, half, 2), :] = before[:, lanes]
    grads = jnp.concatenate([wide[i] for i in range(width // DH)], axis=1)
    grads += token[...].astype(F32)
    for left, weight in ((grad_query, w_query), (grad_key, w_key), (grad_value, w_value)):
        grads += dot_nn(left[...].reshape(rows, width), weight[...].reshape(width, width))
    unit, rate = norm_parts(hidden[...].astype(F32))
    total = jnp.sum(grads * unit, axis=0, keepdims=True)
    grad_in[...] = (grad_middle[...] + norm_back(grads, unit, rate, gain[...])).astype(LOW)
    first = pl.program_id(0) == 0

    @pl.when(first)
    def _():
        grad_gain[...] = total

    @pl.when(jnp.logical_not(first))
    def _():
        grad_gain[...] += total


def finish(
    grad_query, grad_keys, grad_values, comp_grad, token, hidden, grad_middle, gain, weights, later, waits=()):
    batch = comp_grad.shape[0]
    rows, width = hidden.shape
    some = rows // batch
    block = rows_spec(some, width)
    last_part = pl.BlockSpec((1, some, width), lambda i: (2, i, 0))
    shape = jax.ShapeDtypeStruct
    return ordered_call(
        finish_kernel,
        (grad_query, grad_keys, grad_values, comp_grad, token, hidden, grad_middle, gain,
        weights, weights, weights, later, later,),
        waits,
        [block, last_part, last_part]
        + [pl.BlockSpec((1,) + comp_grad.shape[1:], lambda i: (i, 0, 0))]
        + [block] * 3
        + [whole_spec(1, width)]
        + [weight_spec(weights, which) for which in (2, 0, 1)]
        + [weight_spec(later, which) for which in (0, 1)],
        grid=(batch,),
        out_specs=[block, whole_spec(1, width)],
        out_shape=[shape((rows, width), LOW), shape((1, width), F32)],
        scratch_shapes=[pltpu.VMEM((width // DH, some, DH), F32)],
        compiler_params=pltpu.CompilerParams(vmem_limit_bytes=VMEM),
        name="finish",
    )


def outputs_kernel(before, at, mask, middle, branch, live, w_before, w_at, compressed, layer_out):
    width = compressed.shape[1]
    total = dot_nt(before[...], w_before[...].reshape(width, width))
    total += dot_nt(at[...], w_at[...].reshape(width, width))
    compressed[...] = (total * mask[...]).astype(LOW)
    layer_out[...] = ((middle[...] + branch[...]) * live[...]).astype(LOW)


def outputs(before, at, mask, middle, branch, live, later, waits=()):
    rows, width = middle.shape
    some, few = rows // 2, at.shape[0] // 2
    shape = jax.ShapeDtypeStruct
    return ordered_call(
        outputs_kernel,
        (before, at, mask, middle, branch, live, later, later),
        waits,
        [rows_spec(few, width), rows_spec(few, width), rows_spec(few, 1)]
        + [rows_spec(some, width), rows_spec(some, width), rows_spec(some, 1)]
        + [weight_spec(later, which) for which in (0, 1)],
        grid=(2,),
        out_specs=[rows_spec(few, width), rows_spec(some, width)],
        out_shape=[shape(at.shape, LOW), shape((rows, width), LOW)],
        compiler_params=pltpu.CompilerParams(vmem_limit_bytes=VMEM),
        name="outputs",
    )


def join_kernel(context, hidden, gain, weight, middle, ffn):
    width = middle.shape[1]
    middle[...] = hidden[...].astype(F32) + dot_nt(
        context[...], weight[...].reshape(width, width)
    )
    unit, _ = norm_parts(middle[...])
    ffn[...] = (unit * gain[...]).astype(LOW)


def join(context, hidden, gain, weights, waits=()):
    rows, width = hidden.shape
    some = rows // 2
    block = rows_spec(some, width)
    shape = jax.ShapeDtypeStruct
    return ordered_call(
        join_kernel,
        (context, hidden, gain, weights,),
        waits,
        [block, block, whole_spec(1, width), weight_spec(weights, 0)],
        grid=(2,),
        out_specs=[block, block],
        out_shape=[shape((rows, width), F32), shape((rows, width), LOW)],
        compiler_params=pltpu.CompilerParams(vmem_limit_bytes=VMEM),
        name="join",
    )


def part_kernel(
    grad_ffn, middle, cot, live, gain, weight, grad_middle, grad_low, grad_context, grad_gain
):
    width = middle.shape[1]
    unit, rate = norm_parts(middle[...])
    grads = grad_ffn[...]
    grad_middle[...] = cot[...].astype(F32) * live[...] + norm_back(
        grads, unit, rate, gain[...]
    )
    grad_low[...] = grad_middle[...].astype(LOW)
    grad_context[...] = dot_nn(grad_low[...], weight[...].reshape(width, width)).astype(LOW)
    total = jnp.sum(grads * unit, axis=0, keepdims=True)
    first = pl.program_id(0) == 0

    @pl.when(first)
    def _():
        grad_gain[...] = total

    @pl.when(jnp.logical_not(first))
    def _():
        grad_gain[...] += total


def part(grad_ffn, middle, cot, live, gain, weights, waits=()):
    rows, width = middle.shape
    some = rows // 2
    block = rows_spec(some, width)
    shape = jax.ShapeDtypeStruct
    return ordered_call(
        part_kernel,
        (grad_ffn, middle, cot, live, gain, weights,),
        waits,
        [block] * 3
        + [rows_spec(some, 1), whole_spec(1, width), weight_spec(weights, 0)],
        grid=(2,),
        out_specs=[block] * 3 + [whole_spec(1, width)],
        out_shape=[
            shape((rows, width), F32),
            shape((rows, width), LOW),
            shape((rows, width), LOW),
            shape((1, width), F32),
        ],
        compiler_params=pltpu.CompilerParams(vmem_limit_bytes=VMEM),
        name="part",
    )


def head_spec(rows):
    return pl.BlockSpec((rows, TOGETHER * DH), lambda b, h: (b, h))


def keys_spec(rows):
    return pl.BlockSpec((3, rows, TOGETHER * DH), lambda b, h: (0, b, h))


def table_spec(rows):
    return pl.BlockSpec((rows, DH), lambda b, h: (0, 0))


def attn_spec(keys, rows):
    return pl.BlockSpec((1, TOGETHER, keys, rows), lambda b, h: (b, h, 0, 0))


def attend(late, query, ka, kb, va, vb, batch, waits=()):
    rows, width = query.shape[0] // batch, query.shape[1]
    keys = 3 * rows
    shape = jax.ShapeDtypeStruct
    return ordered_call(
        attend_kernel,
        (late, query, ka, kb, va, vb,),
        waits,
        [pl.BlockSpec(memory_space=pltpu.SMEM), head_spec(rows)] + [keys_spec(rows)] * 4,
        grid=(batch, H // TOGETHER),
        out_specs=[head_spec(rows)] + [attn_spec(keys, rows)] * 2,
        out_shape=[shape((batch * rows, width), LOW)]
        + [shape((batch, H, keys, rows), LOW)] * 2,
        compiler_params=pltpu.CompilerParams(vmem_limit_bytes=VMEM),
        name="attend",
    )


def attend_back(grad, query, ka, kb, va, vb, pa, pb, tables, batch, waits=()):
    rows, width = query.shape[0] // batch, query.shape[1]
    keys = 3 * rows
    shape = jax.ShapeDtypeStruct
    return ordered_call(
        attend_back_kernel,
        (grad, query, ka, kb, va, vb, pa, pb, *tables,),
        waits,
        [head_spec(rows)] * 2
        + [keys_spec(rows)] * 4
        + [attn_spec(keys, rows)] * 2
        + [table_spec(keys)] * 4,
        grid=(batch, H // TOGETHER),
        out_specs=[head_spec(rows)] + [keys_spec(rows)] * 4,
        out_shape=[shape((batch * rows, width), LOW)]
        + [shape((3, batch * rows, width), LOW)] * 4,
        compiler_params=pltpu.CompilerParams(vmem_limit_bytes=VMEM),
        name="attend_back",
    )


def local_general(
    hidden_in, memory, compressed_in, lengths, gain_attn, gain_ffn,
    w_query, w_key, w_value, w_out, w_up, w_down, w_compress, cot_out, cot_comp,
):
    micro, streams, block, width = hidden_in.shape
    batch = micro * streams
    rows = batch * block
    late = lax.axis_index("tm")
    windows_each = block // COMP

    hidden = hidden_in.reshape(batch, block, width)
    mem = memory.reshape(batch, -1, width)
    cmem = compressed_in.reshape(batch, -1, width)
    hidden_far = swap(hidden, 0)
    mem_far = swap(mem, 0)
    cmem_far = swap(cmem, 0)

    gains = gather(
        jnp.stack([gain_attn, gain_ffn]).reshape(2, 1, -1), gather_order("x_first")
    ).reshape(2, width).astype(F32)
    gain_first, gain_second = gains[0], gains[1]
    key_value = gather(jnp.stack([w_key.T, w_value.T]), gather_order("x_first"))
    query_out = gather(jnp.stack([w_query.T, w_out.T]), gather_order("x_first"))
    up_t = gather(w_up.T[None], gather_order("x"))[0]
    down_t = gather(w_down.T[None], gather_order("y"))[0]
    compress_t = gather(w_compress.T[None], gather_order("y"))[0]
    key_t, value_t = key_value[0], key_value[1]
    query_t, out_t = query_out[0], query_out[1]

    cmem_size, mem_size = cmem.shape[1], mem.shape[1]

    def positions(half):
        return jnp.concatenate(
            [
                COMP * (half * cmem_size + jnp.arange(cmem_size, dtype=jnp.int32) - CMEM) - MEM,
                half * mem_size + jnp.arange(mem_size, dtype=jnp.int32) - MEM,
                half * block + jnp.arange(block, dtype=jnp.int32),
            ]
        )

    tables = turn_tables(positions(late)) + turn_tables(positions(1 - late))
    lens = lengths.reshape(batch)
    query_pos = late * block + jnp.arange(block, dtype=jnp.int32)
    window_end = late * block + COMP * jnp.arange(windows_each, dtype=jnp.int32)
    row_mask = (query_pos[None, :] < lens[:, None]).astype(F32)[..., None]
    window_mask = (window_end[None, :] < lens[:, None]).astype(F32)[..., None]

    inputs = hidden.astype(F32)
    unit, rate = norm_parts(inputs)
    normed = (unit * gain_first).astype(LOW)
    unit_far, _ = norm_parts(hidden_far.astype(F32))
    normed_far = (unit_far * gain_first).astype(LOW)

    rim = normed_far[:, block - 1 :] * (late == 1).astype(LOW)
    padded = jnp.concatenate([rim, normed[:, : block - 1]], axis=1)
    windows = padded.reshape(batch * windows_each, COMP * width)
    comp_grad = (
        (cot_comp.reshape(batch, windows_each, width).astype(F32) * window_mask)
        .astype(LOW)
        .reshape(batch * windows_each, width)
    )
    compressed = dot_nt(windows, compress_t).reshape(batch, windows_each, width) * window_mask
    grad_compress = scatter(dot_tn(comp_grad, windows).astype(LOW), scatter_order("y"))
    grad_windows = dot_nn(comp_grad, compress_t).reshape(batch, block, width)
    rim_grad = swap(grad_windows[:, :1].astype(LOW), 0).astype(F32) * (late == 0).astype(F32)
    grad_shifted = jnp.concatenate([grad_windows[:, 1:], rim_grad], axis=1)

    near = jnp.stack([cmem, mem, normed]).reshape(-1, width)
    far = jnp.stack([cmem_far, mem_far, normed_far]).reshape(-1, width)
    normed = normed.reshape(rows, width)

    def by_head(lin, cosine, sine):
        shape = (-1, batch, block, H, DH)
        cosine, sine = (table.reshape(-1, 1, block, 1, DH) for table in (cosine, sine))
        lin = lin.reshape(shape)
        turn = lin * cosine + jnp.roll(lin, DH // 2, axis=-1) * sine
        return turn.astype(LOW).reshape(-1, rows, width)

    query = by_head(dot_nt(normed, query_t), tables[0][-block:], tables[1][-block:])[0]
    ka = by_head(dot_nt(near, key_t), *tables[:2])
    kb = by_head(dot_nt(far, key_t), *tables[2:])
    va, vb = (
        dot_nt(part, value_t).astype(LOW).reshape(3, rows, width) for part in (near, far)
    )
    context, pa, pb = attend(late.reshape(1), query, ka, kb, va, vb, batch)
    middle = inputs.reshape(rows, width) + dot_nt(context, out_t)

    unit_ffn, rate_ffn = norm_parts(middle)
    ffn = (unit_ffn * gain_second).astype(LOW)
    upper = dot_nt(ffn, up_t)
    slope = math.sqrt(2.0 / math.pi)
    bent = jnp.tanh(slope * (upper + 0.044715 * upper * upper * upper))
    active = (0.5 * upper * (1.0 + bent)).astype(LOW)
    gelu_slope = 0.5 * (1.0 + bent) + 0.5 * upper * (1.0 - bent * bent) * slope * (
        1.0 + 3.0 * 0.044715 * upper * upper
    )
    branch = dot_nt(active, down_t)
    live = row_mask.reshape(rows, 1)
    layer_out = ((middle + branch) * live).astype(LOW)
    grad_live = cot_out.reshape(rows, width).astype(F32) * live
    grad_branch = grad_live.astype(LOW)
    grad_upper = (dot_nn(grad_branch, down_t) * gelu_slope).astype(LOW)
    grad_down = scatter(dot_tn(grad_branch, active).astype(LOW), scatter_order("y"))
    grad_up = scatter(dot_tn(grad_upper, ffn).astype(LOW), scatter_order("x"))
    grad_ffn = dot_nn(grad_upper, up_t)
    grad_gain_ffn = jnp.sum(grad_ffn * unit_ffn, axis=0)
    grad_middle = grad_live + norm_back(grad_ffn, unit_ffn, rate_ffn, gain_second)

    grad_attended = grad_middle.astype(LOW)
    grad_out = scatter(dot_tn(grad_attended, context).astype(LOW), scatter_order("y"))
    grad_context = dot_nn(grad_attended, out_t).astype(LOW)
    gq, *parts = attend_back(grad_context, query, ka, kb, va, vb, pa, pb, tables, batch)
    gka, gkb, gva, gvb = (part.reshape(-1, width) for part in parts)
    grad_value = scatter(
        (dot_tn(gva, near) + dot_tn(gvb, far)).astype(LOW), scatter_order("x")
    )
    grad_key = scatter((dot_tn(gka, near) + dot_tn(gkb, far)).astype(LOW), scatter_order("y"))
    grad_query = scatter(dot_tn(gq, normed).astype(LOW), scatter_order("x"))

    def token_rows(values):
        return values[-rows:]

    token_far = dot_nn(token_rows(gkb), key_t) + dot_nn(token_rows(gvb), value_t)
    token_back = swap(token_far.astype(LOW), 0).astype(F32)
    grad_normed = (
        dot_nn(gq, query_t)
        + dot_nn(token_rows(gka), key_t)
        + dot_nn(token_rows(gva), value_t)
        + grad_shifted.reshape(rows, width)
        + token_back
    )
    unit = unit.reshape(rows, width)
    grad_gain_attn = jnp.sum(grad_normed * unit, axis=0)
    grad_in = grad_middle + norm_back(grad_normed, unit, rate.reshape(rows, 1), gain_first)
    gain_grads = scatter(
        jnp.stack([grad_gain_attn, grad_gain_ffn], axis=1), scatter_order("x"), F32
    )

    return (
        layer_out.reshape(hidden_in.shape),
        compressed.astype(LOW).reshape(cot_comp.shape),
        grad_in.astype(LOW).reshape(hidden_in.shape),
        gain_grads[:, 0],
        gain_grads[:, 1],
        grad_query.T,
        grad_key.T,
        grad_value.T,
        grad_out.T,
        grad_up.T,
        grad_down.T,
        grad_compress.T,
    )


def local(
    hidden_in, memory, compressed_in, lengths, gain_attn, gain_ffn,
    w_query, w_key, w_value, w_out, w_up, w_down, w_compress, cot_out, cot_comp,
):
    count = lax.axis_size(BOTH)
    micro, streams, block, width = hidden_in.shape
    unit_rows, hidden_rows = width // count, w_up.shape[1]
    if unit_rows % 32 or hidden_rows % 128:
        return local_general(
            hidden_in, memory, compressed_in, lengths, gain_attn, gain_ffn,
            w_query, w_key, w_value, w_out, w_up, w_down, w_compress, cot_out, cot_comp,
        )
    batch = micro * streams
    rows = batch * block
    late, core = lax.axis_index("tm"), bit_of(1)
    windows_each = block // COMP
    hidden = hidden_in.reshape(batch, block, width)
    mem = memory.reshape(batch, -1, width)
    cmem = compressed_in.reshape(batch, -1, width)
    high = list(range(bit_count() - 1, 2, -1))
    early = [0] + high + [2, 1]

    half_unit = unit_rows // 2

    def gathered_groups(parts, *waits):
        shard = jnp.concatenate(parts).reshape(1, -1, half_unit, width)
        shard = copied(shard, waits) if waits else shard
        return shard, lax.all_gather(shard, BOTH, axis=0, tiled=True)

    gain_rows = jnp.zeros((half_unit, width), LOW)
    gain_rows = gain_rows.at[0, : 2 * unit_rows].set(jnp.concatenate([gain_attn, gain_ffn]))
    _, attention_in = gathered_groups([w_key.T, w_value.T, w_query.T, gain_rows])
    _, out_in = gathered_groups([w_out.T])
    hidden, mem, cmem = (part.reshape(rows, width) for part in (hidden, mem, cmem))
    up_in = Gathering(w_up.T[None], [0] + high + [2])
    down_in = Gathering(w_down.T[None], high + [2, 0])
    hidden_far, cmem_far, mem_far = (swap(part, 0) for part in (hidden, cmem, mem))

    positions = np.concatenate(
        [
            COMP * (np.arange(CMEM) - CMEM) - MEM,
            np.arange(MEM) - MEM,
            np.arange(2 * block),
        ]
    ).astype(np.float32)
    frequency = np.exp(
        np.arange(DH // 2, dtype=np.float32) * np.float32(-2.0 * math.log(ROPE_BASE) / DH)
    ).astype(np.float32)
    angles = positions[:, None] * frequency[None, :]
    turns = np.stack(
        [
            np.concatenate([np.cos(angles), np.cos(angles)], axis=1),
            np.concatenate([-np.sin(angles), np.sin(angles)], axis=1),
        ]
    ).astype(np.float32)
    turns = jnp.asarray(turns.reshape(2, 3, 2, -1, DH))

    def tables_of(half):
        return tuple(lax.dynamic_index_in_dim(turns, half, 2, False).reshape(2, -1, DH))

    tables = tables_of(late) + tables_of(1 - late)
    lens = lengths.reshape(batch)
    query_pos = late * block + jnp.arange(block, dtype=jnp.int32)
    window_end = late * block + COMP * jnp.arange(windows_each, dtype=jnp.int32)
    row_mask = (query_pos[None, :] < lens[:, None]).astype(F32)[..., None]
    window_mask = (window_end[None, :] < lens[:, None]).astype(F32)[..., None]
    live = row_mask.reshape(rows, 1)
    grad_live = cot_out.reshape(rows, width).astype(F32) * live
    grad_branch = grad_live.astype(LOW)

    outward = high[::-1]
    last = down_in.step()
    last = up_in.step(last)
    last = down_in.step(last)
    last = up_in.step(last)


    ones = jnp.ones((1, width), F32)
    _, unit_even, unit_odd = norm_rows(hidden, ones, (last,))
    unit_far, _, _ = norm_rows(hidden_far, ones, (unit_even,))

    def rows_before(far_rows, odd_rows):
        far_rows, odd_rows = (value.reshape(batch, -1, width) for value in (far_rows, odd_rows))
        rim = far_rows[:, block - 1 :] * (late == 1).astype(LOW)
        return jnp.concatenate([rim, odd_rows[:, : windows_each - 1]], axis=1).reshape(-1, width)

    comp_grad = (cot_comp.reshape(batch, windows_each, width).astype(F32) * window_mask).astype(LOW)
    comp_rows = comp_grad.reshape(-1, width)
    keep, send = weight_grads(
        core,
        [[(comp_rows, rows_before(unit_far, unit_odd))], [(comp_rows, unit_even)]],
        unit_rows,
    )
    compress_sum = Chain(keep, send, outward + [2, 0], (2 * unit_rows, width))
    last = down_in.step(keep, grad_branch, *tables)
    last = up_in.step(last)
    last = compress_sum.step(last)
    up_held, up_other, down_held, down_other = (
        part.reshape(shape)
        for chain, shape in (
            (up_in, (count // 8, -1, width)),
            (down_in, (-1, hidden_rows * count)),
        )
        for part in (chain.held, chain.other)
    )

    gains = (
        attention_in[:, 6, 0, : 2 * unit_rows]
        .reshape(count, 2, unit_rows)
        .transpose(1, 0, 2)
        .reshape(2, width)
        .astype(F32)
    )
    gain_first, gain_second = gains[:1], gains[1:]
    normed, even, odd = norm_rows(hidden, gain_first, (last,))
    ka, va, query = project(cmem, mem, normed, attention_in, tables[:2], True)
    normed_far, _, _ = norm_rows(hidden_far, gain_first, (query,))
    kb, vb = project(cmem_far, mem_far, normed_far, attention_in, tables[2:], False)

    context, pa, pb = attend(late.reshape(1), query, ka, kb, va, vb, batch)
    last, compress_in = gathered_groups([w_compress[:width].T, w_compress[width:].T], context)
    up_other, down_other = gate(up_other, last), gate(down_other, last)
    up_parts = [up_held, swap(up_held, 1), up_other, swap(up_other, 1)]
    down_parts = [down_held, swap(down_held, 1), down_other, swap(down_other, 1)]
    middle, ffn = join(context, hidden, gain_second, out_in, (last,))

    branch, grad_ffn, up_keep, up_send, down_keep, down_send = feed_forward(
        jnp.stack([core, bit_of(2), late]), ffn, grad_branch, up_parts, down_parts
    )
    up_sum = Chain(up_keep, up_send, [0, 2] + outward, up_keep.shape[2:])
    down_sum = Chain(
        down_keep, down_send, [2, 0] + outward, (unit_rows, hidden_rows * count)
    )

    grad_middle, grad_low, grad_context, grad_gain_ffn = part(
        grad_ffn, middle, cot_out.reshape(rows, width), live, gain_second, out_in
    )
    last = up_sum.step(grad_context)
    last = down_sum.step(last)

    gq, gka, gkb, gva, gvb = attend_back(
        grad_context, query, ka, kb, va, vb, pa, pb, tables, batch, (last,)
    )
    before = rows_before(normed_far, odd)
    sources = (cmem, mem, normed, cmem_far, mem_far, normed_far)

    def source_problem(near, far):
        grads = [(grad, i) for grad in (near, far) for i in range(3)]
        return list(zip(grads, sources))

    keep, send = weight_grads(
        core, [source_problem(gva, gvb), [(grad_low, context)]], unit_rows
    )
    value_sum = Chain(keep, send, [2, 0] + outward, (2 * unit_rows, width))
    token_far = far_back(late, gkb, gvb, comp_grad, attention_in, compress_in, (keep,))
    token_back = swap(token_far, 0)
    last = up_sum.step(token_far)
    last = down_sum.step(last)
    last = value_sum.step(last)
    keep, send = weight_grads(
        core, [source_problem(gka, gkb), [(gq, normed)]], unit_rows, (last,)
    )
    key_sum = Chain(keep, send, [0, 2] + outward, (2 * unit_rows, width))
    last = up_sum.step(keep)
    last = key_sum.step(last)
    last = compress_sum.step(last)

    grad_in, grad_gain_attn = finish(
        gq, gka, gva, comp_grad, token_back, hidden, grad_middle, gain_first,
        attention_in, compress_in, (last,),
    )
    gain_pair = (
        jnp.concatenate([grad_gain_attn, grad_gain_ffn])
        .reshape(2, -1, 2, 2, unit_rows)
        .transpose(2, 1, 3, 0, 4)
        .reshape(2, -1, 2, 1, 2 * unit_rows)
        .astype(LOW)
    )
    gain_pair = jnp.pad(gain_pair, ((0, 0),) * 3 + ((0, 15), (0, DH - 2 * unit_rows)))
    gain_sum = Chain(
        lax.dynamic_index_in_dim(gain_pair, core, 0, keepdims=False),
        lax.dynamic_index_in_dim(gain_pair, 1 - core, 0, keepdims=False),
        [2, 0] + outward,
        (16, DH),
    )
    last = round_of([value_sum, down_sum, up_sum], (grad_in,))
    last = round_of([key_sum, gain_sum], (last,))
    last = round_of([value_sum, down_sum, compress_sum], (last,))
    last = round_of([key_sum, gain_sum, up_sum], (last,))
    last = round_of([value_sum, compress_sum], (last,))
    last = round_of([key_sum, down_sum, gain_sum], (last,))
    compressed, layer_out = outputs(
        before, even, window_mask.reshape(-1, 1), middle, branch, live, compress_in, (last,)
    )
    last = round_of([value_sum, compress_sum], (compressed,))
    last = round_of([key_sum, gain_sum], (last,))
    round_of([gain_sum], (last,))
    grad_value, grad_out = jnp.split(value_sum.total, 2)
    grad_before, grad_at = jnp.split(compress_sum.total * gain_first, 2)
    gain_grads = gain_sum.total[0, : 2 * unit_rows]
    grad_key, grad_query = jnp.split(key_sum.total, 2)

    return (
        layer_out.reshape(hidden_in.shape),
        compressed.reshape(cot_comp.shape),
        grad_in.reshape(hidden_in.shape),
        gain_grads[:unit_rows],
        gain_grads[unit_rows:],
        grad_query.T,
        grad_key.T,
        grad_value.T,
        grad_out.T,
        up_sum.total,
        down_sum.total.T,
        jnp.concatenate([grad_before.T, grad_at.T]),
    )


def solution(mesh):
    rows = P(None, "dp", "tm", None)
    columns = P(None, BOTH)
    return jax.shard_map(
        local,
        mesh=mesh,
        in_specs=(rows, rows, rows, P(None, "dp"), P(BOTH), P(BOTH))
        + (columns,) * 7
        + (rows, rows),
        out_specs=(rows, rows, rows, P(BOTH), P(BOTH)) + (columns,) * 7,
        check_vma=False,
    )
```

```python
import functools
import math

import jax
import jax.numpy as jnp
import numpy as np
from jax import lax
from jax.experimental import pallas as pl
from jax.experimental.pallas import tpu as pltpu
from jax.sharding import PartitionSpec as P

H = 8
DH = 128
MEM = 512
CMEM = 512
COMP = 2

EPSILON = 1e-05
ROPE_BASE = 10000.0
NEG_LARGE = -1e30
SCALE = 1.0 / math.sqrt(DH)
BOTH = ("dp", "tm")
LOW = jnp.bfloat16
F32 = jnp.float32


VMEM = 60 * 2**20
TOGETHER = 2
SMALL = 16 * 2**20
LONG = pl.CostEstimate(flops=10**11, bytes_accessed=2**20, transcendentals=0)


def bit_of(bit):
    return (lax.axis_index("dp") * lax.axis_size("tm") + lax.axis_index("tm")) >> bit & 1


def swap(value, bit):
    count = lax.axis_size(BOTH)
    return lax.ppermute(value, BOTH, [(i, i ^ (1 << bit)) for i in range(count)])


def bit_count():
    return lax.axis_size(BOTH).bit_length() - 1


def ordered_call(kernel, args, waits, in_specs, **settings):
    count, more = len(args), len(waits)

    def body(*refs):
        kernel(*refs[:count], *refs[count + more :])

    return pl.pallas_call(
        body,
        in_specs=list(in_specs) + [pl.BlockSpec(memory_space=pl.ANY)] * more,
        cost_estimate=LONG,
        **settings,
    )(*args, *waits)


def gate_kernel(value, out):
    pass


def gate(value, *waits):
    anywhere = pl.BlockSpec(memory_space=pl.ANY)
    return ordered_call(
        gate_kernel,
        (value,),
        waits,
        [anywhere],
        out_specs=anywhere,
        out_shape=jax.ShapeDtypeStruct(value.shape, value.dtype),
        input_output_aliases={0: 0},
        compiler_params=pltpu.CompilerParams(vmem_limit_bytes=VMEM),
        name="gate",
    )


def copy_kernel(value, out):
    out[...] = value[...]


def copied(value, waits):
    block = pl.BlockSpec(value.shape, lambda i: (0,) * value.ndim)
    return ordered_call(
        copy_kernel,
        (value,),
        waits,
        [block],
        grid=(1,),
        out_specs=block,
        out_shape=jax.ShapeDtypeStruct(value.shape, value.dtype),
        compiler_params=pltpu.CompilerParams(vmem_limit_bytes=VMEM),
        name="copied",
    )


def merge_kernel(mine, own, other, out):
    out[:, mine[0]] = own[...]
    out[:, 1 - mine[0]] = other[...]


def merged(own, other, mine, before, waits):
    width = own.shape[-1]
    own, other = own.reshape(before, -1, width), other.reshape(before, -1, width)
    rest = own.shape[1]
    each = max(1, min(before, 2**18 // (rest * width)))
    block = pl.BlockSpec((each, rest, width), lambda i: (i, 0, 0))
    return ordered_call(
        merge_kernel,
        (mine.reshape(1), own, other),
        waits,
        [pl.BlockSpec(memory_space=pltpu.SMEM), block, block],
        grid=(before // each,),
        out_specs=pl.BlockSpec((each, 2, rest, width), lambda i: (i, 0, 0, 0)),
        out_shape=jax.ShapeDtypeStruct((before, 2, rest, width), own.dtype),
        compiler_params=pltpu.CompilerParams(vmem_limit_bytes=VMEM),
        name="merge",
    )


class Gathering:
    def __init__(self, shard, order):
        self.held, self.order, self.done = shard, list(order), []
        self.lead, self.width = shard.shape[0], shard.shape[-1]
        self.other = swap(shard, order[0])

    def step(self, *waits):
        bit = self.order.pop(0)
        before = self.lead * 2 ** sum(1 for d in self.done if d > bit)
        self.held = merged(self.held, self.other, bit_of(bit), before, waits).reshape(
            self.lead, -1, self.width
        )
        self.done.append(bit)
        if self.order:
            self.other = swap(self.held, self.order[0])
        return self.held


def combine_kernel(count, mine, *refs):
    refs, out = refs[:count], refs[-1]
    total = sum(ref[...].reshape(out.shape).astype(F32) for ref in refs)
    out[...] = total.astype(out.dtype)


def combine_both_kernel(count, axis, bit, mine, *refs):
    refs, (send, kept) = refs[:count], refs[-2:]
    shape = kept.shape[:axis] + (2,) + kept.shape[axis:]
    total = sum(ref[...].reshape(shape).astype(F32) for ref in refs)
    zero, one = (lax.index_in_dim(total, i, axis, keepdims=False) for i in range(2))
    first = mine[bit] == 0
    send[...] = jnp.where(first, one, zero).astype(LOW)
    kept[...] = jnp.where(first, zero, one)


def combined(terms, rest, bit, done, free, waits, both=False):
    whole, size = [], math.prod(rest)
    for b in reversed(free):
        if size < 2**18:
            whole, size = whole + [b], size * 2
    stepped = [b for b in free if b not in whole]

    def spec(bits):
        def index(g, mine):
            place = []
            for b in bits:
                if b == bit:
                    place.append(0 if both else 1 - mine[b])
                elif b in done:
                    place.append(mine[b])
                elif b in whole:
                    place.append(0)
                else:
                    place.append(g >> (len(stepped) - 1 - stepped.index(b)) & 1)
            return tuple(place) + (0,) * len(rest)

        dims = tuple(2 if b in whole or (both and b == bit) else 1 for b in bits)
        return pl.BlockSpec(dims + rest, index)

    out = jax.ShapeDtypeStruct((2,) * len(free) + rest, F32 if bit is None else LOW)
    if both:
        axis = sum(1 for b in free if b > bit)
        kernel = lambda *refs: combine_both_kernel(len(terms), axis, bit, *refs)
        outs, out_specs = [out, jax.ShapeDtypeStruct(out.shape, F32)], [spec(free)] * 2
    else:
        kernel = lambda *refs: combine_kernel(len(terms), *refs)
        outs, out_specs = out, spec(free)
    large = sum(term.size for term, _ in terms) > 2**21
    return pl.pallas_call(
        kernel,
        grid_spec=pltpu.PrefetchScalarGridSpec(
            num_scalar_prefetch=1,
            grid=(2 ** len(stepped),),
            in_specs=[spec(bits) for _, bits in terms]
            + [pl.BlockSpec(memory_space=pl.ANY)] * len(waits),
            out_specs=out_specs,
        ),
        out_shape=outs,
        compiler_params=pltpu.CompilerParams(vmem_limit_bytes=VMEM if large else SMALL),
        cost_estimate=LONG,
        name="combine",
    )(jnp.stack([bit_of(b) for b in range(bit_count())]), *[term for term, _ in terms], *waits)


def round_kernel(plans, mine, *refs):
    ins, outs = refs[: sum(plan[0] for plan in plans)], refs[-sum(1 + plan[3] for plan in plans) :]
    at, out_at = 0, 0
    for count, axis, bit, both in plans:
        terms, at = ins[at : at + count], at + count
        if both:
            send, kept = outs[out_at : out_at + 2]
            combine_both_kernel(count, axis, bit, mine, *terms, send, kept)
        else:
            combine_kernel(count, mine, *terms, outs[out_at])
        out_at += 1 + both


def round_of(chains, waits):
    in_specs, out_specs, outs, args, plans = [], [], [], [], []
    for chain in chains:
        bit = chain.order.pop(0) if chain.order else None
        free = [b for b in chain.bits if b != bit]
        both = bit is not None and len(chain.done) > 1

        def spec(bits, bit=bit, free=free, both=both, done=tuple(chain.done), rest=chain.rest):
            def index(g, mine):
                place = [
                    (0 if both else 1 - mine[b]) if b == bit else mine[b] if b in done else 0
                    for b in bits
                ]
                return tuple(place) + (0,) * len(rest)

            dims = tuple(2 if b in free or (both and b == bit) else 1 for b in bits)
            return pl.BlockSpec(dims + rest, index)

        for term, bits in chain.terms:
            args.append(term)
            in_specs.append(spec(bits))
        shape = (2,) * len(free) + chain.rest
        outs.append(jax.ShapeDtypeStruct(shape, F32 if bit is None else LOW))
        outs.extend([jax.ShapeDtypeStruct(shape, F32)] * both)
        out_specs.extend([spec(free)] * (1 + both))
        axis = sum(1 for b in free if bit is not None and b > bit)
        plans.append((len(chain.terms), axis, bit, both))
    results = list(
        pl.pallas_call(
            lambda *refs: round_kernel(plans, *refs),
            grid_spec=pltpu.PrefetchScalarGridSpec(
                num_scalar_prefetch=1,
                grid=(1,),
                in_specs=in_specs + [pl.BlockSpec(memory_space=pl.ANY)] * len(waits),
                out_specs=out_specs,
            ),
            out_shape=outs,
            compiler_params=pltpu.CompilerParams(vmem_limit_bytes=VMEM),
            cost_estimate=LONG,
            name="round",
        )(jnp.stack([bit_of(b) for b in range(bit_count())]), *args, *waits)
    )
    last = results[0]
    for chain, (_, _, bit, both) in zip(chains, plans):
        send = results.pop(0)
        if bit is None:
            chain.total = send
            continue
        chain.bits = [b for b in chain.bits if b != bit]
        if both:
            chain.terms = [(results.pop(0), chain.bits)]
        chain.done.append(bit)
        chain.terms.append((swap(send, bit), chain.bits))
    return last


class Chain:
    def __init__(self, keep, send, order, rest):
        self.bits = [b for b in range(bit_count() - 1, -1, -1) if b != 1]
        self.rest = rest
        shape = (2,) * len(self.bits) + rest
        self.terms = [
            (keep.reshape(shape), self.bits),
            (swap(send.reshape(shape), 1), self.bits),
        ]
        self.order, self.done = list(order), [1]

    def step(self, *waits):
        bit = self.order.pop(0)
        self.bits = [b for b in self.bits if b != bit]
        both = len(self.done) > 1
        send = combined(self.terms, self.rest, bit, self.done, self.bits, waits, both)
        if both:
            send, kept = send
            self.terms = [(kept, self.bits)]
        self.done.append(bit)
        self.terms.append((swap(send, bit), self.bits))
        return send

    def finish(self, *waits):
        return combined(self.terms, self.rest, None, self.done, [], waits)


def gather_order(last):
    high = list(range(bit_count() - 1, 2, -1))
    return {"y": high + [0, 2, 1], "x": high + [2, 0, 1], "x_first": [0] + high + [2, 1]}[last]


def gather(shard, order):
    held, done = shard, []
    for bit in order:
        other = swap(held, bit)
        mine = bit_of(bit) == 1
        axis = 1 + sum(1 for d in done if d > bit)
        held = jnp.stack(
            [jnp.where(mine, other, held), jnp.where(mine, held, other)], axis=axis
        )
        done.append(bit)
    return held.reshape(shard.shape[0], -1, shard.shape[2])


def scatter(whole, order, kept=LOW):
    count = lax.axis_size(BOTH)
    bits = bit_count()
    held = whole.reshape((2,) * bits + (whole.shape[0] // count, whole.shape[1]))
    left = list(range(bits))
    for bit in order:
        axis = sum(1 for d in left if d > bit)
        mine = bit_of(bit)
        other = swap(lax.dynamic_index_in_dim(held, 1 - mine, axis, keepdims=False), bit)
        keep = lax.dynamic_index_in_dim(held, mine, axis, keepdims=False)
        left.remove(bit)
        held = keep.astype(F32) + other.astype(F32)
        if left:
            held = held.astype(kept)
    return held


def scatter_order(first):
    high = list(range(3, bit_count()))
    return {"y": [1, 2, 0] + high, "x": [1, 0, 2] + high}[first]


def norm_parts(values):
    centre = values - jnp.mean(values, axis=-1, keepdims=True)
    spread = jnp.mean(centre * centre, axis=-1, keepdims=True)
    rate = lax.rsqrt(spread + EPSILON)
    return centre * rate, rate


def norm_back(grad, unit, rate, gain):
    scaled = grad * gain
    return rate * (
        scaled
        - jnp.mean(scaled, axis=-1, keepdims=True)
        - unit * jnp.mean(scaled * unit, axis=-1, keepdims=True)
    )


def turn_tables(positions):
    half = DH // 2
    frequency = jnp.exp(jnp.arange(half, dtype=F32) * (-2.0 * math.log(ROPE_BASE) / DH))
    angles = positions.astype(F32)[:, None] * frequency[None, :]
    cosine, sine = jnp.cos(angles), jnp.sin(angles)
    return (
        jnp.concatenate([cosine, cosine], axis=1),
        jnp.concatenate([-sine, sine], axis=1),
    )


def turned(values, cosine, sine):
    return values * cosine + pltpu.roll(values, DH // 2, 1) * sine


def unturned(values, cosine, sine):
    return values * cosine - pltpu.roll(values, DH // 2, 1) * sine


def dot_nt(left, right):
    return lax.dot_general(left, right, (((1,), (1,)), ((), ())), preferred_element_type=F32)


def dot_nn(left, right):
    return lax.dot_general(left, right, (((1,), (0,)), ((), ())), preferred_element_type=F32)


def dot_tn(left, right):
    return lax.dot_general(left, right, (((0,), (0,)), ((), ())), preferred_element_type=F32)


def attend_kernel(late, query, ka, kb, va, vb, context, pa_out, pb_out):
    rows = query.shape[0]
    base = SCALE * math.log2(math.e)
    sides = ((ka, va, pa_out), (kb, vb, pb_out))
    for head in range(query.shape[1] // DH):
        lanes = slice(head * DH, (head + 1) * DH)
        scores = []
        for side, (key, _, _) in enumerate(sides):
            for part in range(3):
                score = dot_nt(key[part, :, lanes], query[:, lanes])
                if part == 2:
                    key_at = lax.broadcasted_iota(jnp.int32, (rows, rows), 0)
                    if side == 0:
                        seen = key_at <= lax.broadcasted_iota(jnp.int32, (rows, rows), 1)
                    else:
                        seen = key_at < late[0] * rows
                    score = jnp.where(seen, score, NEG_LARGE)
                scores.append(score)
        top = functools.reduce(jnp.maximum, scores)
        top = jnp.max(top, axis=0, keepdims=True) * base
        exps = [jnp.exp2(score * base - top) for score in scores]
        total = jnp.sum(sum(exps), axis=0, keepdims=True)
        share = 1.0 / total
        mixed = 0.0
        for i, value in enumerate(exps):
            attn = (value * share).astype(LOW)
            side, part = divmod(i, 3)
            sides[side][2][0, head, part * rows : (part + 1) * rows, :] = attn
            mixed += dot_tn(sides[side][1][part, :, lanes], attn)
        context[:, lanes] = mixed.T.astype(LOW)


def attend_back_kernel(
    grad, query, ka, kb, va, vb, pa, pb, cos_a, sin_a, cos_b, sin_b,
    gq_out, gka_out, gkb_out, gva_out, gvb_out,
):
    rows = query.shape[0]
    lead = 2 * rows
    sides = (
        (ka, va, pa, cos_a, sin_a, gka_out, gva_out),
        (kb, vb, pb, cos_b, sin_b, gkb_out, gvb_out),
    )
    for head in range(query.shape[1] // DH):
        lanes = slice(head * DH, (head + 1) * DH)
        here, own = grad[:, lanes], query[:, lanes]
        backs, inner = [], 0.0
        for _, value, attn, _, _, _, out in sides:
            for part in range(3):
                weights = attn[0, head, part * rows : (part + 1) * rows, :]
                back = dot_nt(value[part, :, lanes], here)
                inner += weights.astype(F32) * back
                out[part, :, lanes] = dot_nn(weights, here).astype(LOW)
                backs.append(back)
        inner = jnp.sum(inner, axis=0, keepdims=True)
        mixed = 0.0
        for i, back in enumerate(backs):
            side, part = divmod(i, 3)
            key, _, attn, cosine, sine, out, _ = sides[side]
            at = slice(part * rows, (part + 1) * rows)
            score = (attn[0, head, at, :].astype(F32) * (back - inner)).astype(LOW)
            grads = dot_nn(score, own) * SCALE
            out[part, :, lanes] = unturned(grads, cosine[at, :], sine[at, :]).astype(LOW)
            mixed += dot_tn(key[part, :, lanes], score)
        gq_out[:, lanes] = unturned(mixed.T * SCALE, cos_a[lead:, :], sin_a[lead:, :]).astype(LOW)


def feed_kernel(
    mine, ffn, grad, up_a_own, up_a_far, up_b_own, up_b_far,
    down_p_own, down_p_far, down_q_own, down_q_far,
    branch, grad_ffn, up_keep, up_send, down_keep, down_send, ffn_t, grad_t, up_nat, down_nat,
):
    half = up_a_own.shape[1]
    core, across = mine[0], mine[2]
    own_at = pl.multiple_of(core * half, half)
    far_at = pl.multiple_of((1 - core) * half, half)
    step = pl.program_id(0)
    first = step == 0
    group, _, _, each, _ = down_nat.shape

    @pl.when(first)
    def _():
        ffn_t[...] = ffn[...].T
        grad_t[...] = grad[...].T.reshape(grad_t.shape)

    for place, (own, far) in enumerate(((up_a_own, up_a_far), (up_b_own, up_b_far))):

        @pl.when(step % 2 == place)
        def _():
            up_nat[:half] = own[0]
            up_nat[half:] = far[0]

    for ref, at_core, at in (
        (down_p_own, core, across),
        (down_p_far, 1 - core, across),
        (down_q_own, core, 1 - across),
        (down_q_far, 1 - core, 1 - across),
    ):
        down_nat[:, at_core, at, :, :half] = ref[:, pl.ds(own_at, half)].reshape(group, each, half)
        down_nat[:, at_core, at, :, half:] = ref[:, pl.ds(far_at, half)].reshape(group, each, half)
    up_rows = up_nat[...]
    down_rows = down_nat[...].reshape(-1, 2 * half)
    upper = dot_nt(ffn[...], up_rows)
    slope = math.sqrt(2.0 / math.pi)
    square = upper * upper
    bent = jnp.tanh(slope * upper * (1.0 + 0.044715 * square))
    share = 0.5 + 0.5 * bent
    active = (upper * share).astype(LOW)
    gelu_slope = share + 0.5 * upper * (1.0 - bent * bent) * (
        slope + (3.0 * 0.044715 * slope) * square
    )
    grad_hidden = (dot_nn(grad[...], down_rows) * gelu_slope).astype(LOW)
    more_out = dot_nt(active, down_rows)
    more_grad = dot_nn(grad_hidden, up_rows)

    @pl.when(first)
    def _():
        branch[...] = more_out
        grad_ffn[...] = more_grad

    @pl.when(jnp.logical_not(first))
    def _():
        branch[...] += more_out
        grad_ffn[...] += more_grad

    for ref, at in ((up_keep, 0), (up_send, half)):
        part = dot_nn(ffn_t[...], grad_hidden[:, at : at + half]).astype(LOW)
        ref[0, 0] = part[:, : half // 2]
        ref[0, 1] = part[:, half // 2 :]
    for ref, at in ((down_keep, core), (down_send, 1 - core)):
        part = dot_nn(grad_t[:, at].reshape(group * 2 * each, -1), active).astype(LOW)
        ref[:, pl.ds(own_at, half)] = part[:, :half]
        ref[:, pl.ds(far_at, half)] = part[:, half:]


def feed_forward(mine, ffn, grad_branch, up_parts, down_parts):
    rows, width = ffn.shape
    groups, half = up_parts[0].shape[:2]
    steps, wide = 2 * groups, 2 * half

    def whole(*dims):
        return pl.BlockSpec(dims, lambda t, m: (0,) * len(dims))

    def place(t, m):
        return t // 2 * 2 + (m[1] + t) % 2

    shape = jax.ShapeDtypeStruct
    up_in = pl.BlockSpec((1, half, width), lambda t, m: (t // 2, 0, 0))
    up_out = pl.BlockSpec((1, 2, width, half // 2), lambda t, m: (place(t, m), 0, 0, 0))

    def lanes(count):
        return pl.BlockSpec((count, wide), lambda t, m: (0, place(t, m)))

    return pl.pallas_call(
        feed_kernel,
        grid_spec=pltpu.PrefetchScalarGridSpec(
            num_scalar_prefetch=1,
            grid=(steps,),
            in_specs=[whole(rows, width)] * 2 + [up_in] * 4 + [lanes(width // 4)] * 4,
            out_specs=[whole(rows, width)] * 2 + [up_out] * 2 + [lanes(width // 2)] * 2,
            scratch_shapes=[
                pltpu.VMEM((width, rows), LOW),
                pltpu.VMEM((steps, 2, width // 2 // steps, rows), LOW),
                pltpu.VMEM((wide, width), LOW),
                pltpu.VMEM((steps, 2, 2, width // 4 // steps, wide), LOW),
            ],
        ),
        out_shape=[shape((rows, width), F32)] * 2
        + [shape((steps, 2, width, half // 2), LOW)] * 2
        + [shape((width // 2, steps * wide), LOW)] * 2,
        compiler_params=pltpu.CompilerParams(vmem_limit_bytes=VMEM),
        cost_estimate=LONG,
        name="feed_forward",
    )(mine, ffn, grad_branch, *up_parts, *down_parts)


def norm_kernel(hidden, gain, normed, even, odd, wide):
    rows, width = hidden.shape
    unit, _ = norm_parts(hidden[...].astype(F32))
    normed[...] = (unit * gain[...]).astype(LOW)
    for i in range(width // DH):
        lanes = slice(i * DH, (i + 1) * DH)
        wide[i] = normed[:, lanes].astype(F32)
        even[:, lanes] = wide[i, pl.ds(0, rows // 2, 2), :].astype(LOW)
        odd[:, lanes] = wide[i, pl.ds(1, rows // 2, 2), :].astype(LOW)


def norm_rows(hidden, gain, waits=()):
    rows, width = hidden.shape
    some = rows // 2
    block, half = rows_spec(some, width), rows_spec(some // 2, width)
    shape = jax.ShapeDtypeStruct
    return ordered_call(
        norm_kernel,
        (hidden, gain,),
        waits,
        [block, whole_spec(1, width)],
        grid=(2,),
        out_specs=[block, half, half],
        out_shape=[shape((rows, width), LOW)] + [shape((rows // 2, width), LOW)] * 2,
        scratch_shapes=[pltpu.VMEM((width // DH, some, DH), F32)],
        compiler_params=pltpu.CompilerParams(vmem_limit_bytes=VMEM),
        name="norm_rows",
    )


def project_kernel(own, cmem, mem, normed, weight, cosine, sine, key, value, *query):
    rows, width = cmem.shape
    which, segment = pl.program_id(0), pl.program_id(1)
    times = rows // cosine.shape[1]

    def product(source):
        return dot_nt(source[...], weight[...].reshape(width, width))

    def turned_product(source, out):
        lin = product(source)
        cos = jnp.concatenate([cosine[0]] * times, axis=0)
        sin = jnp.concatenate([sine[0]] * times, axis=0)
        for head in range(width // DH):
            lanes = slice(head * DH, (head + 1) * DH)
            out[:, lanes] = turned(lin[:, lanes], cos, sin).astype(LOW)

    for i, source in enumerate((cmem, mem, normed)):

        @pl.when((segment == i) & (which == 0))
        def _():
            turned_product(source, key.at[0])

        @pl.when((segment == i) & (which == 1))
        def _():
            value[0] = product(source).astype(LOW)

    if own:

        @pl.when((segment == 2) & (which == 2))
        def _():
            turned_product(normed, query[0])


def project(cmem, mem, normed, weights, tables, own, waits=()):
    rows, width = normed.shape
    count, _, unit, _ = weights.shape
    per = width // count // unit
    shape = jax.ShapeDtypeStruct
    whole = pl.BlockSpec((rows, width), lambda w, i: (0, 0))
    tables = [table.reshape(3, -1, DH) for table in tables]
    table = pl.BlockSpec((1,) + tables[0].shape[1:], lambda w, i: (jnp.where(w < 2, i, 2), 0, 0))
    outs = [
        pl.BlockSpec((1, rows, width), lambda w, i: (jnp.where(w == 0, i, 2), 0, 0)),
        pl.BlockSpec(
            (1, rows, width),
            lambda w, i: (jnp.where(w == 0, 0, jnp.where(w == 1, i, 2)), 0, 0),
        ),
    ]
    return ordered_call(
        lambda *refs: project_kernel(own, *refs),
        (cmem, mem, normed, weights, *tables,),
        waits,
        [whole] * 3
        + [pl.BlockSpec((count, per, unit, width), lambda w, i: (0, w, 0, 0))]
        + [table] * 2,
        grid=(3 if own else 2, 3),
        out_specs=outs + [whole] * own,
        out_shape=[shape((3, rows, width), LOW)] * 2 + [shape((rows, width), LOW)] * own,
        compiler_params=pltpu.CompilerParams(vmem_limit_bytes=VMEM),
        name="project",
    )


def weight_grads_kernel(counts, each, core, *refs):
    total_count = sum(counts)
    grads, sources = refs[:total_count], refs[total_count : 2 * total_count]
    *extra, keep, send = refs[2 * total_count :]
    first, at = core[0] == 0, 0
    groups, depth = keep.shape[0], keep.shape[-1]
    for place, count in enumerate(counts):
        total = sum(dot_tn(grads[i][0], sources[i][...]) for i in range(at, at + count))
        at += count
        total = total.astype(LOW).reshape(groups, 2, 2, each, depth)
        rows = slice(place * each, (place + 1) * each)
        keep[:, :, rows] = jnp.where(first, total[:, 0], total[:, 1])
        send[:, :, rows] = jnp.where(first, total[:, 1], total[:, 0])
    if extra:
        rows = slice(len(counts) * each, None)
        keep[:, :, rows] = extra[0][...]
        send[:, :, rows] = extra[1][...]


def weight_grads(core, problems, each, waits=(), extra=()):
    pairs = [pair for problem in problems for pair in problem]
    grads = [g if isinstance(g, tuple) else (g[None], 0) for g, _ in pairs]
    sources = [source for _, source in pairs]
    width, depth = grads[0][0].shape[2], sources[0].shape[1]
    groups = 4
    wide = groups * 4 * each
    more = extra[0].shape[2] if extra else 0

    def spec(array, place):
        return pl.BlockSpec((1, array.shape[1], wide), lambda i: (place, 0, i))

    out = (groups, 2, len(problems) * each + more, depth)
    return ordered_call(
        lambda *refs: weight_grads_kernel([len(p) for p in problems], each, *refs),
        (core.reshape(1), *[array for array, _ in grads], *sources, *extra),
        waits,
        [pl.BlockSpec(memory_space=pltpu.SMEM)]
        + [spec(array, place) for array, place in grads]
        + [whole_spec(*source.shape) for source in sources]
        + [pl.BlockSpec((groups, 2, more, depth), lambda i: (i, 0, 0, 0))] * len(extra),
        grid=(width // wide,),
        out_specs=[pl.BlockSpec(out, lambda i: (i, 0, 0, 0))] * 2,
        out_shape=[jax.ShapeDtypeStruct((width // (4 * each),) + out[1:], LOW)] * 2,
        compiler_params=pltpu.CompilerParams(vmem_limit_bytes=VMEM),
        name="weight_grads",
    )


def weight_spec(weights, which):
    count, _, unit, width = weights.shape
    per = width // count // unit
    return pl.BlockSpec((count, per, unit, width), lambda i: (0, which, 0, 0))


def rows_spec(rows, width):
    return pl.BlockSpec((rows, width), lambda i: (i, 0))


def whole_spec(*dims):
    return pl.BlockSpec(dims, lambda i: (0,) * len(dims))


def far_kernel(late, grad_key, grad_value, comp, w_key, w_value, w_before, out):
    rows, width = out.shape
    total = dot_nn(grad_key[0], w_key[...].reshape(width, width))
    total += dot_nn(grad_value[0], w_value[...].reshape(width, width))
    rim = dot_nn(comp[0, :16], w_before[...].reshape(width, width))[:1] * late[0].astype(F32)
    last = lax.broadcasted_iota(jnp.int32, (rows, width), 0) == rows - 1
    out[...] = (total + jnp.where(last, rim, 0.0)).astype(LOW)


def far_back(late, grad_keys, grad_values, comp_grad, weights, later, waits=()):
    batch, _, width = comp_grad.shape
    rows = grad_keys.shape[1] // batch
    last_part = pl.BlockSpec((1, rows, width), lambda i: (2, i, 0))
    return ordered_call(
        far_kernel,
        (late.reshape(1), grad_keys, grad_values, comp_grad, weights, weights, later,),
        waits,
        [pl.BlockSpec(memory_space=pltpu.SMEM), last_part, last_part]
        + [pl.BlockSpec((1,) + comp_grad.shape[1:], lambda i: (i, 0, 0))]
        + [weight_spec(weights, 0), weight_spec(weights, 1), weight_spec(later, 0)],
        grid=(batch,),
        out_specs=rows_spec(rows, width),
        out_shape=jax.ShapeDtypeStruct((batch * rows, width), LOW),
        compiler_params=pltpu.CompilerParams(vmem_limit_bytes=VMEM),
        name="far_back",
    )


def finish_kernel(
    grad_query, grad_key, grad_value, comp, token, hidden, grad_middle, gain,
    w_query, w_key, w_value, w_before, w_at, grad_in, grad_gain, wide,
):
    rows, width = hidden.shape
    half = rows // 2
    before = dot_nn(comp[0], w_before[...].reshape(width, width))
    before = jnp.where(
        lax.broadcasted_iota(jnp.int32, (half, width), 0) == half - 1,
        0.0,
        pltpu.roll(before, half - 1, 0),
    )
    at = dot_nn(comp[0], w_at[...].reshape(width, width))
    for i in range(width // DH):
        lanes = slice(i * DH, (i + 1) * DH)
        wide[i, pl.ds(0, half, 2), :] = at[:, lanes]
        wide[i, pl.ds(1, half, 2), :] = before[:, lanes]
    grads = jnp.concatenate([wide[i] for i in range(width // DH)], axis=1)
    grads += token[...].astype(F32)
    for left, weight in ((grad_query, w_query), (grad_key, w_key), (grad_value, w_value)):
        grads += dot_nn(left[...].reshape(rows, width), weight[...].reshape(width, width))
    unit, rate = norm_parts(hidden[...].astype(F32))
    total = jnp.sum(grads * unit, axis=0, keepdims=True)
    grad_in[...] = (grad_middle[...] + norm_back(grads, unit, rate, gain[...])).astype(LOW)
    first = pl.program_id(0) == 0

    @pl.when(first)
    def _():
        grad_gain[...] = total

    @pl.when(jnp.logical_not(first))
    def _():
        grad_gain[...] += total


def finish(
    grad_query, grad_keys, grad_values, comp_grad, token, hidden, grad_middle, gain, weights, later, waits=()):
    batch = comp_grad.shape[0]
    rows, width = hidden.shape
    some = rows // batch
    block = rows_spec(some, width)
    last_part = pl.BlockSpec((1, some, width), lambda i: (2, i, 0))
    shape = jax.ShapeDtypeStruct
    return ordered_call(
        finish_kernel,
        (grad_query, grad_keys, grad_values, comp_grad, token, hidden, grad_middle, gain,
        weights, weights, weights, later, later,),
        waits,
        [block, last_part, last_part]
        + [pl.BlockSpec((1,) + comp_grad.shape[1:], lambda i: (i, 0, 0))]
        + [block] * 3
        + [whole_spec(1, width)]
        + [weight_spec(weights, which) for which in (2, 0, 1)]
        + [weight_spec(later, which) for which in (0, 1)],
        grid=(batch,),
        out_specs=[block, whole_spec(1, width)],
        out_shape=[shape((rows, width), LOW), shape((1, width), F32)],
        scratch_shapes=[pltpu.VMEM((width // DH, some, DH), F32)],
        compiler_params=pltpu.CompilerParams(vmem_limit_bytes=VMEM),
        name="finish",
    )


def outputs_kernel(before, at, mask, middle, branch, live, w_before, w_at, compressed, layer_out):
    width = compressed.shape[1]
    total = dot_nt(before[...], w_before[...].reshape(width, width))
    total += dot_nt(at[...], w_at[...].reshape(width, width))
    compressed[...] = (total * mask[...]).astype(LOW)
    layer_out[...] = ((middle[...] + branch[...]) * live[...]).astype(LOW)


def outputs(before, at, mask, middle, branch, live, later, waits=()):
    rows, width = middle.shape
    some, few = rows // 2, at.shape[0] // 2
    shape = jax.ShapeDtypeStruct
    return ordered_call(
        outputs_kernel,
        (before, at, mask, middle, branch, live, later, later),
        waits,
        [rows_spec(few, width), rows_spec(few, width), rows_spec(few, 1)]
        + [rows_spec(some, width), rows_spec(some, width), rows_spec(some, 1)]
        + [weight_spec(later, which) for which in (0, 1)],
        grid=(2,),
        out_specs=[rows_spec(few, width), rows_spec(some, width)],
        out_shape=[shape(at.shape, LOW), shape((rows, width), LOW)],
        compiler_params=pltpu.CompilerParams(vmem_limit_bytes=VMEM),
        name="outputs",
    )


def join_kernel(context, hidden, gain, weight, middle, ffn):
    width = middle.shape[1]
    middle[...] = hidden[...].astype(F32) + dot_nt(
        context[...], weight[...].reshape(width, width)
    )
    unit, _ = norm_parts(middle[...])
    ffn[...] = (unit * gain[...]).astype(LOW)


def join(context, hidden, gain, weights, waits=()):
    rows, width = hidden.shape
    some = rows // 2
    block = rows_spec(some, width)
    shape = jax.ShapeDtypeStruct
    return ordered_call(
        join_kernel,
        (context, hidden, gain, weights,),
        waits,
        [block, block, whole_spec(1, width), weight_spec(weights, 0)],
        grid=(2,),
        out_specs=[block, block],
        out_shape=[shape((rows, width), F32), shape((rows, width), LOW)],
        compiler_params=pltpu.CompilerParams(vmem_limit_bytes=VMEM),
        name="join",
    )


def part_kernel(
    grad_ffn, middle, cot, live, gain, weight, grad_middle, grad_low, grad_context, grad_gain
):
    width = middle.shape[1]
    unit, rate = norm_parts(middle[...])
    grads = grad_ffn[...]
    grad_middle[...] = cot[...].astype(F32) * live[...] + norm_back(
        grads, unit, rate, gain[...]
    )
    grad_low[...] = grad_middle[...].astype(LOW)
    grad_context[...] = dot_nn(grad_low[...], weight[...].reshape(width, width)).astype(LOW)
    total = jnp.sum(grads * unit, axis=0, keepdims=True)
    first = pl.program_id(0) == 0

    @pl.when(first)
    def _():
        grad_gain[...] = total

    @pl.when(jnp.logical_not(first))
    def _():
        grad_gain[...] += total


def part(grad_ffn, middle, cot, live, gain, weights, waits=()):
    rows, width = middle.shape
    some = rows // 2
    block = rows_spec(some, width)
    shape = jax.ShapeDtypeStruct
    return ordered_call(
        part_kernel,
        (grad_ffn, middle, cot, live, gain, weights,),
        waits,
        [block] * 3
        + [rows_spec(some, 1), whole_spec(1, width), weight_spec(weights, 0)],
        grid=(2,),
        out_specs=[block] * 3 + [whole_spec(1, width)],
        out_shape=[
            shape((rows, width), F32),
            shape((rows, width), LOW),
            shape((rows, width), LOW),
            shape((1, width), F32),
        ],
        compiler_params=pltpu.CompilerParams(vmem_limit_bytes=VMEM),
        name="part",
    )


def head_spec(rows):
    return pl.BlockSpec((rows, TOGETHER * DH), lambda b, h: (b, h))


def keys_spec(rows):
    return pl.BlockSpec((3, rows, TOGETHER * DH), lambda b, h: (0, b, h))


def table_spec(rows):
    return pl.BlockSpec((rows, DH), lambda b, h: (0, 0))


def attn_spec(keys, rows):
    return pl.BlockSpec((1, TOGETHER, keys, rows), lambda b, h: (b, h, 0, 0))


def attend(late, query, ka, kb, va, vb, batch, waits=()):
    rows, width = query.shape[0] // batch, query.shape[1]
    keys = 3 * rows
    shape = jax.ShapeDtypeStruct
    return ordered_call(
        attend_kernel,
        (late, query, ka, kb, va, vb,),
        waits,
        [pl.BlockSpec(memory_space=pltpu.SMEM), head_spec(rows)] + [keys_spec(rows)] * 4,
        grid=(batch, H // TOGETHER),
        out_specs=[head_spec(rows)] + [attn_spec(keys, rows)] * 2,
        out_shape=[shape((batch * rows, width), LOW)]
        + [shape((batch, H, keys, rows), LOW)] * 2,
        compiler_params=pltpu.CompilerParams(vmem_limit_bytes=VMEM),
        name="attend",
    )


def attend_back(grad, query, ka, kb, va, vb, pa, pb, tables, batch, waits=()):
    rows, width = query.shape[0] // batch, query.shape[1]
    keys = 3 * rows
    shape = jax.ShapeDtypeStruct
    return ordered_call(
        attend_back_kernel,
        (grad, query, ka, kb, va, vb, pa, pb, *tables,),
        waits,
        [head_spec(rows)] * 2
        + [keys_spec(rows)] * 4
        + [attn_spec(keys, rows)] * 2
        + [table_spec(keys)] * 4,
        grid=(batch, H // TOGETHER),
        out_specs=[head_spec(rows)] + [keys_spec(rows)] * 4,
        out_shape=[shape((batch * rows, width), LOW)]
        + [shape((3, batch * rows, width), LOW)] * 4,
        compiler_params=pltpu.CompilerParams(vmem_limit_bytes=VMEM),
        name="attend_back",
    )


def local_general(
    hidden_in, memory, compressed_in, lengths, gain_attn, gain_ffn,
    w_query, w_key, w_value, w_out, w_up, w_down, w_compress, cot_out, cot_comp,
):
    micro, streams, block, width = hidden_in.shape
    batch = micro * streams
    rows = batch * block
    late = lax.axis_index("tm")
    windows_each = block // COMP

    hidden = hidden_in.reshape(batch, block, width)
    mem = memory.reshape(batch, -1, width)
    cmem = compressed_in.reshape(batch, -1, width)
    hidden_far = swap(hidden, 0)
    mem_far = swap(mem, 0)
    cmem_far = swap(cmem, 0)

    gains = gather(
        jnp.stack([gain_attn, gain_ffn]).reshape(2, 1, -1), gather_order("x_first")
    ).reshape(2, width).astype(F32)
    gain_first, gain_second = gains[0], gains[1]
    key_value = gather(jnp.stack([w_key.T, w_value.T]), gather_order("x_first"))
    query_out = gather(jnp.stack([w_query.T, w_out.T]), gather_order("x_first"))
    up_t = gather(w_up.T[None], gather_order("x"))[0]
    down_t = gather(w_down.T[None], gather_order("y"))[0]
    compress_t = gather(w_compress.T[None], gather_order("y"))[0]
    key_t, value_t = key_value[0], key_value[1]
    query_t, out_t = query_out[0], query_out[1]

    cmem_size, mem_size = cmem.shape[1], mem.shape[1]

    def positions(half):
        return jnp.concatenate(
            [
                COMP * (half * cmem_size + jnp.arange(cmem_size, dtype=jnp.int32) - CMEM) - MEM,
                half * mem_size + jnp.arange(mem_size, dtype=jnp.int32) - MEM,
                half * block + jnp.arange(block, dtype=jnp.int32),
            ]
        )

    tables = turn_tables(positions(late)) + turn_tables(positions(1 - late))
    lens = lengths.reshape(batch)
    query_pos = late * block + jnp.arange(block, dtype=jnp.int32)
    window_end = late * block + COMP * jnp.arange(windows_each, dtype=jnp.int32)
    row_mask = (query_pos[None, :] < lens[:, None]).astype(F32)[..., None]
    window_mask = (window_end[None, :] < lens[:, None]).astype(F32)[..., None]

    inputs = hidden.astype(F32)
    unit, rate = norm_parts(inputs)
    normed = (unit * gain_first).astype(LOW)
    unit_far, _ = norm_parts(hidden_far.astype(F32))
    normed_far = (unit_far * gain_first).astype(LOW)

    rim = normed_far[:, block - 1 :] * (late == 1).astype(LOW)
    padded = jnp.concatenate([rim, normed[:, : block - 1]], axis=1)
    windows = padded.reshape(batch * windows_each, COMP * width)
    comp_grad = (
        (cot_comp.reshape(batch, windows_each, width).astype(F32) * window_mask)
        .astype(LOW)
        .reshape(batch * windows_each, width)
    )
    compressed = dot_nt(windows, compress_t).reshape(batch, windows_each, width) * window_mask
    grad_compress = scatter(dot_tn(comp_grad, windows).astype(LOW), scatter_order("y"))
    grad_windows = dot_nn(comp_grad, compress_t).reshape(batch, block, width)
    rim_grad = swap(grad_windows[:, :1].astype(LOW), 0).astype(F32) * (late == 0).astype(F32)
    grad_shifted = jnp.concatenate([grad_windows[:, 1:], rim_grad], axis=1)

    near = jnp.stack([cmem, mem, normed]).reshape(-1, width)
    far = jnp.stack([cmem_far, mem_far, normed_far]).reshape(-1, width)
    normed = normed.reshape(rows, width)

    def by_head(lin, cosine, sine):
        shape = (-1, batch, block, H, DH)
        cosine, sine = (table.reshape(-1, 1, block, 1, DH) for table in (cosine, sine))
        lin = lin.reshape(shape)
        turn = lin * cosine + jnp.roll(lin, DH // 2, axis=-1) * sine
        return turn.astype(LOW).reshape(-1, rows, width)

    query = by_head(dot_nt(normed, query_t), tables[0][-block:], tables[1][-block:])[0]
    ka = by_head(dot_nt(near, key_t), *tables[:2])
    kb = by_head(dot_nt(far, key_t), *tables[2:])
    va, vb = (
        dot_nt(part, value_t).astype(LOW).reshape(3, rows, width) for part in (near, far)
    )
    context, pa, pb = attend(late.reshape(1), query, ka, kb, va, vb, batch)
    middle = inputs.reshape(rows, width) + dot_nt(context, out_t)

    unit_ffn, rate_ffn = norm_parts(middle)
    ffn = (unit_ffn * gain_second).astype(LOW)
    upper = dot_nt(ffn, up_t)
    slope = math.sqrt(2.0 / math.pi)
    bent = jnp.tanh(slope * (upper + 0.044715 * upper * upper * upper))
    active = (0.5 * upper * (1.0 + bent)).astype(LOW)
    gelu_slope = 0.5 * (1.0 + bent) + 0.5 * upper * (1.0 - bent * bent) * slope * (
        1.0 + 3.0 * 0.044715 * upper * upper
    )
    branch = dot_nt(active, down_t)
    live = row_mask.reshape(rows, 1)
    layer_out = ((middle + branch) * live).astype(LOW)
    grad_live = cot_out.reshape(rows, width).astype(F32) * live
    grad_branch = grad_live.astype(LOW)
    grad_upper = (dot_nn(grad_branch, down_t) * gelu_slope).astype(LOW)
    grad_down = scatter(dot_tn(grad_branch, active).astype(LOW), scatter_order("y"))
    grad_up = scatter(dot_tn(grad_upper, ffn).astype(LOW), scatter_order("x"))
    grad_ffn = dot_nn(grad_upper, up_t)
    grad_gain_ffn = jnp.sum(grad_ffn * unit_ffn, axis=0)
    grad_middle = grad_live + norm_back(grad_ffn, unit_ffn, rate_ffn, gain_second)

    grad_attended = grad_middle.astype(LOW)
    grad_out = scatter(dot_tn(grad_attended, context).astype(LOW), scatter_order("y"))
    grad_context = dot_nn(grad_attended, out_t).astype(LOW)
    gq, *parts = attend_back(grad_context, query, ka, kb, va, vb, pa, pb, tables, batch)
    gka, gkb, gva, gvb = (part.reshape(-1, width) for part in parts)
    grad_value = scatter(
        (dot_tn(gva, near) + dot_tn(gvb, far)).astype(LOW), scatter_order("x")
    )
    grad_key = scatter((dot_tn(gka, near) + dot_tn(gkb, far)).astype(LOW), scatter_order("y"))
    grad_query = scatter(dot_tn(gq, normed).astype(LOW), scatter_order("x"))

    def token_rows(values):
        return values[-rows:]

    token_far = dot_nn(token_rows(gkb), key_t) + dot_nn(token_rows(gvb), value_t)
    token_back = swap(token_far.astype(LOW), 0).astype(F32)
    grad_normed = (
        dot_nn(gq, query_t)
        + dot_nn(token_rows(gka), key_t)
        + dot_nn(token_rows(gva), value_t)
        + grad_shifted.reshape(rows, width)
        + token_back
    )
    unit = unit.reshape(rows, width)
    grad_gain_attn = jnp.sum(grad_normed * unit, axis=0)
    grad_in = grad_middle + norm_back(grad_normed, unit, rate.reshape(rows, 1), gain_first)
    gain_grads = scatter(
        jnp.stack([grad_gain_attn, grad_gain_ffn], axis=1), scatter_order("x"), F32
    )

    return (
        layer_out.reshape(hidden_in.shape),
        compressed.astype(LOW).reshape(cot_comp.shape),
        grad_in.astype(LOW).reshape(hidden_in.shape),
        gain_grads[:, 0],
        gain_grads[:, 1],
        grad_query.T,
        grad_key.T,
        grad_value.T,
        grad_out.T,
        grad_up.T,
        grad_down.T,
        grad_compress.T,
    )


def local(
    hidden_in, memory, compressed_in, lengths, gain_attn, gain_ffn,
    w_query, w_key, w_value, w_out, w_up, w_down, w_compress, cot_out, cot_comp,
):
    count = lax.axis_size(BOTH)
    micro, streams, block, width = hidden_in.shape
    unit_rows, hidden_rows = width // count, w_up.shape[1]
    if unit_rows % 32 or hidden_rows % 128:
        return local_general(
            hidden_in, memory, compressed_in, lengths, gain_attn, gain_ffn,
            w_query, w_key, w_value, w_out, w_up, w_down, w_compress, cot_out, cot_comp,
        )
    batch = micro * streams
    rows = batch * block
    late, core = lax.axis_index("tm"), bit_of(1)
    windows_each = block // COMP
    hidden = hidden_in.reshape(batch, block, width)
    mem = memory.reshape(batch, -1, width)
    cmem = compressed_in.reshape(batch, -1, width)
    high = list(range(bit_count() - 1, 2, -1))
    early = [0] + high + [2, 1]

    half_unit = unit_rows // 2

    def gathered_groups(parts, *waits):
        shard = jnp.concatenate(parts).reshape(1, -1, half_unit, width)
        shard = copied(shard, waits) if waits else shard
        return shard, lax.all_gather(shard, BOTH, axis=0, tiled=True)

    gain_rows = jnp.zeros((half_unit, width), LOW)
    gain_rows = gain_rows.at[0, : 2 * unit_rows].set(jnp.concatenate([gain_attn, gain_ffn]))
    _, attention_in = gathered_groups([w_key.T, w_value.T, w_query.T, gain_rows])
    _, out_in = gathered_groups([w_out.T])
    hidden, mem, cmem = (part.reshape(rows, width) for part in (hidden, mem, cmem))
    up_in = Gathering(w_up.T[None], [0] + high + [2])
    down_in = Gathering(w_down.T[None], high + [2, 0])
    hidden_far, cmem_far, mem_far = (swap(part, 0) for part in (hidden, cmem, mem))

    positions = np.concatenate(
        [
            COMP * (np.arange(CMEM) - CMEM) - MEM,
            np.arange(MEM) - MEM,
            np.arange(2 * block),
        ]
    ).astype(np.float32)
    frequency = np.exp(
        np.arange(DH // 2, dtype=np.float32) * np.float32(-2.0 * math.log(ROPE_BASE) / DH)
    ).astype(np.float32)
    angles = positions[:, None] * frequency[None, :]
    turns = np.stack(
        [
            np.concatenate([np.cos(angles), np.cos(angles)], axis=1),
            np.concatenate([-np.sin(angles), np.sin(angles)], axis=1),
        ]
    ).astype(np.float32)
    turns = jnp.asarray(turns.reshape(2, 3, 2, -1, DH))

    def tables_of(half):
        return tuple(lax.dynamic_index_in_dim(turns, half, 2, False).reshape(2, -1, DH))

    tables = tables_of(late) + tables_of(1 - late)
    lens = lengths.reshape(batch)
    query_pos = late * block + jnp.arange(block, dtype=jnp.int32)
    window_end = late * block + COMP * jnp.arange(windows_each, dtype=jnp.int32)
    row_mask = (query_pos[None, :] < lens[:, None]).astype(F32)[..., None]
    window_mask = (window_end[None, :] < lens[:, None]).astype(F32)[..., None]
    live = row_mask.reshape(rows, 1)
    grad_live = cot_out.reshape(rows, width).astype(F32) * live
    grad_branch = grad_live.astype(LOW)

    outward = high[::-1]
    last = down_in.step()
    last = up_in.step(last)
    last = down_in.step(last)
    last = up_in.step(last)


    ones = jnp.ones((1, width), F32)
    _, unit_even, unit_odd = norm_rows(hidden, ones, (last,))
    unit_far, _, _ = norm_rows(hidden_far, ones, (unit_even,))

    def rows_before(far_rows, odd_rows):
        far_rows, odd_rows = (value.reshape(batch, -1, width) for value in (far_rows, odd_rows))
        rim = far_rows[:, block - 1 :] * (late == 1).astype(LOW)
        return jnp.concatenate([rim, odd_rows[:, : windows_each - 1]], axis=1).reshape(-1, width)

    comp_grad = (cot_comp.reshape(batch, windows_each, width).astype(F32) * window_mask).astype(LOW)
    comp_rows = comp_grad.reshape(-1, width)
    keep, send = weight_grads(
        core,
        [[(comp_rows, rows_before(unit_far, unit_odd))], [(comp_rows, unit_even)]],
        unit_rows,
    )
    compress_sum = Chain(keep, send, outward + [2, 0], (2 * unit_rows, width))
    last = down_in.step(keep, grad_branch, *tables)
    last = up_in.step(last)
    last = compress_sum.step(last)
    up_held, up_other, down_held, down_other = (
        part.reshape(shape)
        for chain, shape in (
            (up_in, (count // 8, -1, width)),
            (down_in, (-1, hidden_rows * count)),
        )
        for part in (chain.held, chain.other)
    )

    gains = (
        attention_in[:, 6, 0, : 2 * unit_rows]
        .reshape(count, 2, unit_rows)
        .transpose(1, 0, 2)
        .reshape(2, width)
        .astype(F32)
    )
    gain_first, gain_second = gains[:1], gains[1:]
    normed, even, odd = norm_rows(hidden, gain_first, (last,))
    ka, va, query = project(cmem, mem, normed, attention_in, tables[:2], True)
    normed_far, _, _ = norm_rows(hidden_far, gain_first, (query,))
    kb, vb = project(cmem_far, mem_far, normed_far, attention_in, tables[2:], False)

    context, pa, pb = attend(late.reshape(1), query, ka, kb, va, vb, batch)
    last, compress_in = gathered_groups([w_compress[:width].T, w_compress[width:].T], context)
    up_other, down_other = gate(up_other, last), gate(down_other, last)
    up_parts = [up_held, swap(up_held, 1), up_other, swap(up_other, 1)]
    down_parts = [down_held, swap(down_held, 1), down_other, swap(down_other, 1)]
    middle, ffn = join(context, hidden, gain_second, out_in, (last,))

    branch, grad_ffn, up_keep, up_send, down_keep, down_send = feed_forward(
        jnp.stack([core, bit_of(2), late]), ffn, grad_branch, up_parts, down_parts
    )
    up_sum = Chain(up_keep, up_send, [0, 2] + outward, up_keep.shape[2:])
    down_sum = Chain(
        down_keep, down_send, [2, 0] + outward, (unit_rows, hidden_rows * count)
    )

    grad_middle, grad_low, grad_context, grad_gain_ffn = part(
        grad_ffn, middle, cot_out.reshape(rows, width), live, gain_second, out_in
    )
    last = up_sum.step(grad_context)
    last = down_sum.step(last)

    gq, gka, gkb, gva, gvb = attend_back(
        grad_context, query, ka, kb, va, vb, pa, pb, tables, batch, (last,)
    )
    before = rows_before(normed_far, odd)
    sources = (cmem, mem, normed, cmem_far, mem_far, normed_far)

    def source_problem(near, far):
        grads = [(grad, i) for grad in (near, far) for i in range(3)]
        return list(zip(grads, sources))

    keep, send = weight_grads(
        core, [source_problem(gva, gvb), [(grad_low, context)]], unit_rows
    )
    value_sum = Chain(keep, send, [2, 0] + outward, (2 * unit_rows, width))
    token_far = far_back(late, gkb, gvb, comp_grad, attention_in, compress_in, (keep,))
    token_back = swap(token_far, 0)
    last = up_sum.step(token_far)
    last = down_sum.step(last)
    last = value_sum.step(last)
    keep, send = weight_grads(
        core, [source_problem(gka, gkb), [(gq, normed)]], unit_rows, (last,)
    )
    key_sum = Chain(keep, send, [0, 2] + outward, (2 * unit_rows, width))
    last = up_sum.step(keep)
    last = key_sum.step(last)
    last = compress_sum.step(last)

    grad_in, grad_gain_attn = finish(
        gq, gka, gva, comp_grad, token_back, hidden, grad_middle, gain_first,
        attention_in, compress_in, (last,),
    )
    gain_pair = (
        jnp.concatenate([grad_gain_attn, grad_gain_ffn])
        .reshape(2, -1, 2, 2, unit_rows)
        .transpose(2, 1, 3, 0, 4)
        .reshape(2, -1, 2, 1, 2 * unit_rows)
        .astype(LOW)
    )
    gain_pair = jnp.pad(gain_pair, ((0, 0),) * 3 + ((0, 15), (0, DH - 2 * unit_rows)))
    gain_sum = Chain(
        lax.dynamic_index_in_dim(gain_pair, core, 0, keepdims=False),
        lax.dynamic_index_in_dim(gain_pair, 1 - core, 0, keepdims=False),
        [2, 0] + outward,
        (16, DH),
    )
    last = round_of([value_sum, down_sum, up_sum], (grad_in,))
    last = round_of([key_sum, gain_sum], (last,))
    compressed, layer_out = outputs(
        before, even, window_mask.reshape(-1, 1), middle, branch, live, compress_in, (last,)
    )
    last = round_of([value_sum, down_sum, compress_sum], (compressed,))
    last = round_of([key_sum, gain_sum, up_sum], (last,))
    last = round_of([value_sum, compress_sum], (last,))
    last = round_of([key_sum, down_sum, gain_sum], (last,))
    last = round_of([value_sum, compress_sum], (last,))
    last = round_of([key_sum, gain_sum], (last,))
    round_of([gain_sum], (last,))
    grad_value, grad_out = jnp.split(value_sum.total, 2)
    grad_before, grad_at = jnp.split(compress_sum.total * gain_first, 2)
    gain_grads = gain_sum.total[0, : 2 * unit_rows]
    grad_key, grad_query = jnp.split(key_sum.total, 2)

    return (
        layer_out.reshape(hidden_in.shape),
        compressed.reshape(cot_comp.shape),
        grad_in.reshape(hidden_in.shape),
        gain_grads[:unit_rows],
        gain_grads[unit_rows:],
        grad_query.T,
        grad_key.T,
        grad_value.T,
        grad_out.T,
        up_sum.total,
        down_sum.total.T,
        jnp.concatenate([grad_before.T, grad_at.T]),
    )


def solution(mesh):
    rows = P(None, "dp", "tm", None)
    columns = P(None, BOTH)
    return jax.shard_map(
        local,
        mesh=mesh,
        in_specs=(rows, rows, rows, P(None, "dp"), P(BOTH), P(BOTH))
        + (columns,) * 7
        + (rows, rows),
        out_specs=(rows, rows, rows, P(BOTH), P(BOTH)) + (columns,) * 7,
        check_vma=False,
    )
```
